32 devices in a mesh: dp: 8 (over y, x, core), tensor: 4 (over z).
Axes of the slice: x: 2, y: 2, z: 4, core: 2. Of those that a mesh axis runs over, the one named last changes fastest.
Arguments:
- tokens: bfloat16 [16384, 1024], P(('dp', 'tensor')), may hold values from -6 to 6
- gate_value_weight: bfloat16 [2, 1024, 2, 2048], P(None, 'dp', None, 'tensor'), may hold values from -0.1875 to 0.1875
- w_bc: bfloat16 [2, 1024, 256], P(None, 'dp'), may hold values from -0.1875 to 0.1875
- w_dt: bfloat16 [2, 1024, 32], P(None, 'dp', 'tensor'), may hold values from -0.1875 to 0.1875
- w_out: bfloat16 [2, 1024, 2048], P(None, 'dp', 'tensor'), may hold values from -0.125 to 0.125
- norm_gain: float32 [2, 1024], replicated, may hold values from 0.5 to 1.5
- conv_value_w: float32 [2, 4, 2048], P(None, None, 'tensor'), may hold values from -3 to 3
- conv_value_b: float32 [2, 2048], P(None, 'tensor'), may hold values from -2 to 2
- conv_shared_w: float32 [2, 4, 256], replicated, may hold values from -3 to 3
- conv_shared_b: float32 [2, 256], replicated, may hold values from -2 to 2
- step_bias: float32 [2, 32], P(None, 'tensor'), may hold values from -7 to -3
- decay_log: float32 [2, 32], P(None, 'tensor'), may hold values from 0 to 2.77
- skip_gain: float32 [2, 32], P(None, 'tensor'), may hold values from 0.5 to 1.5
- gate_gain: float32 [2, 2048], P(None, 'tensor'), may hold values from 0.5 to 1.5
- starts: int32 [8, 4], P('dp'), may hold values from 0 to 2047, as said below
- cotangent: bfloat16 [16384, 1024], P(('dp', 'tensor')), may hold values from -6 to 6
Outputs:
- output: bfloat16 [16384, 1024], P(('dp', 'tensor'))
- grad_input: float32 [16384, 1024], P(('dp', 'tensor'))
- grad_w_zx: float32 [2, 1024, 2, 2048], P(None, 'dp', None, 'tensor')
- grad_w_bc: float32 [2, 1024, 256], P(None, 'dp')
- grad_w_dt: float32 [2, 1024, 32], P(None, 'dp', 'tensor')
- grad_w_out: float32 [2, 1024, 2048], P(None, 'dp', 'tensor')
- grad_norm_gain: float32 [2, 1024], replicated
- grad_conv_value_w: float32 [2, 4, 2048], P(None, None, 'tensor')
- grad_conv_value_b: float32 [2, 2048], P(None, 'tensor')
- grad_conv_shared_w: float32 [2, 4, 256], replicated
- grad_conv_shared_b: float32 [2, 256], replicated
- grad_step_bias: float32 [2, 32], P(None, 'tensor')
- grad_decay_log: float32 [2, 32], P(None, 'tensor')
- grad_skip_gain: float32 [2, 32], P(None, 'tensor')
- grad_gate_gain: float32 [2, 2048], P(None, 'tensor')
The draws below stay inside these ranges and needn't reach their ends.
Inputs may be any that keep to these rules, and one draw needn't show every extreme that they name: Each row lists the first positions of its 4 documents in increasing order, the first being 0; in each row one document starts before position 512 and ends at position 1536 or later.
All inputs are finite; a program needn't handle non-finite values.
Results may differ from the reference program's by a relative error of at most 0.013.
Values may be sent and summed in bfloat16 or wider, within the bound.
A program may use at most 256 MiB of HBM per device.

```python
import jax
import jax.numpy as jnp
from jax import lax

D = 1024
INNER = 2048
HEADS = 32
STATE = 128
CONV = 4
SPAN = 256
LAYERS = 2
SEGS = 4
TOK_DEV = 512
ROWS = 8
TOKENS = 16384
N_TENSOR = 4


def draw_starts(key, part):
    key = jax.random.fold_in(key, 7)
    long_key = jax.random.fold_in(key, 1)
    jitter_key = jax.random.fold_in(key, 2)
    pitch = TOK_DEV // SEGS
    longest = jax.random.randint(long_key, (ROWS, 1), 0, SEGS)
    jitter = jax.random.randint(jitter_key, (ROWS, SEGS), 0, pitch)
    index = jnp.arange(SEGS, dtype=jnp.int32)[None, :]
    early = index * pitch + jitter
    late = 3 * TOK_DEV + 1 + (index - 1) * pitch + jitter
    chosen = jnp.where(index <= longest, early, late)
    chosen = jnp.where(index == 0, 0, chosen)
    return chosen.astype(jnp.int32)


def shard_levels(rng, shape, cuts, low, high):
    factor_of, own = 1.0, jax.random.fold_in(rng, 6)
    for axis_at, shards_of in cuts:
        draws = jnp.exp(jax.random.uniform(jax.random.fold_in(own, axis_at), (shards_of,), jnp.float32, low / len(cuts), high / len(cuts)))
        factor_of = factor_of * jnp.repeat(draws, shape[axis_at] // shards_of).reshape([-1 if axis == axis_at else 1 for axis in range(len(shape))])
    return factor_of


def scatter_about(own_key, dims, spread, most, split=(), kind=jnp.bfloat16):
    entries = spread * jax.random.normal(own_key, dims, jnp.float32)
    if split:
        entries = entries * shard_levels(own_key, dims, split, -0.22, 0.18)
    return jnp.clip(entries, -most, most).astype(kind)


def setup_inputs(seed: int = 0) -> dict:
    key_list = jax.random.split(jax.random.key(seed), 17)
    return {
        "tokens": scatter_about(key_list[0], (TOKENS, D), 1.0, 6.0, ((0, 32),)),
        "gate_value_weight": scatter_about(key_list[1], (LAYERS, D, 2, INNER), D ** -0.5, 0.1875, ((1, 8), (3, 4))),
        "w_bc": scatter_about(key_list[2], (LAYERS, D, 2 * STATE), D ** -0.5, 0.1875, ((1, 8),)),
        "w_dt": scatter_about(key_list[3], (LAYERS, D, HEADS), D ** -0.5, 0.1875, ((1, 8), (2, 4))),
        "w_out": scatter_about(key_list[4], (LAYERS, D, INNER), INNER ** -0.5, 0.125, ((1, 8), (2, 4))),
        "norm_gain": jnp.clip(1.0 + 0.1 * jax.random.normal(key_list[5], (LAYERS, D), jnp.float32), 0.5, 1.5),
        "conv_value_w": scatter_about(key_list[6], (LAYERS, CONV, INNER), 0.5, 3.0, ((2, 4),), jnp.float32),
        "conv_value_b": scatter_about(key_list[7], (LAYERS, INNER), 0.3, 2.0, ((1, 4),), jnp.float32),
        "conv_shared_w": scatter_about(key_list[8], (LAYERS, CONV, 2 * STATE), 0.5, 3.0, (), jnp.float32),
        "conv_shared_b": scatter_about(key_list[9], (LAYERS, 2 * STATE), 0.3, 2.0, (), jnp.float32),
        "step_bias": jnp.clip(-7.0 + 4.0 * jax.random.uniform(key_list[10], (LAYERS, HEADS), jnp.float32) ** shard_levels(key_list[10], (LAYERS, HEADS), ((1, 4),), -0.2, 0.2), -7.0, -3.0),
        "decay_log": jnp.clip(2.77 * jax.random.uniform(key_list[11], (LAYERS, HEADS), jnp.float32) ** shard_levels(key_list[11], (LAYERS, HEADS), ((1, 4),), -0.2, 0.2), 0.0, 2.77),
        "skip_gain": jnp.clip(0.5 + 1.0 * jax.random.uniform(key_list[12], (LAYERS, HEADS), jnp.float32) ** shard_levels(key_list[12], (LAYERS, HEADS), ((1, 4),), -0.2, 0.2), 0.5, 1.5),
        "gate_gain": jnp.clip(1.0 + 0.1 * jax.random.normal(key_list[13], (LAYERS, INNER), jnp.float32), 0.5, 1.5),
        "starts": draw_starts(jax.random.fold_in(key_list[16], 71), 0),
        "cotangent": scatter_about(key_list[15], (TOKENS, D), 1.0, 6.0, ((0, 32),)),
    }


norm_eps = 1e-05
highest_precision = lax.Precision.HIGHEST

@jax.custom_vjp
def low(v):
    return lax.optimization_barrier(v.astype(jnp.bfloat16)).astype(jnp.float32)

@jax.custom_vjp
def low_back(v):
    return v

def low_keep(v):
    return (low(v), None)

def low_pass(kept, grad):
    return (grad,)

def back_keep(v):
    return (v, None)

def back_low(kept, grad):
    return (low(grad),)
low.defvjp(low_keep, low_pass)
low_back.defvjp(back_keep, back_low)

def causal_conv(values, weight, bias, segment):
    length = values.shape[0]
    total = jnp.zeros_like(values) + bias
    for shift in range(weight.shape[0]):
        moved = jnp.pad(values, ((shift, 0), (0, 0)))[:length]
        moved_label = jnp.pad(segment, (shift, 0), constant_values=-1)[:length]
        keep = (moved_label == segment).astype(values.dtype)
        total = total + weight[shift] * moved * keep[:, None]
    return total

def span_scan(per_head, steps, decays, in_map, out_map, segment):
    length, heads, width = per_head.shape
    count = length // SPAN
    blocks = (per_head.reshape(count, SPAN, heads, width), steps.reshape(count, SPAN, heads), decays.reshape(count, SPAN, heads), in_map.reshape(count, SPAN, -1), out_map.reshape(count, SPAN, -1), segment.reshape(count, SPAN))

    def advance(carry, block):
        state, before = carry
        values, sizes, rates, keys_in, reads_out, labels = block
        summed = jnp.cumsum(rates, axis=0)
        order = jnp.arange(SPAN, dtype=jnp.int32)
        same = (labels[:, None] == labels[None, :]) & (order[:, None] >= order[None, :])
        across = summed.T[:, :, None] - summed.T[:, None, :]
        decay_mask = jnp.where(same[None], jnp.exp(jnp.where(same[None], across, 0.0)), 0.0)
        intersection = jnp.dot(reads_out, keys_in.T, precision=highest_precision)
        layer_parameters = intersection[None] * decay_mask * sizes.T[:, None, :]
        inside = jnp.einsum('hts,shp->thp', layer_parameters, values, precision=highest_precision)
        carried = (labels == before).astype(summed.dtype)
        reach = jnp.exp(summed) * carried[:, None]
        outside = jnp.einsum('tn,hpn->thp', reads_out, state, precision=highest_precision) * reach[:, :, None]
        final = labels[SPAN - 1].astype(jnp.int32)
        tail = (labels == final).astype(summed.dtype)
        toward = jnp.exp(summed[SPAN - 1][None, :] - summed) * sizes * tail[:, None]
        kept_part = jnp.exp(summed[SPAN - 1]) * (final == before).astype(summed.dtype)
        weighted = values * toward[:, :, None]
        fresh = jnp.einsum('shp,sn->hpn', weighted, keys_in, precision=highest_precision)
        return ((kept_part[:, None, None] * state + fresh, final), inside + outside)
    begin = (jnp.zeros((heads, width, in_map.shape[1]), per_head.dtype), jnp.int32(-1))
    ended, outputs = lax.scan(jax.checkpoint(advance), begin, blocks)
    return outputs.reshape(length, heads, width)

def mixer_local(gate_in, value_in, shared_in, step_in, conv_value_w, conv_value_b, conv_shared_w, conv_shared_b, step_bias, decay_log, skip_gain, segment=None):
    state_size = shared_in.shape[1] // 2
    heads = step_in.shape[1]
    values = jax.nn.silu(causal_conv(value_in, conv_value_w, conv_value_b, segment))
    shared = jax.nn.silu(causal_conv(shared_in, conv_shared_w, conv_shared_b, segment))
    steps = jax.nn.softplus(step_in + step_bias)
    decays = -steps * jnp.exp(decay_log)
    per_head = values.reshape(values.shape[0], heads, -1)
    scanned = span_scan(per_head, steps, decays, shared[:, :state_size], shared[:, state_size:], segment)
    scanned = scanned + skip_gain[None, :, None] * per_head
    return scanned.reshape(values.shape) * jax.nn.silu(gate_in)

def layer_step(resid, layer_parameters, labels):
    gate_value_weight, w_bc, w_dt, w_out, norm_gain, conv_value_w, conv_value_b, conv_shared_w, conv_shared_b, step_bias, decay_log, skip_gain, gate_gain = layer_parameters
    length = N_TENSOR * TOK_DEV
    scaled = resid * lax.rsqrt(lax.optimization_barrier(jnp.mean(resid * resid, axis=1, keepdims=True)) + norm_eps) * norm_gain
    normed = low(scaled).reshape(-1, length, resid.shape[1])

    def row_mixer(item):
        input_rows, segment = item
        paired_pieces = low_back(jnp.einsum('ql,lga->qga', input_rows, gate_value_weight, precision=highest_precision))
        shared = low_back(jnp.dot(input_rows, w_bc, precision=highest_precision))
        step_in = low_back(jnp.dot(input_rows, w_dt, precision=highest_precision))
        gated = mixer_local(paired_pieces[:, 0], paired_pieces[:, 1], shared, step_in, conv_value_w, conv_value_b, conv_shared_w, conv_shared_b, step_bias, decay_log, skip_gain, segment=segment)
        factor = lax.rsqrt(lax.optimization_barrier(jnp.mean(gated * gated, axis=1, keepdims=True)) + norm_eps)
        mixed_in = low(gated * factor * gate_gain)
        return jnp.einsum('ti,di->td', mixed_in, w_out, precision=highest_precision)
    branch = lax.map(jax.checkpoint(row_mixer), (normed, labels))
    return resid + low_back(branch.reshape(resid.shape))

def reference(tokens, gate_value_weight, w_bc, w_dt, w_out, norm_gain, conv_value_w, conv_value_b, conv_shared_w, conv_shared_b, step_bias, decay_log, skip_gain, gate_gain, starts, cotangent):
    length = N_TENSOR * TOK_DEV
    positions = jnp.arange(length, dtype=jnp.int32)
    labels = lax.optimization_barrier(jnp.sum((positions[None, :, None] >= starts[:, None, :]).astype(jnp.int32), axis=2, dtype=jnp.int32)) - jnp.int32(1)
    params = tuple((item.astype(jnp.float32) for item in (gate_value_weight, w_bc, w_dt, w_out, norm_gain, conv_value_w, conv_value_b, conv_shared_w, conv_shared_b, step_bias, decay_log, skip_gain, gate_gain)))

    def forward(resid, layer_parameters):
        for layer in range(LAYERS):
            resid = layer_step(resid, tuple((item[layer] for item in layer_parameters)), labels)
        return resid
    result, pullback = jax.vjp(forward, tokens.astype(jnp.float32), params)
    grad_in, grads = pullback(cotangent.astype(jnp.float32))
    return (result.astype(jnp.bfloat16), grad_in, grads[0], grads[1], grads[2], grads[3], grads[4], grads[5], grads[6], grads[7], grads[8], grads[9], grads[10], grads[11], grads[12])
```

```python
from functools import partial

import jax
import jax.numpy as jnp
from jax import lax
from jax.experimental import pallas as pl
from jax.experimental.pallas import tpu as pltpu
from jax.sharding import PartitionSpec as P

LAYERS = 2
EPS = 1e-05
HALO = 16
CH = 128
GC = 256
HD = 64
HG = GC // HD
LANES = 128
STATE = 128
NEG = -1e30
VMEM_LIMIT = 60 * 1024 * 1024
MESH = pl.DeviceIdType.MESH
HI = lax.Precision.HIGHEST
F32 = jnp.float32
BF = jnp.bfloat16


def dot_nn(a, b, precision=None):
    return lax.dot_general(a, b, (((1,), (0,)), ((), ())), precision=precision, preferred_element_type=F32)


def dot_nt(a, b):
    return lax.dot_general(a, b, (((1,), (1,)), ((), ())), preferred_element_type=F32)


def dot_tn(a, b):
    return lax.dot_general(a, b, (((0,), (0,)), ((), ())), preferred_element_type=F32)


def sigmoid(v):
    return 0.5 * jnp.tanh(0.5 * v) + 0.5


def twice(v):
    return jnp.concatenate([v, v], axis=1)


def split2(v):
    high = v.astype(BF)
    return jnp.concatenate([high, (v - high.astype(F32)).astype(BF)], axis=1)


def iota2(shape, dim):
    return lax.broadcasted_iota(jnp.int32, shape, dim)


def spread(group):
    row = iota2((2 * LANES, GC), 0) % LANES
    head = iota2((2 * LANES, GC), 1) // HD + group * HG
    return (row == head).astype(F32).astype(BF)


def collect(group):
    head = (iota2((2 * GC, LANES), 0) % GC) // HD + group * HG
    return (head == iota2((2 * GC, LANES), 1)).astype(F32).astype(BF)


def conv(load, keep_ref, weights, tokens):
    total = weights[4:5] + weights[0:1] * load(0)
    for k in range(1, 4):
        total = total + weights[k : k + 1] * (load(k) * twice(keep_ref[k - 1]))
    return total


def conv_back(grad, load, keep_ref, weights, tokens):
    rows = []
    total = None
    for k in range(4):
        part = grad if k == 0 else grad * twice(keep_ref[k - 1])
        rows.append(jnp.sum(part * load(k), axis=0, keepdims=True))
        wide = jnp.concatenate([jnp.zeros((HALO, grad.shape[1]), F32), weights[k : k + 1] * part], axis=0)
        if k:
            wide = pltpu.roll(wide, tokens + HALO - k, 0)
        total = wide if total is None else total + wide
    rows.append(jnp.sum(grad, axis=0, keepdims=True))
    return total, rows


def step_terms(step_in, heads_ref, carried_ref, tail_ref, kept_ref, tokens):
    chunks = tokens // CH
    raw = step_in + heads_ref[0:1]
    steps = jnp.maximum(raw, 0.0) + jnp.log1p(jnp.exp(-jnp.abs(raw)))
    rates = -steps * heads_ref[1:2]
    lower = (iota2((CH, CH), 0) >= iota2((CH, CH), 1)).astype(F32)
    sums, toward, kept = [], [], []
    for c in range(chunks):
        summed = dot_nn(lower, rates[c * CH : (c + 1) * CH], HI)
        last = summed[CH - 1 : CH]
        sums.append(summed)
        toward.append(jnp.exp(last - summed))
        kept.append(jnp.exp(last) * kept_ref[c : c + 1])
    kept.append(jnp.zeros((8 - chunks, LANES), F32))
    summed = jnp.concatenate(sums, axis=0)
    toward = jnp.concatenate(toward, axis=0) * tail_ref[...]
    reach = jnp.exp(summed) * carried_ref[...]
    return raw, steps, rates, summed, toward, reach, jnp.concatenate(kept, axis=0)


def put_sums(summed, col_ref, row_ref, groups, tokens):
    for c in range(tokens // CH):
        turned = summed[c * CH : (c + 1) * CH].T
        for group in range(groups):
            row_ref[group, 0:HG, c * CH : (c + 1) * CH] = turned[group * HG : (group + 1) * HG]
    for group in range(groups):
        shift = (LANES - group * HG) % LANES
        col_ref[group] = pltpu.roll(summed, shift, 1) if shift else summed


def halves(v):
    first = iota2(v.shape, 1) < HD
    return jnp.concatenate([jnp.where(first, v, 0.0), jnp.where(first, 0.0, v)], axis=0).astype(BF)


def forward_kernel(
    dims,
    x_ref, gain_ref, w_ref, wo_ref, wbc_ref, wdt_ref, gp_ref, gpb_ref, csw_ref, heads_ref,
    keep_ref, bias_ref, carried_ref, tail_ref, kept_ref,
    next_ref, normed_ref, gate_ref, val_ref, y_ref, state_ref, shared_ref, step_ref, r_ref,
    nx, inb, inbt, outb, cross, col, row, terms, ke, intra, xs, gs, fresh, fold, incoming, outgoing, branch, squares,
    halo_send, halo_recv, send, recv,
):
    pieces, groups, tokens, skew = dims
    chunks = tokens // CH
    i = pl.program_id(0)
    z = lax.axis_index("tensor")
    right, left = jnp.minimum(z + 1, pieces - 1), jnp.maximum(z - 1, 0)

    def halo_copy():
        return pltpu.make_async_remote_copy(
            src_ref=nx.at[pl.ds(tokens, HALO)], dst_ref=nx.at[pl.ds(0, HALO)],
            send_sem=halo_send, recv_sem=halo_recv, device_id={"tensor": right}, device_id_type=MESH,
        )

    def state_copy(group):
        return pltpu.make_async_remote_copy(
            src_ref=outgoing.at[group], dst_ref=incoming.at[group],
            send_sem=send.at[group], recv_sem=recv.at[group], device_id={"tensor": right}, device_id_type=MESH,
        )

    @pl.when(i == 0)
    def _():
        barrier = pltpu.get_barrier_semaphore()

        @pl.when(z > 0)
        def _():
            pl.semaphore_signal(barrier, inc=1, device_id={"tensor": left}, device_id_type=MESH)

        x = x_ref[...]
        scale = lax.rsqrt(jnp.mean(x * x, axis=1, keepdims=True) + EPS)
        nx[pl.ds(HALO, tokens), :] = (x * scale * gain_ref[...]).astype(BF)

        @pl.when(z < pieces - 1)
        def _():
            pl.semaphore_wait(barrier, 1)
            halo_copy().start()

        @pl.when(z == 0)
        def _():
            nx[pl.ds(0, HALO), :] = jnp.zeros((HALO, nx.shape[1]), BF)
            incoming[...] = jnp.zeros(incoming.shape, BF)

        step_in = dot_nn(nx[pl.ds(HALO, tokens), :], wdt_ref[...])
        step_ref[...] = step_in
        _, steps, _, summed, toward, reach, kept = step_terms(
            step_in, heads_ref, carried_ref, tail_ref, kept_ref, tokens
        )
        put_sums(summed, col, row, groups, tokens)
        terms[0] = split2(steps)
        terms[1] = split2(toward)
        terms[2] = split2(reach)
        kept2 = split2(kept)
        for group in range(groups):
            ke[group] = dot_nn(kept2, spread(group))

        @pl.when(z > 0)
        def _():
            halo_copy().wait_recv()

        shared_ref[...] = dot_nn(nx[...], wbc_ref[...])
        mixed = conv(lambda k: shared_ref[pl.ds(HALO - k, tokens), :], keep_ref, csw_ref[...], tokens)
        maps = mixed * sigmoid(mixed)
        for c in range(chunks):
            part = maps[c * CH : (c + 1) * CH]
            into, out = part[:, :STATE], part[:, STATE:].astype(BF)
            inb[c], outb[c], inbt[c] = into.astype(BF), out, into.T.astype(BF)
            cross[c] = dot_nt(out, into.astype(BF))
        branch[...] = jnp.zeros(branch.shape, F32)
        squares[...] = jnp.zeros(squares.shape, F32)

    @pl.when(i < groups)
    def _():
        depth = nx.shape[1]
        group = i
        slot = lax.rem(group, skew + 1)
        gate_ref[0] = dot_nn(nx[pl.ds(HALO, tokens), :], w_ref[:, 0, 0].reshape(depth, GC))
        val_ref[0] = dot_nn(nx[...], w_ref[:, 0, 1].reshape(depth, GC))
        mixed = conv(lambda k: val_ref[0, pl.ds(HALO - k, tokens), :], keep_ref, gp_ref[0], tokens)
        xs[slot] = mixed * sigmoid(mixed)
        gate = gate_ref[0]
        gs[slot] = gate * sigmoid(gate)
        spreader = spread(group)
        state = jnp.zeros((STATE, GC), F32)
        for c in range(chunks):
            rows = pl.ds(c * CH, CH)
            sized = xs[slot, rows, :] * dot_nn(terms[0, rows, :], spreader)
            weighted = (sized * dot_nn(terms[1, rows, :], spreader)).astype(BF)
            new = dot_nn(inbt[c], weighted)
            fresh[slot, c] = new
            state = ke[group, c : c + 1] * state + new
            for pair in range(HG // 2):
                lanes = pl.ds(pair * LANES, LANES)
                decayed = []
                for j in (2 * pair, 2 * pair + 1):
                    across = col[group, rows, j : j + 1] - row[group, j : j + 1, rows]
                    decayed.append((cross[c] * jnp.exp(jnp.minimum(across, bias_ref[c]))).astype(BF))
                blocks = halves(sized[:, pair * LANES : (pair + 1) * LANES])
                intra[slot, rows, lanes] = dot_nn(jnp.concatenate(decayed, axis=1), blocks)
        fold[slot] = state

    j = i - z

    @pl.when(jnp.logical_and(j >= 0, j < groups))
    def _():
        @pl.when(z > 0)
        def _():
            state_copy(j).wait_recv()

        @pl.when(z < pieces - 1)
        def _():
            total = ke[j, 0:1]
            for c in range(1, chunks):
                total = total * ke[j, c : c + 1]
            outgoing[j] = (total * incoming[j].astype(F32) + fold[lax.rem(j, skew + 1)]).astype(BF)
            state_copy(j).start()

    @pl.when(i >= skew)
    def _():
        group = i - skew
        slot = lax.rem(group, skew + 1)
        depth = nx.shape[1]
        spreader = spread(group)
        gp = gpb_ref[0]
        state = incoming[group].astype(F32)
        for c in range(chunks):
            rows = pl.ds(c * CH, CH)
            low = state.astype(BF)
            state_ref[0, c] = low
            y = intra[slot, rows, :] + dot_nn(outb[c], low) * dot_nn(terms[2, rows, :], spreader)
            y_ref[0, rows, :] = y
            gated = (y + gp[6:7] * xs[slot, rows, :]) * gs[slot, rows, :]
            squares[rows, :] += jnp.sum(gated * gated, axis=1, keepdims=True)
            intra[slot, rows, :] = gated * gp[5:6]
            if c < chunks - 1:
                state = ke[group, c : c + 1] * state + fresh[slot, c]
        branch[...] += dot_nt(intra[slot].astype(BF), wo_ref[:, 0].reshape(depth, GC))

    @pl.when(i == groups + skew - 1)
    def _():
        inner = groups * GC
        factor = lax.rsqrt(squares[...] * (1.0 / inner) + EPS)
        r_ref[...] = factor
        next_ref[...] = x_ref[...] + branch[...] * factor[:, 0:1]
        normed_ref[...] = nx[...]

        @pl.when(z < pieces - 1)
        def _():
            halo_copy().wait_send()
            for group in range(groups):
                state_copy(group).wait_send()


def backward_kernel(
    dims,
    g_ref, x_ref, next_ref, gain_ref, normed_ref, r_ref, w_ref, wo_ref, wbc_ref, wdt_ref, gp_ref, gpb_ref, csw_ref,
    heads_ref, keep_ref, biast_ref, carried_ref, tail_ref, kept_ref,
    gate_ref, val_ref, y_ref, valb_ref, yb_ref, state_ref, shared_ref, step_ref,
    gx_ref, gw_ref, gwo_ref, gbc_ref, gdt_ref, ggp_ref, ggate_ref, gcs_ref, gheads_ref, ggain_ref,
    gb, gbt, nxt, nht, r2, inb, outb, outbt, crosst, col, row, terms, ke,
    dys, xs, fs, dgs, us, fold, incoming, outgoing, gnorm, dct, dbt, dgt, sd, sp, sq, se, dxd, hrecv,
    halo_send, halo_recv, send, recv,
):
    pieces, groups, tokens, skew = dims
    chunks = tokens // CH
    i = pl.program_id(0)
    z = lax.axis_index("tensor")
    right, left = jnp.minimum(z + 1, pieces - 1), jnp.maximum(z - 1, 0)
    back = pieces - 1 - z
    depth = x_ref.shape[1]
    inner = groups * GC

    def halo_copy():
        return pltpu.make_async_remote_copy(
            src_ref=gnorm.at[pl.ds(0, HALO)], dst_ref=hrecv,
            send_sem=halo_send, recv_sem=halo_recv, device_id={"tensor": left}, device_id_type=MESH,
        )

    def state_copy(group):
        return pltpu.make_async_remote_copy(
            src_ref=outgoing.at[group], dst_ref=incoming.at[group],
            send_sem=send.at[group], recv_sem=recv.at[group], device_id={"tensor": left}, device_id_type=MESH,
        )

    def shared_conv():
        return conv(lambda k: shared_ref[pl.ds(HALO - k, tokens), :], keep_ref, csw_ref[...], tokens)

    @pl.when(i == 0)
    def _():
        barrier = pltpu.get_barrier_semaphore()

        @pl.when(z < pieces - 1)
        def _():
            pl.semaphore_signal(barrier, inc=1, device_id={"tensor": right}, device_id_type=MESH)

        @pl.when(z > 0)
        def _():
            pl.semaphore_wait(barrier, 1)

        @pl.when(z == pieces - 1)
        def _():
            incoming[...] = jnp.zeros(incoming.shape, BF)

        low = g_ref[...].astype(BF)
        gb[...] = low
        gbt[...] = low.T
        dots = jnp.sum(low.astype(F32) * (next_ref[...] - x_ref[...]), axis=1, keepdims=True)
        r = r_ref[...]
        r2[...] = r * r * dots * (1.0 / inner)
        nxt[...] = normed_ref[pl.ds(HALO, tokens), :].T
        nht[...] = normed_ref[pl.ds(0, HALO), :].T
        _, steps, _, summed, toward, reach, kept = step_terms(
            step_ref[...], heads_ref, carried_ref, tail_ref, kept_ref, tokens
        )
        put_sums(summed, col, row, groups, tokens)
        terms[0] = split2(steps)
        terms[1] = split2(toward)
        terms[2] = split2(reach)
        kept2 = split2(kept)
        for group in range(groups):
            ke[group] = dot_nn(kept2, spread(group))
        mixed = shared_conv()
        maps = mixed * sigmoid(mixed)
        for c in range(chunks):
            part = maps[c * CH : (c + 1) * CH]
            into, out = part[:, :STATE].astype(BF), part[:, STATE:]
            inb[c], outb[c], outbt[c] = into, out.astype(BF), out.T.astype(BF)
            crosst[c] = dot_nt(into, out.astype(BF))
        for ref in (gnorm, dct, dbt, dgt, sd, sp, sq, se):
            ref[...] = jnp.zeros(ref.shape, F32)

    @pl.when(i < groups)
    def _():
        group = i
        slot = lax.rem(group, skew + 1)
        gp = gp_ref[0]
        mixed = conv(lambda k: val_ref[0, pl.ds(HALO - k, tokens), :], keep_ref, gp, tokens)
        part = sigmoid(mixed)
        x = mixed * part
        xs[slot] = x
        fs[slot] = part + x * (1.0 - part)
        r = twice(r_ref[...])
        gm = dot_nn(gb[...], wo_ref[:, 0].reshape(depth, GC))
        scan = y_ref[0] + gp[6:7] * x
        gate = gate_ref[0]
        part = sigmoid(gate)
        silu = gate * part
        gated = scan * silu
        normal = gated * r
        gwo_ref[:, 0] = dot_nn(gbt[...], (normal * gp[5:6]).astype(BF)).astype(BF).reshape(gwo_ref.shape[0], -1, GC)
        ggated = r * gp[5:6] * gm - gated * twice(r2[...])
        dy = ggated * silu
        dys[slot] = dy
        dgs[slot] = (ggated * scan * (part + silu * (1.0 - part))).astype(BF)
        ggate_ref[0] = jnp.concatenate(
            [
                jnp.sum(gm * normal, axis=0, keepdims=True),
                jnp.sum(dy * x, axis=0, keepdims=True),
                jnp.zeros((6, GC), F32),
            ],
            axis=0,
        )
        spreader = spread(group)
        state = jnp.zeros((STATE, GC), F32)
        for c in reversed(range(chunks)):
            rows = pl.ds(c * CH, CH)
            reached = (dys[slot, rows, :] * dot_nn(terms[2, rows, :], spreader)).astype(BF)
            new = dot_nn(outbt[c], reached)
            us[slot, c] = new
            state = ke[group, c : c + 1] * state + new
        fold[slot] = state

    j = i - back

    @pl.when(jnp.logical_and(j >= 0, j < groups))
    def _():
        @pl.when(z < pieces - 1)
        def _():
            state_copy(j).wait_recv()

        @pl.when(z > 0)
        def _():
            total = ke[j, 0:1]
            for c in range(1, chunks):
                total = total * ke[j, c : c + 1]
            outgoing[j] = (total * incoming[j].astype(F32) + fold[lax.rem(j, skew + 1)]).astype(BF)
            state_copy(j).start()

    @pl.when(i >= skew)
    def _():
        group = i - skew
        slot = lax.rem(group, skew + 1)
        gp = gpb_ref[0]
        spreader, collector = spread(group), collect(group)
        grad = incoming[group].astype(F32)
        ends = [None] * chunks
        for c in reversed(range(chunks)):
            rows = pl.ds(c * CH, CH)
            low = grad.astype(BF)
            state = state_ref[0, c]
            ends[c] = jnp.sum(low.astype(F32) * state.astype(F32), axis=0, keepdims=True) * ke[group, c : c + 1]
            grad = ke[group, c : c + 1] * grad + us[slot, c]
            x = xs[slot, rows, :]
            dy = dys[slot, rows, :]
            steps = dot_nn(terms[0, rows, :], spreader)
            toward = dot_nn(terms[1, rows, :], spreader)
            reached = (dy * dot_nn(terms[2, rows, :], spreader)).astype(BF)
            sized = x * steps
            weighted = (sized * toward).astype(BF)
            later = dot_nn(inb[c], low) * toward
            dbt[c] += dot_nt(weighted, low)
            dct[c] += dot_nt(reached, state)
            parts = []
            cross = crosst[c]
            pairs_total = jnp.zeros((CH, CH), F32)
            for pair in range(HG // 2):
                at = slice(pair * LANES, (pair + 1) * LANES)
                dyp = dy[:, at]
                products = dot_nt(halves(sized[:, at]), dyp.astype(BF))
                decayed = []
                for n in range(2):
                    h = 2 * pair + n
                    across = row[group, h : h + 1, rows] - col[group, rows, h : h + 1]
                    decay = jnp.exp(jnp.minimum(across, biast_ref[c]))
                    decayed.append((cross * decay).astype(BF))
                    pairs_total = pairs_total + products[n * CH : (n + 1) * CH] * decay
                parts.append(dot_nn(jnp.concatenate(decayed, axis=1), halves(dyp)))
            dgt[c] += pairs_total
            within = jnp.concatenate(parts, axis=1)
            whole = within + later
            lowered = dy.astype(BF).astype(F32) * yb_ref[0, rows, :] - sized.astype(BF).astype(F32) * within
            sd[rows, :] += dot_nn(split2(whole * x), collector)
            sp[rows, :] += dot_nn(split2(lowered), collector)
            sq[rows, :] += dot_nn(split2(sized * later), collector)
            dxd[rows, :] = (whole * steps + gp[6:7] * dy) * fs[slot, rows, :]
        ends.append(jnp.zeros((8 - chunks, GC), F32))
        se[...] += dot_nn(split2(jnp.concatenate(ends, axis=0)), collector)
        wide, sums = conv_back(
            dxd[...], lambda k: valb_ref[0, pl.ds(HALO - k, tokens), :], keep_ref, gp, tokens
        )
        ggp_ref[0] = jnp.concatenate(sums + [jnp.zeros((3, GC), F32)], axis=0)
        wide = wide.astype(BF)
        dgate = dgs[slot]
        shape = (gw_ref.shape[0], -1, GC)
        gw_ref[:, 0, 0] = dot_nn(nxt[...], dgate).astype(BF).reshape(shape)
        gw_ref[:, 0, 1] = (dot_nn(nxt[...], wide[HALO:]) + dot_nn(nht[...], wide[:HALO])).astype(BF).reshape(shape)
        gnorm[...] += dot_nt(wide, w_ref[:, 0, 1].reshape(depth, GC))
        gnorm[pl.ds(HALO, tokens), :] += dot_nt(dgate, w_ref[:, 0, 0].reshape(depth, GC))

    @pl.when(i == groups + skew - 1)
    def _():
        upper = (iota2((CH, CH), 0) <= iota2((CH, CH), 1)).astype(F32)
        before = (iota2((CH, CH), 0) > iota2((CH, CH), 1)).astype(F32)
        raw, steps, rates, _, _, _, _ = step_terms(step_ref[...], heads_ref, carried_ref, tail_ref, kept_ref, tokens)
        drates, dmaps = [], []
        for c in range(chunks):
            rows = slice(c * CH, (c + 1) * CH)
            drates.append(dot_nn(upper, sp[rows, :], HI) + dot_nn(before, sq[rows, :], HI) + se[c : c + 1])
            low = dgt[c].astype(BF)
            into = dbt[c] + dot_nn(low, outb[c])
            out = dct[c] + dot_tn(low, inb[c])
            dmaps.append(jnp.concatenate([into, out], axis=1))
        drate = jnp.concatenate(drates, axis=0)
        dstep = (sd[...] - drate * heads_ref[1:2]) * sigmoid(raw)
        gheads_ref[...] = jnp.concatenate(
            [
                jnp.sum(dstep, axis=0, keepdims=True),
                jnp.sum(drate * rates, axis=0, keepdims=True),
                jnp.zeros((6, LANES), F32),
            ],
            axis=0,
        )
        mixed = shared_conv()
        part = sigmoid(mixed)
        dmixed = jnp.concatenate(dmaps, axis=0) * (part + mixed * part * (1.0 - part))
        wide, sums = conv_back(
            dmixed, lambda k: shared_ref[pl.ds(HALO - k, tokens), :], keep_ref, csw_ref[...], tokens
        )
        gcs_ref[...] = jnp.concatenate(sums + [jnp.zeros((3, 2 * STATE), F32)], axis=0)
        wide = wide.astype(BF)
        dstep = dstep.astype(BF)
        gnorm[...] += dot_nt(wide, wbc_ref[...])
        gnorm[pl.ds(HALO, tokens), :] += dot_nt(dstep, wdt_ref[...])

        @pl.when(z > 0)
        def _():
            halo_copy().start()

        gbc_ref[...] = (dot_nn(nxt[...], wide[HALO:]) + dot_nn(nht[...], wide[:HALO])).astype(BF)
        gdt_ref[...] = dot_nn(nxt[...], dstep).astype(BF)

        @pl.when(z < pieces - 1)
        def _():
            halo_copy().wait_recv()
            gnorm[pl.ds(tokens, HALO), :] += hrecv[...]

        x = x_ref[...]
        gn = gnorm[pl.ds(HALO, tokens), :]
        q = lax.rsqrt(jnp.mean(x * x, axis=1, keepdims=True) + EPS)
        gained = gn * gain_ref[...]
        inside = jnp.sum(gained * x, axis=1, keepdims=True) * (1.0 / depth)
        gx_ref[...] = g_ref[...] + q * gained - x * (q * q * q * inside)
        ggain_ref[...] = jnp.concatenate(
            [jnp.sum(gn * x * q, axis=0, keepdims=True), jnp.zeros((7, depth), F32)], axis=0
        )

        @pl.when(z > 0)
        def _():
            halo_copy().wait_send()
            for group in range(groups):
                state_copy(group).wait_send()


def whole(shape):
    return pl.BlockSpec(shape, lambda i: (0,) * len(shape))


def layer_forward(dims, x, gain, w, wo, wbc, wdt, gp, csw, heads, masks):
    pieces, groups, tokens, skew = dims
    keep, bias, _, carried, tail, kept = masks
    chunks = tokens // CH
    depth = x.shape[1]
    dp, _, _, share, wide = w.shape
    per = wide // GC
    ext = tokens + HALO
    last = groups - 1
    slots = skew + 1

    def early(i):
        return jnp.minimum(i, last)

    def late(i):
        return jnp.maximum(i - skew, 0)

    def block(rows, at):
        return pl.BlockSpec((1, rows, GC), lambda i: (at(i), 0, 0))

    return pl.pallas_call(
        partial(forward_kernel, dims),
        grid=(groups + skew,),
        in_specs=[
            whole((tokens, depth)), whole((1, depth)),
            pl.BlockSpec((dp, 1, 2, share, GC), lambda i: (0, early(i) // per, 0, 0, early(i) % per)),
            pl.BlockSpec((dp, 1, share, GC), lambda i: (0, late(i) // per, 0, late(i) % per)),
            whole(wbc.shape), whole(wdt.shape), block(8, early), block(8, late), whole(csw.shape), whole(heads.shape),
            whole(keep.shape), whole(bias.shape), whole(carried.shape), whole(tail.shape), whole(kept.shape),
        ],
        out_specs=[
            whole((tokens, depth)), whole((ext, depth)), block(tokens, early), block(ext, early), block(tokens, late),
            pl.BlockSpec((1, chunks, STATE, GC), lambda i: (late(i), 0, 0, 0)),
            whole((ext, 2 * STATE)), whole((tokens, LANES)), whole((tokens, LANES)),
        ],
        out_shape=[
            jax.ShapeDtypeStruct((tokens, depth), F32),
            jax.ShapeDtypeStruct((ext, depth), BF),
            jax.ShapeDtypeStruct((groups, tokens, GC), F32),
            jax.ShapeDtypeStruct((groups, ext, GC), F32),
            jax.ShapeDtypeStruct((groups, tokens, GC), F32),
            jax.ShapeDtypeStruct((groups, chunks, STATE, GC), BF),
            jax.ShapeDtypeStruct((ext, 2 * STATE), F32),
            jax.ShapeDtypeStruct((tokens, LANES), F32),
            jax.ShapeDtypeStruct((tokens, LANES), F32),
        ],
        scratch_shapes=[
            pltpu.VMEM((ext, depth), BF),
            pltpu.VMEM((chunks, CH, STATE), BF),
            pltpu.VMEM((chunks, STATE, CH), BF),
            pltpu.VMEM((chunks, CH, STATE), BF),
            pltpu.VMEM((chunks, CH, CH), F32),
            pltpu.VMEM((groups, tokens, LANES), F32),
            pltpu.VMEM((groups, 8, tokens), F32),
            pltpu.VMEM((3, tokens, 2 * LANES), BF),
            pltpu.VMEM((groups, 8, GC), F32),
            pltpu.VMEM((slots, tokens, GC), F32),
            pltpu.VMEM((slots, tokens, GC), F32),
            pltpu.VMEM((slots, tokens, GC), F32),
            pltpu.VMEM((slots, chunks, STATE, GC), F32),
            pltpu.VMEM((slots, STATE, GC), F32),
            pltpu.VMEM((groups, STATE, GC), BF),
            pltpu.VMEM((groups, STATE, GC), BF),
            pltpu.VMEM((tokens, depth), F32),
            pltpu.VMEM((tokens, LANES), F32),
            pltpu.SemaphoreType.DMA,
            pltpu.SemaphoreType.DMA,
            pltpu.SemaphoreType.DMA((groups,)),
            pltpu.SemaphoreType.DMA((groups,)),
        ],
        compiler_params=pltpu.CompilerParams(
            collective_id=0, has_side_effects=True, vmem_limit_bytes=VMEM_LIMIT, dimension_semantics=("arbitrary",)
        ),
        name="layer_forward",
    )(x, gain, w, wo, wbc, wdt, gp, gp, csw, heads, keep, bias, carried, tail, kept)


def layer_backward(dims, g, x, after, gain, saved, w, wo, wbc, wdt, gp, csw, heads, masks):
    pieces, groups, tokens, skew = dims
    keep, _, biast, carried, tail, kept = masks
    normed, gate, val, y, states, shared, step_in, r = saved
    chunks = tokens // CH
    depth = x.shape[1]
    dp, pieces_w, _, share, wide = w.shape
    per = wide // GC
    ext = tokens + HALO
    last = groups - 1
    slots = skew + 1

    def early(i):
        return jnp.minimum(i, last)

    def late(i):
        return jnp.maximum(i - skew, 0)

    def block(rows, at):
        return pl.BlockSpec((1, rows, GC), lambda i: (at(i), 0, 0))

    def pair_block(at):
        return pl.BlockSpec((dp, 1, 2, share, GC), lambda i: (0, at(i) // per, 0, 0, at(i) % per))

    def single_block(at):
        return pl.BlockSpec((dp, 1, share, GC), lambda i: (0, at(i) // per, 0, at(i) % per))

    return pl.pallas_call(
        partial(backward_kernel, dims),
        grid=(groups + skew,),
        in_specs=[
            whole((tokens, depth)), whole((tokens, depth)), whole((tokens, depth)), whole((1, depth)),
            whole((ext, depth)), whole((tokens, LANES)), pair_block(late), single_block(early),
            whole(wbc.shape), whole(wdt.shape), block(8, early), block(8, late), whole(csw.shape), whole(heads.shape),
            whole(keep.shape), whole(biast.shape), whole(carried.shape), whole(tail.shape), whole(kept.shape),
            block(tokens, early), block(ext, early), block(tokens, early), block(ext, late), block(tokens, late),
            pl.BlockSpec((1, chunks, STATE, GC), lambda i: (late(i), 0, 0, 0)),
            whole((ext, 2 * STATE)), whole((tokens, LANES)),
        ],
        out_specs=[
            whole((tokens, depth)), pair_block(late), single_block(early),
            whole((depth, 2 * STATE)), whole((depth, LANES)), block(8, late), block(8, early),
            whole((8, 2 * STATE)), whole((8, LANES)), whole((8, depth)),
        ],
        out_shape=[
            jax.ShapeDtypeStruct((tokens, depth), F32),
            jax.ShapeDtypeStruct(w.shape, BF),
            jax.ShapeDtypeStruct(wo.shape, BF),
            jax.ShapeDtypeStruct((depth, 2 * STATE), BF),
            jax.ShapeDtypeStruct((depth, LANES), BF),
            jax.ShapeDtypeStruct((groups, 8, GC), F32),
            jax.ShapeDtypeStruct((groups, 8, GC), F32),
            jax.ShapeDtypeStruct((8, 2 * STATE), F32),
            jax.ShapeDtypeStruct((8, LANES), F32),
            jax.ShapeDtypeStruct((8, depth), F32),
        ],
        scratch_shapes=[
            pltpu.VMEM((tokens, depth), BF),
            pltpu.VMEM((depth, tokens), BF),
            pltpu.VMEM((depth, tokens), BF),
            pltpu.VMEM((depth, HALO), BF),
            pltpu.VMEM((tokens, LANES), F32),
            pltpu.VMEM((chunks, CH, STATE), BF),
            pltpu.VMEM((chunks, CH, STATE), BF),
            pltpu.VMEM((chunks, STATE, CH), BF),
            pltpu.VMEM((chunks, CH, CH), F32),
            pltpu.VMEM((groups, tokens, LANES), F32),
            pltpu.VMEM((groups, 8, tokens), F32),
            pltpu.VMEM((3, tokens, 2 * LANES), BF),
            pltpu.VMEM((groups, 8, GC), F32),
            pltpu.VMEM((slots, tokens, GC), F32),
            pltpu.VMEM((slots, tokens, GC), F32),
            pltpu.VMEM((slots, tokens, GC), F32),
            pltpu.VMEM((slots, tokens, GC), BF),
            pltpu.VMEM((slots, chunks, STATE, GC), F32),
            pltpu.VMEM((slots, STATE, GC), F32),
            pltpu.VMEM((groups, STATE, GC), BF),
            pltpu.VMEM((groups, STATE, GC), BF),
            pltpu.VMEM((ext, depth), F32),
            pltpu.VMEM((chunks, CH, STATE), F32),
            pltpu.VMEM((chunks, CH, STATE), F32),
            pltpu.VMEM((chunks, CH, CH), F32),
            pltpu.VMEM((tokens, LANES), F32),
            pltpu.VMEM((tokens, LANES), F32),
            pltpu.VMEM((tokens, LANES), F32),
            pltpu.VMEM((8, LANES), F32),
            pltpu.VMEM((tokens, GC), F32),
            pltpu.VMEM((HALO, depth), F32),
            pltpu.SemaphoreType.DMA,
            pltpu.SemaphoreType.DMA,
            pltpu.SemaphoreType.DMA((groups,)),
            pltpu.SemaphoreType.DMA((groups,)),
        ],
        compiler_params=pltpu.CompilerParams(
            collective_id=1, has_side_effects=True, vmem_limit_bytes=VMEM_LIMIT, dimension_semantics=("arbitrary",)
        ),
        name="layer_backward",
    )(
        g, x, after, gain, normed, r, w, wo, wbc, wdt, gp, gp, csw, heads, keep, biast, carried, tail, kept,
        gate, val, y, val, y, states, shared, step_in,
    )


def build_masks(starts, tokens, z):
    chunks = tokens // CH
    positions = z * tokens - HALO + lax.iota(jnp.int32, tokens + HALO)
    labels = jnp.sum((positions[:, None] >= starts[None, :]).astype(jnp.int32), axis=1) - 1
    own = labels[HALO:]
    keep = jnp.stack([(labels[HALO - k : HALO - k + tokens] == own).astype(F32) for k in range(1, 4)])
    keep = jnp.broadcast_to(keep[:, :, None], (3, tokens, LANES))
    cut = own.reshape(chunks, CH)
    order = lax.iota(jnp.int32, CH)
    seen = (cut[:, :, None] == cut[:, None, :]) & (order[:, None] >= order[None, :])[None]
    bias = jnp.where(seen, 0.0, NEG).astype(F32)
    before = labels[HALO - 1 :: CH][:chunks]
    final = cut[:, CH - 1]
    carried = (cut == before[:, None]).astype(F32).reshape(tokens, 1)
    tail = (cut == final[:, None]).astype(F32).reshape(tokens, 1)
    kept = jnp.pad((final == before).astype(F32), (0, 8 - chunks))[:, None]
    lanes = lambda v: jnp.broadcast_to(v, (v.shape[0], LANES))
    return keep, bias, jnp.swapaxes(bias, 1, 2), lanes(carried), lanes(tail), lanes(kept)


def local(
    tokens, gate_value_weight, w_bc, w_dt, w_out, norm_gain, conv_value_w, conv_value_b, conv_shared_w, conv_shared_b,
    step_bias, decay_log, skip_gain, gate_gain, starts, cotangent,
):
    pieces, dp = lax.axis_size("tensor"), lax.axis_size("dp")
    z = lax.axis_index("tensor")
    count, depth = tokens.shape
    inner = pieces * conv_value_b.shape[1]
    heads = pieces * step_bias.shape[1]
    groups = inner // GC
    dims = (pieces, groups, count, pieces - 1)
    both = ("dp", "tensor")
    masks = build_masks(starts[0], count, z)

    own = conv_value_b.shape[1]
    few = step_bias.shape[1]
    extra = jnp.concatenate([step_bias, decay_log, jnp.zeros((LAYERS, own - 2 * few), F32)], axis=1)
    pack = jnp.concatenate(
        [
            conv_value_w, conv_value_b[:, None], gate_gain[:, None],
            jnp.repeat(skip_gain, HD, axis=1)[:, None], extra[:, None],
        ],
        axis=1,
    )
    pack = lax.all_gather(pack, "tensor", axis=0)
    extra = pack[:, :, 7]
    heads_in = jnp.stack(
        [
            jnp.swapaxes(extra[:, :, :few], 0, 1).reshape(LAYERS, heads),
            jnp.exp(jnp.swapaxes(extra[:, :, few : 2 * few], 0, 1).reshape(LAYERS, heads)),
        ],
        axis=1,
    )
    heads_in = jnp.pad(heads_in, ((0, 0), (0, 6), (0, LANES - heads)))
    gp = pack.reshape(pieces, LAYERS, 8, own // GC, GC).transpose(1, 0, 3, 2, 4).reshape(LAYERS, groups, 8, GC)
    csw = jnp.pad(jnp.concatenate([conv_shared_w, conv_shared_b[:, None]], axis=1), ((0, 0), (0, 3), (0, 0)))

    params = []
    for layer in range(LAYERS):
        pair = jnp.swapaxes(gate_value_weight[layer], 0, 1)
        pair = lax.all_gather(pair, both, axis=0).reshape((dp, pieces) + pair.shape)
        out = lax.all_gather(w_out[layer], both, axis=0).reshape((dp, pieces) + w_out.shape[1:])
        wbc = lax.all_gather(w_bc[layer], "dp", axis=0, tiled=True)
        wdt = lax.all_gather(w_dt[layer], both, axis=0).reshape((dp, pieces) + w_dt.shape[1:])
        wdt = jnp.pad(wdt.transpose(0, 2, 1, 3).reshape(depth, heads), ((0, 0), (0, LANES - heads)))
        params.append((pair, out, wbc, wdt, gp[layer], csw[layer], heads_in[layer]))

    x = tokens.astype(F32)
    line = [x]
    saved = []
    for layer in range(LAYERS):
        x, *kept = layer_forward(dims, x, norm_gain[layer][None], *params[layer], masks)
        line.append(x)
        saved.append(kept)
    grad = cotangent.astype(F32)
    big, small = [None] * LAYERS, [None] * LAYERS
    for layer in reversed(range(LAYERS)):
        grad, gw, gwo, gbc, gdt, ggp, ggate, gcs, gheads, ggain = layer_backward(
            dims, grad, line[layer], line[layer + 1], norm_gain[layer][None], saved[layer], *params[layer], masks
        )
        gdt = gdt[:, :heads].reshape(dp, depth // dp, pieces, few).transpose(0, 2, 1, 3)

        def scatter(v):
            v = lax.psum_scatter(v, "dp", scatter_dimension=0, tiled=True)
            return lax.psum_scatter(v, "tensor", scatter_dimension=1, tiled=True)[0, 0].astype(F32)

        gbc = lax.psum(lax.psum_scatter(gbc, "dp", scatter_dimension=0, tiled=True), "tensor").astype(F32)
        big[layer] = (jnp.swapaxes(scatter(gw), 0, 1), gbc, scatter(gdt), scatter(gwo))
        rows = jnp.concatenate([ggp[:, :5], ggate[:, :2]], axis=1)
        rows = rows.reshape(pieces, own // GC, 7, GC).transpose(0, 2, 1, 3).reshape(pieces, 7, own)
        small[layer] = (rows, gcs[:5], gheads[:2, :heads], ggain[0])
    small = lax.psum(small, both)

    def stacked(group, member):
        return jnp.stack([group[layer][member] for layer in range(LAYERS)], axis=0)

    rows = lax.dynamic_index_in_dim(stacked(small, 0), z, axis=1, keepdims=False)
    gcs = stacked(small, 1)
    gheads = lax.dynamic_slice_in_dim(stacked(small, 2), z * few, few, axis=2)
    return (
        x.astype(BF), grad, stacked(big, 0), stacked(big, 1), stacked(big, 2), stacked(big, 3), stacked(small, 3),
        rows[:, :4], rows[:, 4], gcs[:, :4], gcs[:, 4], gheads[:, 0], gheads[:, 1],
        jnp.sum(rows[:, 6].reshape(LAYERS, few, HD), axis=2), rows[:, 5],
    )


def solution(mesh):
    in_specs = (
        P(("dp", "tensor"), None),
        P(None, "dp", None, "tensor"),
        P(None, "dp", None),
        P(None, "dp", "tensor"),
        P(None, "dp", "tensor"),
        P(),
        P(None, None, "tensor"),
        P(None, "tensor"),
        P(),
        P(),
        P(None, "tensor"),
        P(None, "tensor"),
        P(None, "tensor"),
        P(None, "tensor"),
        P("dp", None),
        P(("dp", "tensor"), None),
    )
    out_specs = (
        P(("dp", "tensor"), None),
        P(("dp", "tensor"), None),
        P(None, "dp", None, "tensor"),
        P(None, "dp", None),
        P(None, "dp", "tensor"),
        P(None, "dp", "tensor"),
        P(),
        P(None, None, "tensor"),
        P(None, "tensor"),
        P(),
        P(),
        P(None, "tensor"),
        P(None, "tensor"),
        P(None, "tensor"),
        P(None, "tensor"),
    )
    return jax.shard_map(local, mesh=mesh, in_specs=in_specs, out_specs=out_specs, check_vma=False)
```

```python
from functools import partial

import jax
import jax.numpy as jnp
from jax import lax
from jax.experimental import pallas as pl
from jax.experimental.pallas import tpu as pltpu
from jax.sharding import PartitionSpec as P

LAYERS = 2
EPS = 1e-05
HALO = 16
CH = 128
GC = 256
HD = 64
HG = GC // HD
LANES = 128
STATE = 128
NEG = -1e30
SLOTS = 2
VMEM_LIMIT = 58 * 1024 * 1024
VMEM_LIMIT_FORWARD = 62 * 1024 * 1024
STEP_US = 3.2
TICK = 1.3
MESH = pl.DeviceIdType.MESH
HI = lax.Precision.HIGHEST
F32 = jnp.float32
BF = jnp.bfloat16


def dot_nn(a, b, precision=None):
    return lax.dot_general(a, b, (((1,), (0,)), ((), ())), precision=precision, preferred_element_type=F32)


def dot_nt(a, b):
    return lax.dot_general(a, b, (((1,), (1,)), ((), ())), preferred_element_type=F32)


def dot_tn(a, b):
    return lax.dot_general(a, b, (((0,), (0,)), ((), ())), preferred_element_type=F32)


def sigmoid(v):
    return 0.5 * jnp.tanh(0.5 * v) + 0.5


def twice(v):
    return jnp.concatenate([v, v], axis=1)


def split2(v):
    high = v.astype(BF)
    return jnp.concatenate([high, (v - high.astype(F32)).astype(BF)], axis=1)


def iota2(shape, dim):
    return lax.broadcasted_iota(jnp.int32, shape, dim)


def spread(group):
    row = iota2((2 * LANES, GC), 0) % LANES
    head = iota2((2 * LANES, GC), 1) // HD + group * HG
    return (row == head).astype(F32).astype(BF)


def collect(group):
    head = (iota2((2 * GC, LANES), 0) % GC) // HD + group * HG
    return (head == iota2((2 * GC, LANES), 1)).astype(F32).astype(BF)


def conv(load, keep_ref, weights, tokens):
    total = weights[4:5] + weights[0:1] * load(0)
    for k in range(1, 4):
        total = total + weights[k : k + 1] * (load(k) * twice(keep_ref[k - 1]))
    return total


def conv_back(grad, load, keep_ref, weights, tokens):
    rows = []
    total = None
    for k in range(4):
        part = grad if k == 0 else grad * twice(keep_ref[k - 1])
        rows.append(jnp.sum(part * load(k), axis=0, keepdims=True))
        wide = jnp.concatenate([jnp.zeros((HALO, grad.shape[1]), F32), weights[k : k + 1] * part], axis=0)
        if k:
            wide = pltpu.roll(wide, tokens + HALO - k, 0)
        total = wide if total is None else total + wide
    rows.append(jnp.sum(grad, axis=0, keepdims=True))
    return total, rows


def step_terms(step_in, heads_ref, carried_ref, tail_ref, kept_ref, tokens):
    chunks = tokens // CH
    raw = step_in + heads_ref[0:1]
    steps = jnp.maximum(raw, 0.0) + jnp.log1p(jnp.exp(-jnp.abs(raw)))
    rates = -steps * heads_ref[1:2]
    lower = (iota2((CH, CH), 0) >= iota2((CH, CH), 1)).astype(F32)
    sums, toward, kept = [], [], []
    for c in range(chunks):
        summed = dot_nn(lower, rates[c * CH : (c + 1) * CH], HI)
        last = summed[CH - 1 : CH]
        sums.append(summed)
        toward.append(jnp.exp(last - summed))
        kept.append(jnp.exp(last) * kept_ref[c : c + 1])
    kept.append(jnp.zeros((8 - chunks, LANES), F32))
    summed = jnp.concatenate(sums, axis=0)
    toward = jnp.concatenate(toward, axis=0) * tail_ref[...]
    reach = jnp.exp(summed) * carried_ref[...]
    return raw, steps, rates, summed, toward, reach, jnp.concatenate(kept, axis=0)


def put_sums(summed, col_ref, row_ref, groups, tokens):
    for c in range(tokens // CH):
        turned = summed[c * CH : (c + 1) * CH].T
        for group in range(groups):
            row_ref[group, 0:HG, c * CH : (c + 1) * CH] = turned[group * HG : (group + 1) * HG]
    col_ref[0] = summed


def turn_sums(col_ref, group):
    col_ref[1] = pltpu.roll(col_ref[0], lax.rem(LANES - group * HG, LANES), 1)


def put_heads(rows_ref, heads_ref):
    total = rows_ref[0, 0, 7:8, :]
    for k in range(1, rows_ref.shape[0]):
        total = total + rows_ref[k, 0, 7:8, :]
    heads_ref[...] = jnp.concatenate(
        [total[:, :LANES], jnp.exp(total[:, LANES:]), jnp.zeros((6, LANES), F32)], axis=0
    )


def shared_taps(csw_ref, csb_ref, layer):
    return jnp.concatenate([csw_ref[layer], csb_ref[layer : layer + 1]], axis=0)


def halves(v):
    first = iota2(v.shape, 1) < HD
    return jnp.concatenate([jnp.where(first, v, 0.0), jnp.where(first, 0.0, v)], axis=0).astype(BF)


def forward_kernel(
    dims,
    x_ref, gain_ref, wa, wb, oa, ob, few_ref, pa, pb, qa, qb, rows_ref, csw_ref, csb_ref,
    keep_ref, bias_ref, carried_ref, tail_ref, kept_ref, *rest,
):
    pieces, groups, tokens, skew, bits, layer, gathers = dims
    if gathers:
        few_mine, mine_ref, *rest = rest
    next_ref, nxt_ref, nht_ref, gate_ref, val_ref, y_ref, state_ref, shared_ref, step_ref, r_ref, *rest = rest
    if gathers:
        few_out, wall_ref, *rest = rest
    nx, inb, inbt, outb, cross, col, row, terms, ke, intra, xs, gs, fresh, fold, *rest = rest
    incoming, outgoing, branch, squares, heads_ref, halo_send, halo_recv, send, recv, *rest = rest
    if gathers:
        few_z, few_all, *rest = rest
    place = Place(bits)
    chunks = tokens // CH
    i = pl.program_id(0)
    z = lax.axis_index("tensor")
    right, left = jnp.minimum(z + 1, pieces - 1), jnp.maximum(z - 1, 0)

    def halo_copy():
        return pltpu.make_async_remote_copy(
            src_ref=nx.at[pl.ds(tokens, HALO)], dst_ref=nx.at[pl.ds(0, HALO)],
            send_sem=halo_send, recv_sem=halo_recv, device_id={"tensor": right}, device_id_type=MESH,
        )

    def state_copy(group):
        return pltpu.make_async_remote_copy(
            src_ref=outgoing.at[group], dst_ref=incoming.at[group],
            send_sem=send.at[group], recv_sem=recv.at[group], device_id={"tensor": right}, device_id_type=MESH,
        )

    gather = Gather(place, z, pieces, mine_ref, wall_ref, few_mine, few_z, few_all, *rest) if gathers else None
    steps_all = groups + skew
    plan = [[] for _ in range(steps_all)]
    if gathers:
        for when, act in gather.events():
            plan[min(int((when * TICK + 3.0) / STEP_US), steps_all - 1)].append(act)

    @pl.when(i == 0)
    def _():
        greet(place, z, pieces)
        x = x_ref[...]
        scale = lax.rsqrt(jnp.mean(x * x, axis=1, keepdims=True) + EPS)
        nx[pl.ds(HALO, tokens), :] = (x * scale * gain_ref[layer : layer + 1]).astype(BF)
        put_heads(rows_ref, heads_ref)

        @pl.when(z < pieces - 1)
        def _():
            halo_copy().start()

        if gathers:
            gather.start()

        @pl.when(z == 0)
        def _():
            nx[pl.ds(0, HALO), :] = jnp.zeros((HALO, nx.shape[1]), BF)
            incoming[...] = jnp.zeros(incoming.shape, BF)

        depth = nx.shape[1]
        step_in = dot_nn(nx[pl.ds(HALO, tokens), :], few_ref[:, :, 2 * STATE :].reshape(depth, LANES))
        step_ref[...] = step_in
        _, steps, _, summed, toward, reach, kept = step_terms(
            step_in, heads_ref, carried_ref, tail_ref, kept_ref, tokens
        )
        put_sums(summed, col, row, groups, tokens)
        terms[0] = split2(steps)
        terms[1] = split2(toward)
        terms[2] = split2(reach)
        kept2 = split2(kept)
        for group in range(groups):
            ke[group] = dot_nn(kept2, spread(group))

        @pl.when(z > 0)
        def _():
            halo_copy().wait_recv()

        shared_ref[...] = dot_nn(nx[...], few_ref[:, :, : 2 * STATE].reshape(depth, 2 * STATE))
        taps = shared_taps(csw_ref, csb_ref, layer)
        mixed = conv(lambda k: shared_ref[pl.ds(HALO - k, tokens), :], keep_ref, taps, tokens)
        maps = mixed * sigmoid(mixed)
        for c in range(chunks):
            part = maps[c * CH : (c + 1) * CH]
            into, out = part[:, :STATE], part[:, STATE:].astype(BF)
            inb[c], outb[c], inbt[c] = into.astype(BF), out, into.T.astype(BF)
            cross[c] = dot_nt(out, into.astype(BF))
        branch[...] = jnp.zeros(branch.shape, F32)
        squares[...] = jnp.zeros(squares.shape, F32)

    @pl.when(i < groups)
    def _():
        depth = nx.shape[1]
        group = i
        slot = lax.rem(group, skew + 1)
        gate_ref[0] = dot_nn(nx[pl.ds(HALO, tokens), :], side((wa, wb), 0))
        val_ref[0] = dot_nn(nx[...], side((wa, wb), 1))
        mixed = conv(lambda k: val_ref[0, pl.ds(HALO - k, tokens), :], keep_ref, side_params((pa, pb)), tokens)
        xs[slot] = mixed * sigmoid(mixed)
        gate = gate_ref[0]
        gs[slot] = gate * sigmoid(gate)
        turn_sums(col, group)
        spreader = spread(group)
        state = jnp.zeros((STATE, GC), F32)
        for c in range(chunks):
            rows = pl.ds(c * CH, CH)
            sized = xs[slot, rows, :] * dot_nn(terms[0, rows, :], spreader)
            weighted = (sized * dot_nn(terms[1, rows, :], spreader)).astype(BF)
            new = dot_nn(inbt[c], weighted)
            fresh[slot, c] = new
            state = ke[group, c : c + 1] * state + new
            for pair in range(HG // 2):
                lanes = pl.ds(pair * LANES, LANES)
                decayed = []
                for j in (2 * pair, 2 * pair + 1):
                    across = col[1, rows, j : j + 1] - row[group, j : j + 1, rows]
                    decayed.append((cross[c] * jnp.exp(jnp.minimum(across, bias_ref[c]))).astype(BF))
                blocks = halves(sized[:, pair * LANES : (pair + 1) * LANES])
                intra[slot, rows, lanes] = dot_nn(jnp.concatenate(decayed, axis=1), blocks)
        fold[slot] = state

    j = i - z

    @pl.when(jnp.logical_and(j >= 0, j < groups))
    def _():
        @pl.when(z > 0)
        def _():
            state_copy(j).wait_recv()

        @pl.when(z < pieces - 1)
        def _():
            total = ke[j, 0:1]
            for c in range(1, chunks):
                total = total * ke[j, c : c + 1]
            outgoing[j] = (total * incoming[j].astype(F32) + fold[lax.rem(j, skew + 1)]).astype(BF)
            state_copy(j).start()

    @pl.when(i >= skew)
    def _():
        group = i - skew
        slot = lax.rem(group, skew + 1)
        depth = nx.shape[1]
        spreader = spread(group)
        gp = side_params((qa, qb))
        state = incoming[group].astype(F32)
        for c in range(chunks):
            rows = pl.ds(c * CH, CH)
            low = state.astype(BF)
            state_ref[0, c] = low
            y = intra[slot, rows, :] + dot_nn(outb[c], low) * dot_nn(terms[2, rows, :], spreader)
            y_ref[0, rows, :] = y
            gated = (y + gp[6:7] * xs[slot, rows, :]) * gs[slot, rows, :]
            squares[rows, :] += jnp.sum(gated * gated, axis=1, keepdims=True)
            intra[slot, rows, :] = gated * gp[5:6]
            if c < chunks - 1:
                state = ke[group, c : c + 1] * state + fresh[slot, c]
        branch[...] += dot_nt(intra[slot].astype(BF), side((oa, ob), 0))

    for step, acts in enumerate(plan):
        if acts:

            @pl.when(i == step)
            def _(acts=acts):
                for act in acts:
                    act()

    @pl.when(i == groups + skew - 1)
    def _():
        inner = groups * GC
        factor = lax.rsqrt(squares[...] * (1.0 / inner) + EPS)
        r_ref[...] = factor
        next_ref[...] = x_ref[...] + branch[...] * factor[:, 0:1]
        nxt_ref[...] = nx[pl.ds(HALO, tokens), :].T
        nht_ref[...] = nx[pl.ds(0, HALO), :].T
        if gathers:
            gather.finish()
            few_out[...] = few_all[...]

        @pl.when(z < pieces - 1)
        def _():
            halo_copy().wait_send()
            for group in range(groups):
                state_copy(group).wait_send()


class Place:
    def __init__(self, bits):
        self.bits = bits
        self.index = lax.axis_index("dp")
        self.bit = [lax.rem(self.index // (1 << b), 2) for b in range(bits)]
        self.dims = (2,) * bits
        self.all = (slice(None),) * bits

    def flip(self, b):
        return self.index + (1 << b) * (1 - 2 * self.bit[b])

    def along(self, done):
        return tuple(slice(None) if b in done else self.bit[b] for b in reversed(range(self.bits)))

    def order(self, odd):
        rest = list(range(1, self.bits))
        return [0] + (rest[::-1] if odd else rest)

    def partner(self, odd, step):
        return self.flip(self.order(odd)[step])

    def region(self, odd, step, keep):
        order = self.order(odd)
        at = []
        for b in reversed(range(self.bits)):
            if b in order[:step]:
                at.append(self.bit[b])
            elif b == order[step]:
                at.append(self.bit[b] if keep else 1 - self.bit[b])
            else:
                at.append(slice(None))
        return tuple(at)

    def mine(self):
        return tuple(self.bit[b] for b in reversed(range(self.bits)))


def backward_kernel(
    dims,
    g_ref, x_ref, next_ref, gain_ref, nxt, nht, r_ref, wa, wb, oa, ob, few_ref, pa, pb, qa, qb, rows_ref,
    csw_ref, csb_ref, keep_ref, biast_ref, carried_ref, tail_ref, kept_ref,
    gate_ref, val_ref, y_ref, valb_ref, yb_ref, state_ref, shared_ref, step_ref,
    gx_ref, gw_ref, gm_ref, small_ref,
    gb, gbt, r2, inb, outb, outbt, crosst, col, row, terms, ke,
    dys, xs, fs, dgs, fold, incoming, outgoing, gnorm, dct, dbt, dgt, sd, sp, sq, se, dxd, hrecv,
    own, own_m, got_z, got_m, halo_send, halo_recv, send, recv, sum_send, sum_recv, z_send, z_recv,
    msum_send, msum_recv, mz_send, mz_recv, next_sem, load_sem, heads_ref,
    few_total, few_got, few_z, few_send, few_recv, fz_send, fz_recv, *got,
):
    pieces, groups, tokens, skew, bits, layer = dims
    chunks = tokens // CH
    i = pl.program_id(0)
    z = lax.axis_index("tensor")
    right, left = jnp.minimum(z + 1, pieces - 1), jnp.maximum(z - 1, 0)
    back = pieces - 1 - z
    depth = gb.shape[1]
    inner = groups * GC

    def halo_copy():
        return pltpu.make_async_remote_copy(
            src_ref=gnorm, dst_ref=hrecv,
            send_sem=halo_send, recv_sem=halo_recv, device_id={"tensor": left}, device_id_type=MESH,
        )

    def state_copy(group):
        return pltpu.make_async_remote_copy(
            src_ref=outgoing.at[group], dst_ref=incoming.at[group],
            send_sem=send.at[group], recv_sem=recv.at[group], device_id={"tensor": left}, device_id_type=MESH,
        )

    place = Place(bits)
    parts, parts_m = got[:bits], got[bits:]

    def part(step, group, half):
        left = (slice(None),) * (bits - 1 - step + 2)
        return (lax.rem(group, SLOTS),) + left + (pl.ds(half * LANES, LANES),)

    def held(step, group, half, keep):
        return (group,) + place.region(half, step, keep) + (slice(None), slice(None), pl.ds(half * LANES, LANES))

    def sum_copy(group, step, half):
        return pltpu.make_async_remote_copy(
            src_ref=own.at[held(step, group, half, False)], dst_ref=parts[step].at[part(step, group, half)],
            send_sem=sum_send.at[group, step, half], recv_sem=sum_recv.at[group, step, half],
            device_id={"dp": place.partner(half, step)}, device_id_type=MESH,
        )

    def z_copy(group, half):
        column = group // (pieces // 2)
        return pltpu.make_async_remote_copy(
            src_ref=own.at[(group,) + place.mine() + (slice(None), slice(None), pl.ds(half * LANES, LANES))],
            dst_ref=got_z.at[z, column], send_sem=z_send.at[group, half], recv_sem=z_recv.at[z, column],
            device_id={"tensor": quarter(group, half, pieces)}, device_id_type=MESH,
        )

    def advance(group, step):
        @pl.when(jnp.logical_and(group >= 0, group < groups))
        def _():
            for half in range(2):
                if step:
                    sum_copy(group, step - 1, half).wait_recv()
                    at = held(step - 1, group, half, True)
                    own[at] = own[at] + parts[step - 1][part(step - 1, group, half)]
                if step < bits:
                    sum_copy(group, step, half).start()
                if step == bits:

                    @pl.when(quarter(group, half, pieces) != z)
                    def _(half=half):
                        z_copy(group, half).start()

    def misc_copy(step):
        return pltpu.make_async_remote_copy(
            src_ref=own_m.at[place.region(False, step, False)], dst_ref=parts_m[step],
            send_sem=msum_send.at[step], recv_sem=msum_recv.at[step],
            device_id={"dp": place.partner(False, step)}, device_id_type=MESH,
        )

    def misc_z(k):
        return pltpu.make_async_remote_copy(
            src_ref=own_m.at[place.mine()], dst_ref=got_m.at[z], send_sem=mz_send.at[k], recv_sem=mz_recv.at[z],
            device_id={"tensor": lax.rem(z + k, pieces)}, device_id_type=MESH,
        )

    def misc_advance(step):
        if step:
            misc_copy(step - 1).wait_recv()
            at = place.region(False, step - 1, True)
            own_m[at] = own_m[at] + parts_m[step - 1][...]
        if step < bits:
            misc_copy(step).start()
        else:
            for k in range(1, pieces):
                misc_z(k).start()
            got_m[z] = own_m[place.mine()]

    def drain(late):
        for step in reversed(range(1, bits + 1)):
            if late <= step:
                advance(groups - 1 + late - step, step)

    def few_copy(step):
        return pltpu.make_async_remote_copy(
            src_ref=few_total.at[step], dst_ref=few_got.at[step], send_sem=few_send.at[step],
            recv_sem=few_recv.at[step], device_id={"dp": place.partner(False, step)}, device_id_type=MESH,
        )

    def few_line(k, source):
        return pltpu.make_async_remote_copy(
            src_ref=few_total.at[bits], dst_ref=few_z.at[source], send_sem=fz_send.at[k], recv_sem=fz_recv.at[source],
            device_id={"tensor": lax.rem(z + k, pieces)}, device_id_type=MESH,
        )

    def few_advance(step):
        if step:
            few_copy(step - 1).wait_recv()
            few_total[step] = few_total[step - 1] + few_got[step - 1]
        if step < bits:
            few_copy(step).start()
        else:
            for k in range(1, pieces):
                few_line(k, z).start()
            few_z[z] = few_total[bits]

    def load_blocks():
        found = []
        for k in range(depth // GC):
            cols = pl.ds(k * GC, GC)
            found.append(pltpu.make_async_copy(x_ref.at[:, cols], xs.at[k], load_sem.at[0, k]))
            found.append(pltpu.make_async_copy(g_ref.at[:, cols], fs.at[k], load_sem.at[1, k]))
        return found

    def taps():
        return shared_taps(csw_ref, csb_ref, layer)

    def shared_conv():
        return conv(lambda k: shared_ref[pl.ds(HALO - k, tokens), :], keep_ref, taps(), tokens)

    @pl.when(i == 0)
    def _():
        greet(place, z, pieces)
        put_heads(rows_ref, heads_ref)

        @pl.when(z == pieces - 1)
        def _():
            incoming[...] = jnp.zeros(incoming.shape, BF)

        copies = [pltpu.make_async_copy(next_ref, gx_ref, next_sem)] + load_blocks()
        for copy in copies:
            copy.start()
        for copy in copies:
            copy.wait()
        dots = jnp.zeros((tokens, 1), F32)
        for k in range(depth // GC):
            cols = slice(k * GC, (k + 1) * GC)
            low = fs[k].astype(BF)
            gb[:, cols] = low
            gbt[cols, :] = low.T
            dots = dots + jnp.sum(low.astype(F32) * (gx_ref[:, cols] - xs[k]), axis=1, keepdims=True)
        r = r_ref[...]
        r2[...] = r * r * dots * (1.0 / inner)
        _, steps, _, summed, toward, reach, kept = step_terms(
            step_ref[...], heads_ref, carried_ref, tail_ref, kept_ref, tokens
        )
        put_sums(summed, col, row, groups, tokens)
        terms[0] = split2(steps)
        terms[1] = split2(toward)
        terms[2] = split2(reach)
        kept2 = split2(kept)
        for group in range(groups):
            ke[group] = dot_nn(kept2, spread(group))
        mixed = shared_conv()
        maps = mixed * sigmoid(mixed)
        for c in range(chunks):
            part = maps[c * CH : (c + 1) * CH]
            into, out = part[:, :STATE].astype(BF), part[:, STATE:]
            inb[c], outb[c], outbt[c] = into, out.astype(BF), out.T.astype(BF)
            crosst[c] = dot_nt(into, out.astype(BF))
        for ref in (gx_ref, gnorm, dct, dbt, dgt, sd, sp, sq, se):
            ref[...] = jnp.zeros(ref.shape, F32)

    @pl.when(i < groups)
    def _():
        group = i
        slot = lax.rem(group, skew + 1)
        gp = side_params((pa, pb))
        mixed = conv(lambda k: val_ref[0, pl.ds(HALO - k, tokens), :], keep_ref, gp, tokens)
        part = sigmoid(mixed)
        x = mixed * part
        xs[slot] = x
        fs[slot] = part + x * (1.0 - part)
        r = twice(r_ref[...])
        gm = dot_nn(gb[...], side((oa, ob), 0))
        scan = y_ref[0] + gp[6:7] * x
        gate = gate_ref[0]
        part = sigmoid(gate)
        silu = gate * part
        gated = scan * silu
        normal = gated * r
        own[(group,) + place.all + (2,)] = (
            dot_nn(gbt[...], (normal * gp[5:6]).astype(BF)).astype(BF).reshape(place.dims + (-1, GC))
        )
        ggated = r * gp[5:6] * gm - gated * twice(r2[...])
        dy = ggated * silu
        dys[slot] = dy.astype(BF)
        dgs[slot] = (ggated * scan * (part + silu * (1.0 - part))).astype(BF)
        small_ref[pl.ds(group * 8, 8), :] = jnp.concatenate(
            [
                jnp.zeros((5, GC), F32),
                jnp.sum(gm * normal, axis=0, keepdims=True),
                jnp.sum(dy * x, axis=0, keepdims=True),
                jnp.zeros((1, GC), F32),
            ],
            axis=0,
        )
        spreader = spread(group)
        state = jnp.zeros((STATE, GC), F32)
        for c in reversed(range(chunks)):
            rows = pl.ds(c * CH, CH)
            reached = (dys[slot, rows, :].astype(F32) * dot_nn(terms[2, rows, :], spreader)).astype(BF)
            new = dot_nn(outbt[c], reached)
            state = ke[group, c : c + 1] * state + new
        fold[slot] = state

    j = i - back

    @pl.when(jnp.logical_and(j >= 0, j < groups))
    def _():
        @pl.when(z < pieces - 1)
        def _():
            state_copy(j).wait_recv()

        @pl.when(z > 0)
        def _():
            total = ke[j, 0:1]
            for c in range(1, chunks):
                total = total * ke[j, c : c + 1]
            outgoing[j] = (total * incoming[j].astype(F32) + fold[lax.rem(j, skew + 1)]).astype(BF)
            state_copy(j).start()

    @pl.when(i >= skew)
    def _():
        group = i - skew
        slot = lax.rem(group, skew + 1)
        gp = side_params((qa, qb))
        spreader, collector = spread(group), collect(group)
        turn_sums(col, group)
        grad = incoming[group].astype(F32)
        ends = [None] * chunks
        for c in reversed(range(chunks)):
            rows = pl.ds(c * CH, CH)
            low = grad.astype(BF)
            state = state_ref[0, c]
            ends[c] = jnp.sum(low.astype(F32) * state.astype(F32), axis=0, keepdims=True) * ke[group, c : c + 1]
            x = xs[slot, rows, :]
            dy = dys[slot, rows, :].astype(F32)
            steps = dot_nn(terms[0, rows, :], spreader)
            toward = dot_nn(terms[1, rows, :], spreader)
            reached = (dy * dot_nn(terms[2, rows, :], spreader)).astype(BF)
            grad = ke[group, c : c + 1] * grad + dot_nn(outbt[c], reached)
            sized = x * steps
            weighted = (sized * toward).astype(BF)
            later = dot_nn(inb[c], low) * toward
            dbt[c] += dot_nt(weighted, low)
            dct[c] += dot_nt(reached, state)
            parts = []
            cross = crosst[c]
            pairs_total = jnp.zeros((CH, CH), F32)
            for pair in range(HG // 2):
                at = slice(pair * LANES, (pair + 1) * LANES)
                dyp = dy[:, at]
                products = dot_nt(halves(sized[:, at]), dyp.astype(BF))
                decayed = []
                for n in range(2):
                    h = 2 * pair + n
                    across = row[group, h : h + 1, rows] - col[1, rows, h : h + 1]
                    decay = jnp.exp(jnp.minimum(across, biast_ref[c]))
                    decayed.append((cross * decay).astype(BF))
                    pairs_total = pairs_total + products[n * CH : (n + 1) * CH] * decay
                parts.append(dot_nn(jnp.concatenate(decayed, axis=1), halves(dyp)))
            dgt[c] += pairs_total
            within = jnp.concatenate(parts, axis=1)
            whole = within + later
            lowered = dy * yb_ref[0, rows, :] - sized.astype(BF).astype(F32) * within
            sd[rows, :] += dot_nn(split2(whole * x), collector)
            sp[rows, :] += dot_nn(split2(lowered), collector)
            sq[rows, :] += dot_nn(split2(sized * later), collector)
            dxd[rows, :] = (whole * steps + gp[6:7] * dy) * fs[slot, rows, :]
        for step in reversed(range(1, bits + 1)):
            advance(group - step, step)
        ends.append(jnp.zeros((8 - chunks, GC), F32))
        se[...] += dot_nn(split2(jnp.concatenate(ends, axis=0)), collector)
        wide, sums = conv_back(
            dxd[...], lambda k: valb_ref[0, pl.ds(HALO - k, tokens), :], keep_ref, gp, tokens
        )
        small_ref[pl.ds(group * 8, 8), :] += jnp.concatenate(sums + [jnp.zeros((3, GC), F32)], axis=0)
        wide = wide.astype(BF)
        dgate = dgs[slot]
        shape = place.dims + (-1, GC)
        own[(group,) + place.all + (0,)] = dot_nn(nxt[...], dgate).astype(BF).reshape(shape)
        own[(group,) + place.all + (1,)] = (
            (dot_nn(nxt[...], wide[HALO:]) + dot_nn(nht[...], wide[:HALO])).astype(BF).reshape(shape)
        )
        advance(group, 0)
        back_wide = dot_nt(wide, side((wa, wb), 1))
        gnorm[...] += back_wide[:HALO]
        gx_ref[...] += back_wide[HALO:] + dot_nt(dgate, side((wa, wb), 0))

    @pl.when(i == groups + skew - 1)
    def _():
        for copy in load_blocks():
            copy.start()
        upper = (iota2((CH, CH), 0) <= iota2((CH, CH), 1)).astype(F32)
        before = (iota2((CH, CH), 0) > iota2((CH, CH), 1)).astype(F32)
        raw, steps, rates, _, _, _, _ = step_terms(step_ref[...], heads_ref, carried_ref, tail_ref, kept_ref, tokens)
        drates, dmaps = [], []
        for c in range(chunks):
            rows = slice(c * CH, (c + 1) * CH)
            drates.append(dot_nn(upper, sp[rows, :], HI) + dot_nn(before, sq[rows, :], HI) + se[c : c + 1])
            low = dgt[c].astype(BF)
            into = dbt[c] + dot_nn(low, outb[c])
            out = dct[c] + dot_tn(low, inb[c])
            dmaps.append(jnp.concatenate([into, out], axis=1))
        drate = jnp.concatenate(drates, axis=0)
        dstep = (sd[...] - drate * heads_ref[1:2]) * sigmoid(raw)
        head_sums = jnp.concatenate(
            [jnp.sum(dstep, axis=0, keepdims=True), jnp.sum(drate * rates, axis=0, keepdims=True)], axis=1
        )
        mixed = shared_conv()
        part = sigmoid(mixed)
        dmixed = jnp.concatenate(dmaps, axis=0) * (part + mixed * part * (1.0 - part))
        wide, sums = conv_back(dmixed, lambda k: shared_ref[pl.ds(HALO - k, tokens), :], keep_ref, taps(), tokens)
        small_ref[pl.ds(groups * 8, 8), :] = jnp.concatenate(sums + [jnp.zeros((3, 2 * STATE), F32)], axis=0)
        wide = wide.astype(BF)
        dstep = dstep.astype(BF)
        back_wide = dot_nt(wide, few_ref[:, :, : 2 * STATE].reshape(depth, 2 * STATE))
        gnorm[...] += back_wide[:HALO]

        @pl.when(z > 0)
        def _():
            halo_copy().start()

        gx_ref[...] += back_wide[HALO:] + dot_nt(dstep, few_ref[:, :, 2 * STATE :].reshape(depth, LANES))
        drain(1)
        misc = jnp.concatenate(
            [dot_nn(nxt[...], wide[HALO:]) + dot_nn(nht[...], wide[:HALO]), dot_nn(nxt[...], dstep)], axis=1
        )
        own_m[...] = misc.astype(BF).reshape(own_m.shape)
        misc_advance(0)

        @pl.when(z < pieces - 1)
        def _():
            halo_copy().wait_recv()
            gx_ref[pl.ds(tokens - HALO, HALO), :] += hrecv[...]

        for copy in load_blocks():
            copy.wait()
        blocks = [(k, slice(k * GC, (k + 1) * GC)) for k in range(depth // GC)]
        power = inside = jnp.zeros((tokens, 1), F32)
        for k, cols in blocks:
            power = power + jnp.sum(xs[k] * xs[k], axis=1, keepdims=True)
            gained = gx_ref[:, cols] * gain_ref[layer : layer + 1, cols]
            inside = inside + jnp.sum(gained * xs[k], axis=1, keepdims=True)
        q = lax.rsqrt(power * (1.0 / depth) + EPS)
        inside = inside * (q * q * q) * (1.0 / depth)
        cuts = [jnp.sum(gx_ref[:, cols] * xs[k] * q, axis=0, keepdims=True) for k, cols in blocks]
        few_total[0, pl.ds(0, groups * 8 + 8), :] = small_ref[pl.ds(0, groups * 8 + 8), :]
        few_total[0, pl.ds(groups * 8 + 8, 8), :] = jnp.concatenate(
            cuts + [head_sums, jnp.zeros((7 - len(cuts), GC), F32)], axis=0
        )
        few_advance(0)
        misc_advance(1)
        for k, cols in blocks:
            gx_ref[:, cols] = fs[k] + q * (gx_ref[:, cols] * gain_ref[layer : layer + 1, cols]) - xs[k] * inside
        for step in range(2, bits + 1):
            drain(step)
            few_advance(step - 1)
            misc_advance(step)
        few_advance(bits)
        for k in range(1, pieces):
            few_line(k, lax.rem(z + k, pieces)).wait_recv()
        total = few_z[0]
        for source in range(1, pieces):
            total = total + few_z[source]
        small_ref[...] = total
        for k in range(1, pieces):
            source = lax.rem(z + k, pieces)
            pltpu.make_async_remote_copy(
                src_ref=own_m.at[place.mine()], dst_ref=got_m.at[source], send_sem=mz_send.at[k],
                recv_sem=mz_recv.at[source], device_id={"tensor": source}, device_id_type=MESH,
            ).wait_recv()
        total = got_m[0].astype(F32)
        for source in range(1, pieces):
            total = total + got_m[source].astype(F32)
        gm_ref[...] = total
        upper_half = z >= pieces // 2
        first = jnp.where(upper_half, pieces - 1 - z, z)
        for column in range(groups // (pieces // 2)):
            group = first + column * (pieces // 2)
            for k in range(1, pieces):
                source = lax.rem(z + k, pieces)
                pltpu.make_async_remote_copy(
                    src_ref=got_z.at[source, column], dst_ref=got_z.at[source, column],
                    send_sem=z_send.at[0, 0], recv_sem=z_recv.at[source, column],
                    device_id={"tensor": source}, device_id_type=MESH,
                ).wait_recv()
            for half in range(2):

                @pl.when(upper_half if half else jnp.logical_not(upper_half))
                def _(half=half, group=group, column=column):
                    total = own[(group,) + place.mine() + (slice(None), slice(None), pl.ds(half * LANES, LANES))]
                    total = total.astype(F32)
                    for k in range(1, pieces):
                        total = total + got_z[lax.rem(z + k, pieces), column].astype(F32)
                    gw_ref[:, :, column * LANES : (column + 1) * LANES] = total

        for group in range(groups):
            for step in range(bits):
                for half in range(2):
                    sum_copy(group, step, half).wait_send()

            for half in range(2):

                @pl.when(quarter(group, half, pieces) != z)
                def _(group=group, half=half):
                    z_copy(group, half).wait_send()

        for step in range(bits):
            misc_copy(step).wait_send()
            few_copy(step).wait_send()
        for k in range(1, pieces):
            misc_z(k).wait_send()
            few_line(k, z).wait_send()

        @pl.when(z > 0)
        def _():
            halo_copy().wait_send()
            for group in range(groups):
                state_copy(group).wait_send()


def whole(shape):
    return pl.BlockSpec(shape, lambda i: (0,) * len(shape), pipeline_mode=pl.Buffered(1))


def quarter(group, half, pieces):
    at = group % (pieces // 2)
    return pieces - 1 - at if half else at


def group_specs(dims, wall):
    pieces, groups, _, skew = dims
    dp, _, _, share, _ = wall
    last = groups - 1

    def early(i):
        return jnp.minimum(i, last)

    def late(i):
        return jnp.maximum(i - skew, 0)

    def block(rows, at):
        return pl.BlockSpec((1, rows, GC), lambda i: (at(i), 0, 0))

    def both(make):
        return [make(0), make(1)]

    def column(i, at):
        return at(i) // (pieces // 2)

    def pair(at):
        return both(
            lambda half: pl.BlockSpec(
                (dp, 1, 2, share, LANES), lambda i: (0, quarter(at(i), half, pieces), 0, 0, column(i, at))
            )
        )

    def single(at):
        return both(
            lambda half: pl.BlockSpec(
                (dp, 1, 1, share, LANES), lambda i: (0, quarter(at(i), half, pieces), 2, 0, column(i, at))
            )
        )

    def params(layer, at):
        return both(
            lambda half: pl.BlockSpec(
                (1, 1, 8, LANES), lambda i: (quarter(at(i), half, pieces), layer, 0, column(i, at))
            )
        )

    return early, late, block, pair, single, params


def side(refs, n):
    rows = refs[0].shape[0] * refs[0].shape[3]
    return jnp.concatenate([ref[:, 0, n].reshape(rows, LANES) for ref in refs], axis=1)


def side_params(refs):
    return jnp.concatenate([ref[0, 0] for ref in refs], axis=1)


def fixed(shape, place):
    return pl.BlockSpec(shape, lambda i: place, pipeline_mode=pl.Buffered(1))


def layer_forward(dims, bits, layer, x, gain, w, few, pack, csw, csb, masks, later):
    pieces, groups, tokens, skew = dims
    keep, bias, _, carried, tail, kept = masks
    chunks = tokens // CH
    depth = x.shape[1]
    ext = tokens + HALO
    slots = skew + 1
    early, late, block, pair, single, params = group_specs(dims, w.shape)
    anywhere = pl.BlockSpec(memory_space=pl.ANY)
    near = pl.BlockSpec(memory_space=pltpu.VMEM)
    gathers = later is not None
    cut = (2,) * bits
    buffers, sems = gather_scratch(pieces, bits, w.shape[3])
    if gathers:
        later_few, later = later
    return pl.pallas_call(
        partial(forward_kernel, dims + (bits, layer, gathers)),
        grid=(groups + skew,),
        in_specs=[
            whole((tokens, depth)), whole(gain.shape), *pair(early), *single(late),
            whole(few.shape), *params(layer, early), *params(layer, late), fixed((pieces, 1, 8, 2 * LANES), (0, layer, 0, 0)),
            whole(csw.shape), whole(csb.shape),
            whole(keep.shape), whole(bias.shape), whole(carried.shape), whole(tail.shape), whole(kept.shape),
        ] + [near, anywhere] * gathers,
        out_specs=[
            whole((tokens, depth)), whole((depth, tokens)), whole((depth, HALO)),
            block(tokens, early), block(ext, early), block(tokens, late),
            pl.BlockSpec((1, chunks, STATE, GC), lambda i: (late(i), 0, 0, 0)),
            whole((ext, 2 * STATE)), whole((tokens, LANES)), whole((tokens, LANES)),
        ] + [near, anywhere] * gathers,
        out_shape=[
            jax.ShapeDtypeStruct((tokens, depth), F32),
            jax.ShapeDtypeStruct((depth, tokens), BF),
            jax.ShapeDtypeStruct((depth, HALO), BF),
            jax.ShapeDtypeStruct((groups, tokens, GC), F32),
            jax.ShapeDtypeStruct((groups, ext, GC), F32),
            jax.ShapeDtypeStruct((groups, tokens, GC), F32),
            jax.ShapeDtypeStruct((groups, chunks, STATE, GC), BF),
            jax.ShapeDtypeStruct((ext, 2 * STATE), F32),
            jax.ShapeDtypeStruct((tokens, LANES), F32),
            jax.ShapeDtypeStruct((tokens, LANES), F32),
        ] + (
            [jax.ShapeDtypeStruct(cut + later_few.shape, BF), jax.ShapeDtypeStruct(cut + (pieces,) + later.shape, BF)]
            if gathers
            else []
        ),
        scratch_shapes=[
            pltpu.VMEM((ext, depth), BF),
            pltpu.VMEM((chunks, CH, STATE), BF),
            pltpu.VMEM((chunks, STATE, CH), BF),
            pltpu.VMEM((chunks, CH, STATE), BF),
            pltpu.VMEM((chunks, CH, CH), F32),
            pltpu.VMEM((2, tokens, LANES), F32),
            pltpu.VMEM((groups, 8, tokens), F32),
            pltpu.VMEM((3, tokens, 2 * LANES), BF),
            pltpu.VMEM((groups, 8, GC), F32),
            pltpu.VMEM((slots, tokens, GC), F32),
            pltpu.VMEM((slots, tokens, GC), F32),
            pltpu.VMEM((slots, tokens, GC), F32),
            pltpu.VMEM((slots, chunks, STATE, GC), F32),
            pltpu.VMEM((slots, STATE, GC), F32),
            pltpu.VMEM((groups, STATE, GC), BF),
            pltpu.VMEM((groups, STATE, GC), BF),
            pltpu.VMEM((tokens, depth), F32),
            pltpu.VMEM((tokens, LANES), F32),
            pltpu.VMEM((8, LANES), F32),
            pltpu.SemaphoreType.DMA,
            pltpu.SemaphoreType.DMA,
            pltpu.SemaphoreType.DMA((groups,)),
            pltpu.SemaphoreType.DMA((groups,)),
        ] + (buffers + sems if gathers else []),
        compiler_params=pltpu.CompilerParams(
            collective_id=layer, has_side_effects=True, vmem_limit_bytes=VMEM_LIMIT_FORWARD,
            dimension_semantics=("arbitrary",),
        ),
        name="layer_forward",
    )(
        x, gain, w, w, w, w, few, pack, pack, pack, pack, pack, csw, csb, keep, bias, carried, tail, kept,
        *([later_few, later] if gathers else []),
    )


def layer_backward(dims, bits, layer, g, x, after, gain, saved, w, few, pack, csw, csb, masks):
    pieces, groups, tokens, skew = dims
    keep, _, biast, carried, tail, kept = masks
    nxt, nht, gate, val, y, states, shared, step_in, r = saved
    anywhere = pl.BlockSpec(memory_space=pl.ANY)
    chunks = tokens // CH
    depth = x.shape[1]
    _, _, _, share, wide = w.shape
    ext = tokens + HALO
    slots = max(skew + 1, depth // GC)
    few_shape = (groups * 8 + 16, GC)
    halves_of = [(2,) * (bits - 1 - step) for step in range(bits)]
    early, late, block, pair, single, params = group_specs(dims, w.shape)
    return pl.pallas_call(
        partial(backward_kernel, dims + (bits, layer)),
        grid=(groups + skew,),
        in_specs=[
            anywhere, anywhere, anywhere, whole(gain.shape),
            whole(nxt.shape), whole(nht.shape), whole((tokens, LANES)), *pair(late), *single(early),
            whole(few.shape), *params(layer, early), *params(layer, late), fixed((pieces, 1, 8, 2 * LANES), (0, layer, 0, 0)),
            whole(csw.shape), whole(csb.shape),
            whole(keep.shape), whole(biast.shape), whole(carried.shape), whole(tail.shape), whole(kept.shape),
            block(tokens, early), block(ext, early), block(tokens, early), block(ext, late), block(tokens, late),
            pl.BlockSpec((1, chunks, STATE, GC), lambda i: (late(i), 0, 0, 0)),
            whole((ext, 2 * STATE)), whole((tokens, LANES)),
        ],
        out_specs=[
            whole((tokens, depth)), whole((3, share, wide)), whole((share, 2 * STATE + LANES)),
            whole((groups * 8 + 16, GC)),
        ],
        out_shape=[
            jax.ShapeDtypeStruct((tokens, depth), F32),
            jax.ShapeDtypeStruct((3, share, wide), F32),
            jax.ShapeDtypeStruct((share, 2 * STATE + LANES), F32),
            jax.ShapeDtypeStruct((groups * 8 + 16, GC), F32),
        ],
        scratch_shapes=[
            pltpu.VMEM((tokens, depth), BF),
            pltpu.VMEM((depth, tokens), BF),
            pltpu.VMEM((tokens, LANES), F32),
            pltpu.VMEM((chunks, CH, STATE), BF),
            pltpu.VMEM((chunks, CH, STATE), BF),
            pltpu.VMEM((chunks, STATE, CH), BF),
            pltpu.VMEM((chunks, CH, CH), F32),
            pltpu.VMEM((2, tokens, LANES), F32),
            pltpu.VMEM((groups, 8, tokens), F32),
            pltpu.VMEM((3, tokens, 2 * LANES), BF),
            pltpu.VMEM((groups, 8, GC), F32),
            pltpu.VMEM((slots, tokens, GC), BF),
            pltpu.VMEM((slots, tokens, GC), F32),
            pltpu.VMEM((slots, tokens, GC), F32),
            pltpu.VMEM((slots, tokens, GC), BF),
            pltpu.VMEM((slots, STATE, GC), F32),
            pltpu.VMEM((groups, STATE, GC), BF),
            pltpu.VMEM((groups, STATE, GC), BF),
            pltpu.VMEM((HALO, depth), F32),
            pltpu.VMEM((chunks, CH, STATE), F32),
            pltpu.VMEM((chunks, CH, STATE), F32),
            pltpu.VMEM((chunks, CH, CH), F32),
            pltpu.VMEM((tokens, LANES), F32),
            pltpu.VMEM((tokens, LANES), F32),
            pltpu.VMEM((tokens, LANES), F32),
            pltpu.VMEM((8, LANES), F32),
            pltpu.VMEM((tokens, GC), F32),
            pltpu.VMEM((HALO, depth), F32),
            pltpu.VMEM((groups,) + (2,) * bits + (3, share, GC), BF),
            pltpu.VMEM((2,) * bits + (share, 2 * STATE + LANES), BF),
            pltpu.VMEM((pieces, 2 * groups // pieces, 3, share, LANES), BF),
            pltpu.VMEM((pieces, share, 2 * STATE + LANES), BF),
            pltpu.SemaphoreType.DMA,
            pltpu.SemaphoreType.DMA,
            pltpu.SemaphoreType.DMA((groups,)),
            pltpu.SemaphoreType.DMA((groups,)),
            pltpu.SemaphoreType.DMA((groups, bits, 2)),
            pltpu.SemaphoreType.DMA((groups, bits, 2)),
            pltpu.SemaphoreType.DMA((groups, 2)),
            pltpu.SemaphoreType.DMA((pieces, 2 * groups // pieces)),
            pltpu.SemaphoreType.DMA((bits,)),
            pltpu.SemaphoreType.DMA((bits,)),
            pltpu.SemaphoreType.DMA((pieces,)),
            pltpu.SemaphoreType.DMA((pieces,)),
            pltpu.SemaphoreType.DMA,
            pltpu.SemaphoreType.DMA((2, depth // GC)),
            pltpu.VMEM((8, LANES), F32),
            pltpu.VMEM((bits + 1,) + few_shape, F32),
            pltpu.VMEM((bits,) + few_shape, F32),
            pltpu.VMEM((pieces,) + few_shape, F32),
            pltpu.SemaphoreType.DMA((bits,)),
            pltpu.SemaphoreType.DMA((bits,)),
            pltpu.SemaphoreType.DMA((pieces,)),
            pltpu.SemaphoreType.DMA((pieces,)),
            *[pltpu.VMEM((SLOTS,) + dims_left + (3, share, GC), BF) for dims_left in halves_of],
            *[pltpu.VMEM(dims_left + (share, 2 * STATE + LANES), BF) for dims_left in halves_of],
        ],
        compiler_params=pltpu.CompilerParams(
            collective_id=3 + layer, has_side_effects=True, vmem_limit_bytes=VMEM_LIMIT, dimension_semantics=("arbitrary",)
        ),
        name="layer_backward",
    )(
        g, x, after, gain, nxt, nht, r, w, w, w, w, few, pack, pack, pack, pack, pack, csw, csb, keep, biast, carried, tail, kept,
        gate, val, y, val, y, states, shared, step_in,
    )


def near_first(z, pieces):
    table = [sorted(range(pieces), key=lambda k: (abs(k - at), k > at)) for at in range(pieces)]
    return [sum(jnp.where(z == at, table[at][p], 0) for at in range(pieces)) for p in range(pieces)]


class Gather:
    def __init__(self, place, z, pieces, mine, wall, few, few_z, few_all, *sems):
        self.place, self.z, self.pieces, self.bits = place, z, pieces, place.bits
        self.mine, self.wall, self.few, self.few_z, self.few_all = mine, wall, few, few_z, few_all
        self.own_sem, self.z_send, self.z_recv, self.d_send, self.d_recv, *sems = sems
        self.t_send, self.t_recv, self.f_send, self.f_recv = sems
        wide = mine.shape[-1]
        self.cols = [pl.ds(0, wide // 2), pl.ds(wide // 2, wide // 2)]
        self.few_cols = [pl.ds(0, 2 * STATE), pl.ds(2 * STATE, LANES)]
        self.order = near_first(z, pieces)
        rest = list(range(1, self.bits))
        self.paths = [rest + [0], rest[::-1] + [0]]
        self.own = pltpu.make_async_copy(mine, wall.at[place.mine() + (z,)], self.own_sem)

    def z_copy(self, zi, up):
        src = self.mine if zi is self.z else self.wall.at[self.place.mine() + (zi,)]
        return pltpu.make_async_remote_copy(
            src_ref=src, dst_ref=self.wall.at[self.place.mine() + (zi,)], send_sem=self.z_send.at[int(up), zi],
            recv_sem=self.z_recv.at[zi], device_id={"tensor": self.z + (1 if up else -1)}, device_id_type=MESH,
        )

    def d_copy(self, p, half, step):
        path = self.paths[half]
        cols = (slice(None), slice(None), self.cols[half])
        ref = self.wall.at[self.place.along(path[:step]) + (self.order[p],) + cols]
        return pltpu.make_async_remote_copy(
            src_ref=ref if p or step else self.mine.at[cols], dst_ref=ref, send_sem=self.d_send.at[p, half, step], recv_sem=self.d_recv.at[p, half, step],
            device_id={"dp": self.place.flip(path[step])}, device_id_type=MESH,
        )

    def pass_on(self, zi, act):
        z, last = self.z, self.pieces - 1

        @pl.when(jnp.logical_and(zi <= z, z < last))
        def _():
            act(self.z_copy(zi, True))

        @pl.when(jnp.logical_and(zi >= z, z > 0))
        def _():
            act(self.z_copy(zi, False))

    def line_copy(self, k):
        return pltpu.make_async_remote_copy(
            src_ref=self.few.at[:, self.few_cols[1]], dst_ref=self.few_z.at[self.z], send_sem=self.t_send.at[k],
            recv_sem=self.t_recv.at[k], device_id={"tensor": lax.rem(self.z + k, self.pieces)}, device_id_type=MESH,
        )

    def few_copy(self, half, step):
        path = self.paths[half]
        ref = self.few_all.at[self.place.along(path[:step]) + (slice(None), self.few_cols[half])]
        return pltpu.make_async_remote_copy(
            src_ref=ref, dst_ref=ref, send_sem=self.f_send.at[half, step], recv_sem=self.f_recv.at[half, step],
            device_id={"dp": self.place.flip(path[step])}, device_id_type=MESH,
        )

    def few_event(self, step):
        if step == 0:
            total = self.few[:, self.few_cols[1]]
            for k in range(1, self.pieces):
                self.line_copy(k).wait_recv()
                total = total + self.few_z[lax.rem(self.z + self.pieces - k, self.pieces)]
            self.few_all[self.place.mine()] = jnp.concatenate([self.few[:, self.few_cols[0]], total], axis=1)
        for half in range(2):
            if step:
                self.few_copy(half, step - 1).wait_recv()
            if step < self.bits:
                self.few_copy(half, step).start()

    def start(self):
        for half in range(2):
            self.d_copy(0, half, 0).start()
        self.pass_on(self.z, lambda copy: copy.start())
        self.own.start()
        for k in range(1, self.pieces):
            self.line_copy(k).start()

    def arrive(self, p):
        zi = self.order[p]
        pltpu.make_async_remote_copy(
            src_ref=self.mine, dst_ref=self.wall.at[self.place.mine() + (zi,)], send_sem=self.z_send.at[0, zi],
            recv_sem=self.z_recv.at[zi], device_id={"tensor": zi}, device_id_type=MESH,
        ).wait_recv()
        self.pass_on(zi, lambda copy: copy.start())
        for half in range(2):
            self.d_copy(p, half, 0).start()

    def double(self, p, step):
        if p == 0 and step == 1:
            self.own.wait()
        for half in range(2):
            self.d_copy(p, half, step - 1).wait_recv()
            if step < self.bits:
                self.d_copy(p, half, step).start()

    def events(self):
        found = []
        for p in range(self.pieces):
            if p:
                found.append((10.0 * p, partial(self.arrive, p)))
            for step in range(1, self.bits + 1):
                late = 0.0 if step < self.bits - 1 else 0.8
                found.append((10.0 * p + 9.5 * step + late, partial(self.double, p, step)))
        for step in range(self.bits + 1):
            found.append((5.0 + 8.0 * step, partial(self.few_event, step)))
        return sorted(found, key=lambda event: event[0])

    def finish(self):
        for p in range(self.pieces):
            self.pass_on(self.order[p], lambda copy: copy.wait_send())
            for half in range(2):
                for step in range(self.bits):
                    self.d_copy(p, half, step).wait_send()
        for k in range(1, self.pieces):
            self.line_copy(k).wait_send()
        for half in range(2):
            for step in range(self.bits):
                self.few_copy(half, step).wait_send()


def greet(place, z, pieces):
    barrier = pltpu.get_barrier_semaphore()
    for b in range(place.bits):
        pl.semaphore_signal(barrier, inc=1, device_id={"dp": place.flip(b)}, device_id_type=MESH)
    for k in range(1, pieces):
        pl.semaphore_signal(barrier, inc=1, device_id={"tensor": lax.rem(z + k, pieces)}, device_id_type=MESH)
    pl.semaphore_wait(barrier, place.bits + pieces - 1)


def write_masks(z, tokens, starts_ref, keep_ref, bias_ref, biast_ref, carried_ref, tail_ref, kept_ref):
    first = z * tokens

    def label(position):
        total = None
        for k in range(starts_ref.shape[1]):
            term = jnp.where(position >= starts_ref[0, k], 1.0, 0.0)
            total = term if total is None else total + term
        return total

    def same(a, b):
        return jnp.where(a == b, 1.0, 0.0)

    for c in range(tokens // CH):
        begin = first + c * CH
        down = iota2((CH, LANES), 0) + begin
        across = iota2((CH, LANES), 1) + begin
        own, other = label(down), label(across)
        rows = pl.ds(c * CH, CH)
        for k in range(1, 4):
            keep_ref[k - 1, rows, :] = same(label(down - k), own)
        equal = own == other
        bias_ref[c] = jnp.where(equal, jnp.where(down >= across, 0.0, NEG), NEG)
        biast_ref[c] = jnp.where(equal, jnp.where(down <= across, 0.0, NEG), NEG)
        flat = jnp.zeros((CH, LANES), jnp.int32) + begin
        before, final = label(flat - 1), label(flat + (CH - 1))
        carried_ref[rows, :] = same(own, before)
        tail_ref[rows, :] = same(own, final)
        kept_ref[pl.ds(c, 1), :] = same(final, before)[:1]
    kept_ref[pl.ds(tokens // CH, 8 - tokens // CH), :] = jnp.zeros((8 - tokens // CH, LANES), F32)


def gather_kernel(
    dims, starts, tokens_ref, cotangent_ref, cvw, cvb, gate_gain, skip, bias_in, decay, bc, dt, mine, wall, x_all, g_all,
    few_out, few_later, pack_out, keep, bias, biast, carried, tail, kept,
    x_wide, g_wide, pack, pack_all, few, few_z, few_all, wide_sem, pk_send, pk_recv, *sems,
):
    pieces, tokens, bits = dims
    place = Place(bits)
    z = lax.axis_index("tensor")
    greet(place, z, pieces)
    gather = Gather(place, z, pieces, mine, wall, few, few_z, few_all, *sems)

    heads = skip.shape[1]
    upper_half = z >= pieces // 2
    first = HG * jnp.where(upper_half, pieces - 1 - z, z) + jnp.where(upper_half, HG // 2, 0)

    def lane_of(head):
        return first + HG * (pieces // 2) * (head // 2) + head % 2

    def spot(ref, layer):
        lane = iota2((1, LANES), 1)
        total = jnp.zeros((1, LANES), F32)
        for head in range(heads):
            total = jnp.where(lane == lane_of(head), ref[layer : layer + 1, head : head + 1], total)
        return total

    low, high = iota2((heads, LANES), 0), iota2((heads, LANES), 1)
    chosen = (lane_of(0) + HG * (pieces // 2) * (low // 2) + low % 2 == high).astype(F32).astype(BF)
    for layer in range(LAYERS):
        wide = jnp.concatenate([bc[layer], dot_nn(dt[layer], chosen).astype(BF)], axis=1)
        if layer == 0:
            few[...] = wide
        else:
            few_later[...] = wide
    gather.start()
    channel = iota2((1, cvb.shape[1]), 1) // HD
    for layer in range(LAYERS):
        skips = jnp.zeros(channel.shape, F32)
        for head in range(heads):
            skips = jnp.where(channel == head, skip[layer : layer + 1, head : head + 1], skips)
        own = slice(layer, layer + 1)
        rest = jnp.zeros((1, cvb.shape[1] - 2 * LANES), F32)
        tail_row = jnp.concatenate([spot(bias_in, layer), spot(decay, layer), rest], axis=1)
        pack[layer] = jnp.concatenate([cvw[layer], cvb[own], gate_gain[own], skips, tail_row], axis=0)

    def pack_copy(k):
        return pltpu.make_async_remote_copy(
            src_ref=pack, dst_ref=pack_all.at[z], send_sem=pk_send.at[k], recv_sem=pk_recv.at[k],
            device_id={"tensor": lax.rem(z + k, pieces)}, device_id_type=MESH,
        )

    for k in range(1, pieces):
        pack_copy(k).start()
    pack_all[z] = pack[...]
    wides = []
    for k, (narrow, wide, out) in enumerate(((tokens_ref, x_wide, x_all), (cotangent_ref, g_wide, g_all))):
        wide[...] = narrow[...].astype(F32)
        wides.append(pltpu.make_async_copy(wide, out, wide_sem.at[k]))
        wides[k].start()
    write_masks(z, tokens, starts, keep, bias, biast, carried, tail, kept)
    for _, act in gather.events():
        act()
    gather.finish()
    for copy in wides:
        copy.wait()
    for k in range(1, pieces):
        pack_copy(k).wait()
    few_out[...] = few_all[...]
    pack_out[...] = pack_all[...]


def gather_scratch(pieces, bits, share):
    dma = pltpu.SemaphoreType.DMA
    return [pltpu.VMEM((pieces, share, LANES), BF), pltpu.VMEM((2,) * bits + (share, 2 * STATE + LANES), BF)], [
        dma, dma((2, pieces)), dma((pieces,)), dma((pieces, 2, bits)), dma((pieces, 2, bits)),
        dma((pieces,)), dma((pieces,)), dma((2, bits)), dma((2, bits)),
    ]


def gather_first(dims, starts, x, g, params, bc, dt, share):
    pieces, tokens, bits = dims
    cut = (2,) * bits
    chunks = tokens // CH
    dma = pltpu.SemaphoreType.DMA
    anywhere = pl.BlockSpec(memory_space=pl.ANY)
    near = pl.BlockSpec(memory_space=pltpu.VMEM)
    buffers, sems = gather_scratch(pieces, bits, share.shape[1])
    pack = (LAYERS, 8, params[1].shape[1])
    few = (share.shape[1], 2 * STATE + LANES)
    return pl.pallas_call(
        partial(gather_kernel, dims),
        in_specs=[pl.BlockSpec(memory_space=pltpu.SMEM)] + [near] * 10 + [anywhere],
        out_specs=[anywhere] * 3 + [near] * 9,
        out_shape=[
            jax.ShapeDtypeStruct(cut + (pieces,) + share.shape, BF),
            jax.ShapeDtypeStruct(x.shape, F32),
            jax.ShapeDtypeStruct(g.shape, F32),
            jax.ShapeDtypeStruct(cut + few, BF),
            jax.ShapeDtypeStruct(few, BF),
            jax.ShapeDtypeStruct((pieces,) + pack, F32),
            jax.ShapeDtypeStruct((3, tokens, LANES), F32),
            jax.ShapeDtypeStruct((chunks, CH, CH), F32),
            jax.ShapeDtypeStruct((chunks, CH, CH), F32),
            jax.ShapeDtypeStruct((tokens, LANES), F32),
            jax.ShapeDtypeStruct((tokens, LANES), F32),
            jax.ShapeDtypeStruct((8, LANES), F32),
        ],
        scratch_shapes=[
            pltpu.VMEM(x.shape, F32), pltpu.VMEM(g.shape, F32), pltpu.VMEM(pack, F32), pltpu.VMEM((pieces,) + pack, F32),
            pltpu.VMEM(few, BF),
        ] + buffers + [dma((2,)), dma((pieces,)), dma((pieces,))] + sems,
        compiler_params=pltpu.CompilerParams(collective_id=2, has_side_effects=True, vmem_limit_bytes=VMEM_LIMIT),
        name="gather_first",
    )(starts, x, g, *params, bc, dt, share)


def local(
    tokens, gate_value_weight, w_bc, w_dt, w_out, norm_gain, conv_value_w, conv_value_b, conv_shared_w, conv_shared_b,
    step_bias, decay_log, skip_gain, gate_gain, starts, cotangent,
):
    pieces, dp = lax.axis_size("tensor"), lax.axis_size("dp")
    z = lax.axis_index("tensor")
    bits = (dp - 1).bit_length()
    count, depth = tokens.shape
    own = conv_value_b.shape[1]
    few = step_bias.shape[1]
    groups = pieces * own // GC
    dims = (pieces, groups, count, pieces - 1)

    shares = [
        jnp.concatenate([jnp.swapaxes(gate_value_weight[layer], 0, 1), w_out[layer][None]], axis=0)
        for layer in range(LAYERS)
    ]
    wall, x, grad, few_all, few_later, pack, *masks = gather_first(
        (pieces, count, bits), starts, tokens, cotangent,
        (conv_value_w, conv_value_b, gate_gain, skip_gain, step_bias, decay_log), w_bc, w_dt, shares[0],
    )
    line, saved, weights = [x], [], []
    for layer in range(LAYERS):
        weights.append((wall.reshape((dp,) + wall.shape[bits:]), few_all.reshape((dp,) + few_all.shape[bits:])))
        later = (few_later, shares[layer + 1]) if layer + 1 < LAYERS else None
        x, *kept = layer_forward(
            dims, bits, layer, x, norm_gain, *weights[-1], pack, conv_shared_w, conv_shared_b, masks, later
        )
        if later is not None:
            *kept, few_all, wall = kept
        line.append(x)
        saved.append(kept)
    upper_half = z >= pieces // 2
    at = jnp.where(upper_half, pieces - 1 - z, z)

    def own_heads(v):
        v = v[..., : pieces * few].reshape(v.shape[:-1] + (few // 2, pieces // 2, 2, 2))
        v = lax.dynamic_index_in_dim(v, at, axis=v.ndim - 3, keepdims=False)
        v = lax.dynamic_index_in_dim(v, upper_half.astype(jnp.int32), axis=v.ndim - 2, keepdims=False)
        return v.reshape(v.shape[:-2] + (few,))

    big, small = [None] * LAYERS, [None] * LAYERS
    for layer in reversed(range(LAYERS)):
        grad, gw, gm, small[layer] = layer_backward(
            dims, bits, layer, grad, line[layer], line[layer + 1], norm_gain, saved[layer], *weights[layer], pack,
            conv_shared_w, conv_shared_b, masks,
        )
        gdt = own_heads(gm[:, 2 * STATE :])
        big[layer] = (jnp.swapaxes(gw[:2], 0, 1), gm[:, : 2 * STATE], gdt, gw[2])
    small = jnp.stack(small)

    def stacked(member):
        return jnp.stack([big[layer][member] for layer in range(LAYERS)], axis=0)

    rows = small[:, : groups * 8].reshape(LAYERS, 2 * groups // pieces, pieces // 2, 8, 2, LANES)
    rows = lax.dynamic_index_in_dim(rows, at, axis=2, keepdims=False)
    rows = lax.dynamic_index_in_dim(rows, upper_half.astype(jnp.int32), axis=3, keepdims=False)
    rows = jnp.swapaxes(rows, 1, 2).reshape(LAYERS, 8, own)
    gcs = small[:, groups * 8 : groups * 8 + 8]
    ends = small[:, groups * 8 + 8 :]
    cuts = depth // GC
    gheads = own_heads(ends[:, cuts].reshape(LAYERS, 2, LANES))
    return (
        x.astype(BF), grad, stacked(0), stacked(1), stacked(2), stacked(3), ends[:, :cuts].reshape(LAYERS, depth),
        rows[:, :4], rows[:, 4], gcs[:, :4], gcs[:, 4], gheads[:, 0], gheads[:, 1],
        jnp.sum(rows[:, 6].reshape(LAYERS, few, HD), axis=2), rows[:, 5],
    )


def solution(mesh):
    in_specs = (
        P(("dp", "tensor"), None),
        P(None, "dp", None, "tensor"),
        P(None, "dp", None),
        P(None, "dp", "tensor"),
        P(None, "dp", "tensor"),
        P(),
        P(None, None, "tensor"),
        P(None, "tensor"),
        P(),
        P(),
        P(None, "tensor"),
        P(None, "tensor"),
        P(None, "tensor"),
        P(None, "tensor"),
        P("dp", None),
        P(("dp", "tensor"), None),
    )
    out_specs = (
        P(("dp", "tensor"), None),
        P(("dp", "tensor"), None),
        P(None, "dp", None, "tensor"),
        P(None, "dp", None),
        P(None, "dp", "tensor"),
        P(None, "dp", "tensor"),
        P(),
        P(None, None, "tensor"),
        P(None, "tensor"),
        P(),
        P(),
        P(None, "tensor"),
        P(None, "tensor"),
        P(None, "tensor"),
        P(None, "tensor"),
    )
    return jax.shard_map(local, mesh=mesh, in_specs=in_specs, out_specs=out_specs, check_vma=False)
```

```python
from functools import partial

import jax
import jax.numpy as jnp
from jax import lax
from jax.experimental import pallas as pl
from jax.experimental.pallas import tpu as pltpu
from jax.sharding import PartitionSpec as P

LAYERS = 2
EPS = 1e-05
HALO = 16
CH = 128
GC = 256
HD = 64
HG = GC // HD
LANES = 128
STATE = 128
NEG = -1e30
SLOTS = 2
VMEM_LIMIT = 60 * 1024 * 1024
VMEM_LIMIT_FORWARD = 62 * 1024 * 1024
MESH = pl.DeviceIdType.MESH
HI = lax.Precision.HIGHEST
F32 = jnp.float32
BF = jnp.bfloat16


def dot_nn(a, b, precision=None):
    return lax.dot_general(a, b, (((1,), (0,)), ((), ())), precision=precision, preferred_element_type=F32)


def dot_nt(a, b):
    return lax.dot_general(a, b, (((1,), (1,)), ((), ())), preferred_element_type=F32)


def dot_tn(a, b):
    return lax.dot_general(a, b, (((0,), (0,)), ((), ())), preferred_element_type=F32)


def sigmoid(v):
    return 0.5 * jnp.tanh(0.5 * v) + 0.5


def twice(v):
    return jnp.concatenate([v, v], axis=1)


def split2(v):
    high = v.astype(BF)
    return jnp.concatenate([high, (v - high.astype(F32)).astype(BF)], axis=1)


def iota2(shape, dim):
    return lax.broadcasted_iota(jnp.int32, shape, dim)


def spread(group):
    row = iota2((2 * LANES, GC), 0) % LANES
    head = iota2((2 * LANES, GC), 1) // HD + group * HG
    return (row == head).astype(F32).astype(BF)


def collect(group):
    head = (iota2((2 * GC, LANES), 0) % GC) // HD + group * HG
    return (head == iota2((2 * GC, LANES), 1)).astype(F32).astype(BF)


def conv(load, keep_ref, weights, tokens):
    total = weights[4:5] + weights[0:1] * load(0)
    for k in range(1, 4):
        total = total + weights[k : k + 1] * (load(k) * twice(keep_ref[k - 1]))
    return total


def conv_back(grad, load, keep_ref, weights, tokens):
    rows = []
    total = None
    for k in range(4):
        part = grad if k == 0 else grad * twice(keep_ref[k - 1])
        rows.append(jnp.sum(part * load(k), axis=0, keepdims=True))
        wide = jnp.concatenate([jnp.zeros((HALO, grad.shape[1]), F32), weights[k : k + 1] * part], axis=0)
        if k:
            wide = pltpu.roll(wide, tokens + HALO - k, 0)
        total = wide if total is None else total + wide
    rows.append(jnp.sum(grad, axis=0, keepdims=True))
    return total, rows


def step_terms(step_in, heads_ref, carried_ref, tail_ref, kept_ref, tokens):
    chunks = tokens // CH
    raw = step_in + heads_ref[0:1]
    steps = jnp.maximum(raw, 0.0) + jnp.log1p(jnp.exp(-jnp.abs(raw)))
    rates = -steps * heads_ref[1:2]
    lower = (iota2((CH, CH), 0) >= iota2((CH, CH), 1)).astype(F32)
    sums, toward, kept = [], [], []
    for c in range(chunks):
        summed = dot_nn(lower, rates[c * CH : (c + 1) * CH], HI)
        last = summed[CH - 1 : CH]
        sums.append(summed)
        toward.append(jnp.exp(last - summed))
        kept.append(jnp.exp(last) * kept_ref[c : c + 1])
    kept.append(jnp.zeros((8 - chunks, LANES), F32))
    summed = jnp.concatenate(sums, axis=0)
    toward = jnp.concatenate(toward, axis=0) * tail_ref[...]
    reach = jnp.exp(summed) * carried_ref[...]
    return raw, steps, rates, summed, toward, reach, jnp.concatenate(kept, axis=0)


def put_sums(summed, col_ref, row_ref, groups, tokens):
    for c in range(tokens // CH):
        turned = summed[c * CH : (c + 1) * CH].T
        for group in range(groups):
            row_ref[group, 0:HG, c * CH : (c + 1) * CH] = turned[group * HG : (group + 1) * HG]
    col_ref[0] = summed


def turn_sums(col_ref, group):
    col_ref[1] = pltpu.roll(col_ref[0], lax.rem(LANES - group * HG, LANES), 1)


def put_heads(rows_ref, heads_ref):
    total = rows_ref[0, 0, 7:8, :]
    for k in range(1, rows_ref.shape[0]):
        total = total + rows_ref[k, 0, 7:8, :]
    heads_ref[...] = jnp.concatenate(
        [total[:, :LANES], jnp.exp(total[:, LANES:]), jnp.zeros((6, LANES), F32)], axis=0
    )


def shared_taps(csw_ref, csb_ref, layer):
    return jnp.concatenate([csw_ref[layer], csb_ref[layer : layer + 1]], axis=0)


def halves(v):
    first = iota2(v.shape, 1) < HD
    return jnp.concatenate([jnp.where(first, v, 0.0), jnp.where(first, 0.0, v)], axis=0).astype(BF)


def forward_kernel(
    dims,
    x_ref, gain_ref, wa, wb, oa, ob, few_ref, pa, pb, qa, qb, rows_ref, csw_ref, csb_ref,
    keep_ref, bias_ref, carried_ref, tail_ref, kept_ref, *rest,
):
    pieces, groups, tokens, skew, bits, layer, gathers = dims
    if gathers:
        few_mine, _, *rest = rest
    if layer:
        rest = rest[9:]
    next_ref, nxt_ref, nht_ref, gate_ref, val_ref, y_ref, state_ref, shared_ref, step_ref, r_ref, *rest = rest
    if gathers:
        few_out, wall_ref, *rest = rest
    nx, inb, inbt, outb, cross, col, row, terms, ke, intra, xs, gs, fresh, fold, *rest = rest
    incoming, outgoing, branch, squares, heads_ref, halo_send, halo_recv, send, recv, *rest = rest
    if gathers:
        few_z, few_all, *rest = rest
    place = Place(bits)
    chunks = tokens // CH
    i = pl.program_id(0)
    z = lax.axis_index("tensor")
    right, left = jnp.minimum(z + 1, pieces - 1), jnp.maximum(z - 1, 0)

    def halo_copy():
        return pltpu.make_async_remote_copy(
            src_ref=nx.at[pl.ds(tokens, HALO)], dst_ref=nx.at[pl.ds(0, HALO)],
            send_sem=halo_send, recv_sem=halo_recv, device_id={"tensor": right}, device_id_type=MESH,
        )

    def state_copy(group):
        return pltpu.make_async_remote_copy(
            src_ref=outgoing.at[group], dst_ref=incoming.at[group],
            send_sem=send.at[group], recv_sem=recv.at[group], device_id={"tensor": right}, device_id_type=MESH,
        )

    plan = [[] for _ in range(groups + skew)]
    if gathers:
        plane = Plane(place, z, pieces, None, wall_ref, few_mine, few_z, few_all, *rest)
        for step in range(1, bits + 1):
            for p in range(pieces):
                plan[min(4 * step + p - 2, groups + skew - 1)].append(partial(plane.double, p, step))
        for step in range(bits + 1):
            plan[min(2 * step + 1, groups + skew - 1)].append(partial(plane.few_event, step))

    @pl.when(i == 0)
    def _():
        greet(place, z, pieces)
        x = x_ref[...]
        scale = lax.rsqrt(jnp.mean(x * x, axis=1, keepdims=True) + EPS)
        nx[pl.ds(HALO, tokens), :] = (x * scale * gain_ref[layer : layer + 1]).astype(BF)
        put_heads(rows_ref, heads_ref)

        @pl.when(z < pieces - 1)
        def _():
            halo_copy().start()

        if gathers:
            for p in range(pieces):
                plane.start(p)
            plane.start_few()

        @pl.when(z == 0)
        def _():
            nx[pl.ds(0, HALO), :] = jnp.zeros((HALO, nx.shape[1]), BF)
            incoming[...] = jnp.zeros(incoming.shape, BF)

        depth = nx.shape[1]
        step_in = dot_nn(nx[pl.ds(HALO, tokens), :], few_ref[..., 2 * STATE :].reshape(depth, LANES))
        step_ref[...] = step_in
        _, steps, _, summed, toward, reach, kept = step_terms(
            step_in, heads_ref, carried_ref, tail_ref, kept_ref, tokens
        )
        put_sums(summed, col, row, groups, tokens)
        terms[0] = split2(steps)
        terms[1] = split2(toward)
        terms[2] = split2(reach)
        kept2 = split2(kept)
        for group in range(groups):
            ke[group] = dot_nn(kept2, spread(group))

        @pl.when(z > 0)
        def _():
            halo_copy().wait_recv()

        shared_ref[...] = dot_nn(nx[...], few_ref[..., : 2 * STATE].reshape(depth, 2 * STATE))
        taps = shared_taps(csw_ref, csb_ref, layer)
        mixed = conv(lambda k: shared_ref[pl.ds(HALO - k, tokens), :], keep_ref, taps, tokens)
        maps = mixed * sigmoid(mixed)
        for c in range(chunks):
            part = maps[c * CH : (c + 1) * CH]
            into, out = part[:, :STATE], part[:, STATE:].astype(BF)
            inb[c], outb[c], inbt[c] = into.astype(BF), out, into.T.astype(BF)
            cross[c] = dot_nt(out, into.astype(BF))
        branch[...] = jnp.zeros(branch.shape, F32)
        squares[...] = jnp.zeros(squares.shape, F32)

    @pl.when(i < groups)
    def _():
        depth = nx.shape[1]
        group = i
        slot = lax.rem(group, skew + 1)
        gate_ref[0] = dot_nn(nx[pl.ds(HALO, tokens), :], side((wa, wb), 0))
        val_ref[0] = dot_nn(nx[...], side((wa, wb), 1))
        mixed = conv(lambda k: val_ref[0, pl.ds(HALO - k, tokens), :], keep_ref, side_params((pa, pb)), tokens)
        xs[slot] = mixed * sigmoid(mixed)
        gate = gate_ref[0]
        gs[slot] = gate * sigmoid(gate)
        turn_sums(col, group)
        spreader = spread(group)
        state = jnp.zeros((STATE, GC), F32)
        for c in range(chunks):
            rows = pl.ds(c * CH, CH)
            sized = xs[slot, rows, :] * dot_nn(terms[0, rows, :], spreader)
            weighted = (sized * dot_nn(terms[1, rows, :], spreader)).astype(BF)
            new = dot_nn(inbt[c], weighted)
            fresh[slot, c] = new
            state = ke[group, c : c + 1] * state + new
            for pair in range(HG // 2):
                lanes = pl.ds(pair * LANES, LANES)
                decayed = []
                for j in (2 * pair, 2 * pair + 1):
                    across = col[1, rows, j : j + 1] - row[group, j : j + 1, rows]
                    decayed.append((cross[c] * jnp.exp(jnp.minimum(across, bias_ref[c]))).astype(BF))
                blocks = halves(sized[:, pair * LANES : (pair + 1) * LANES])
                intra[slot, rows, lanes] = dot_nn(jnp.concatenate(decayed, axis=1), blocks)
        fold[slot] = state

    j = i - z

    @pl.when(jnp.logical_and(j >= 0, j < groups))
    def _():
        @pl.when(z > 0)
        def _():
            state_copy(j).wait_recv()

        @pl.when(z < pieces - 1)
        def _():
            total = ke[j, 0:1]
            for c in range(1, chunks):
                total = total * ke[j, c : c + 1]
            outgoing[j] = (total * incoming[j].astype(F32) + fold[lax.rem(j, skew + 1)]).astype(BF)
            state_copy(j).start()

    @pl.when(i >= skew)
    def _():
        group = i - skew
        slot = lax.rem(group, skew + 1)
        depth = nx.shape[1]
        spreader = spread(group)
        gp = side_params((qa, qb))
        state = incoming[group].astype(F32)
        for c in range(chunks):
            rows = pl.ds(c * CH, CH)
            low = state.astype(BF)
            state_ref[0, c] = low
            y = intra[slot, rows, :] + dot_nn(outb[c], low) * dot_nn(terms[2, rows, :], spreader)
            y_ref[0, rows, :] = y
            gated = (y + gp[6:7] * xs[slot, rows, :]) * gs[slot, rows, :]
            squares[rows, :] += jnp.sum(gated * gated, axis=1, keepdims=True)
            intra[slot, rows, :] = gated * gp[5:6]
            if c < chunks - 1:
                state = ke[group, c : c + 1] * state + fresh[slot, c]
        branch[...] += dot_nt(intra[slot].astype(BF), side((oa, ob), 0))

    for step, acts in enumerate(plan):
        if acts:

            @pl.when(i == step)
            def _(acts=acts):
                for act in acts:
                    act()

    @pl.when(i == groups + skew - 1)
    def _():
        inner = groups * GC
        factor = lax.rsqrt(squares[...] * (1.0 / inner) + EPS)
        r_ref[...] = factor
        next_ref[...] = x_ref[...] + branch[...] * factor[:, 0:1]
        nxt_ref[...] = nx[pl.ds(HALO, tokens), :].T
        nht_ref[...] = nx[pl.ds(0, HALO), :].T
        if gathers:
            plane.finish()
            few_out[...] = few_all[...]

        @pl.when(z < pieces - 1)
        def _():
            halo_copy().wait_send()
            for group in range(groups):
                state_copy(group).wait_send()


class Place:
    def __init__(self, bits):
        self.bits = bits
        self.index = lax.axis_index("dp")
        self.bit = [lax.rem(self.index // (1 << b), 2) for b in range(bits)]
        self.dims = (2,) * bits
        self.all = (slice(None),) * bits

    def flip(self, b):
        return self.index + (1 << b) * (1 - 2 * self.bit[b])

    def along(self, done):
        return tuple(slice(None) if b in done else self.bit[b] for b in reversed(range(self.bits)))

    def order(self, odd):
        rest = list(range(1, self.bits))
        return [0] + (rest[::-1] if odd else rest)

    def partner(self, odd, step):
        return self.flip(self.order(odd)[step])

    def region(self, odd, step, keep):
        order = self.order(odd)
        at = []
        for b in reversed(range(self.bits)):
            if b in order[:step]:
                at.append(self.bit[b])
            elif b == order[step]:
                at.append(self.bit[b] if keep else 1 - self.bit[b])
            else:
                at.append(slice(None))
        return tuple(at)

    def mine(self):
        return tuple(self.bit[b] for b in reversed(range(self.bits)))


def backward_kernel(
    dims,
    g_ref, *refs,
):
    pieces, groups, tokens, skew, bits = dims
    line_refs, refs = refs[: LAYERS + 1], refs[LAYERS + 1 :]
    weights, refs = [refs[5 * n : 5 * n + 5] for n in range(LAYERS)], refs[5 * LAYERS :]
    gain_ref, nxt, nht, r_ref, pa, pb, qa, qb, rows_ref, *refs = refs
    csw_ref, csb_ref, keep_ref, biast_ref, carried_ref, tail_ref, kept_ref, *refs = refs
    gate_ref, val_ref, y_ref, valb_ref, state_ref, shared_ref, step_ref, *refs = refs
    gx_ref, gw_ref, gm_ref, small_ref, mid_ref, *refs = refs
    gb, gbt, r2, inb, outb, outbt, crosst, col, row, terms, ke, *refs = refs
    dys, xs, fs, dgs, fold, incoming, outgoing, gnorm, dct, dbt, dgt, sd, sp, sq, se, dxd, hrecv, *refs = refs
    own, own_m, got_z, got_m, halo_send, halo_recv, send, recv, sum_send, sum_recv, z_send, z_recv, *refs = refs
    msum_send, msum_recv, mz_send, mz_recv, next_sem, load_sem, heads_ref, *refs = refs
    few_total, few_got, few_z, few_send, few_recv, fz_send, fz_recv, *got = refs
    chunks = tokens // CH
    phase, i = pl.program_id(0), pl.program_id(1)
    layer = LAYERS - 1 - phase
    z = lax.axis_index("tensor")
    right, left = jnp.minimum(z + 1, pieces - 1), jnp.maximum(z - 1, 0)
    back = pieces - 1 - z
    depth = gb.shape[1]
    inner = groups * GC

    def halo_copy():
        return pltpu.make_async_remote_copy(
            src_ref=gnorm, dst_ref=hrecv.at[phase], send_sem=halo_send, recv_sem=halo_recv.at[phase],
            device_id={"tensor": left}, device_id_type=MESH,
        )

    def state_copy(group):
        return pltpu.make_async_remote_copy(
            src_ref=outgoing.at[group], dst_ref=incoming.at[phase, group],
            send_sem=send.at[group], recv_sem=recv.at[phase, group], device_id={"tensor": left}, device_id_type=MESH,
        )

    place = Place(bits)
    parts, parts_m = got[:bits], got[bits:]

    def part(step, group, half):
        left = (slice(None),) * (bits - 1 - step + 2)
        return (lax.rem(group, SLOTS),) + left + (pl.ds(half * LANES, LANES),)

    def held(step, group, half, keep):
        return (group,) + place.region(half, step, keep) + (slice(None), slice(None), pl.ds(half * LANES, LANES))

    def sum_copy(group, step, half):
        return pltpu.make_async_remote_copy(
            src_ref=own.at[held(step, group, half, False)], dst_ref=parts[step].at[part(step, group, half)],
            send_sem=sum_send.at[group, step, half], recv_sem=sum_recv.at[group, step, half],
            device_id={"dp": place.partner(half, step)}, device_id_type=MESH,
        )

    def z_copy(group, half, turn):
        column = lax.div(group, pieces // 2)
        return pltpu.make_async_remote_copy(
            src_ref=own.at[(group,) + place.mine() + (slice(None), slice(None), pl.ds(half * LANES, LANES))],
            dst_ref=got_z.at[turn, z, column], send_sem=z_send.at[group, half], recv_sem=z_recv.at[turn, z, column],
            device_id={"tensor": quarter(group, half, pieces)}, device_id_type=MESH,
        )

    def advance(group, step, turn):
        @pl.when(jnp.logical_and(group >= 0, group < groups))
        def _():
            for half in range(2):
                if step:
                    sum_copy(group, step - 1, half).wait_recv()
                    at = held(step - 1, group, half, True)
                    own[at] = own[at] + parts[step - 1][part(step - 1, group, half)]
                if step < bits:
                    sum_copy(group, step, half).start()
                if step == bits:

                    @pl.when(quarter(group, half, pieces) != z)
                    def _(half=half):
                        z_copy(group, half, turn).start()

    def misc_copy(step):
        return pltpu.make_async_remote_copy(
            src_ref=own_m.at[place.region(False, step, False)], dst_ref=parts_m[step],
            send_sem=msum_send.at[step], recv_sem=msum_recv.at[step],
            device_id={"dp": place.partner(False, step)}, device_id_type=MESH,
        )

    def misc_z(k, turn, source):
        return pltpu.make_async_remote_copy(
            src_ref=own_m.at[place.mine()], dst_ref=got_m.at[turn, source], send_sem=mz_send.at[k],
            recv_sem=mz_recv.at[turn, source],
            device_id={"tensor": lax.rem(z + k, pieces)}, device_id_type=MESH,
        )

    def misc_advance(step, turn):
        if step:
            misc_copy(step - 1).wait_recv()
            at = place.region(False, step - 1, True)
            own_m[at] = own_m[at] + parts_m[step - 1][...]
        if step < bits:
            misc_copy(step).start()
        else:
            for k in range(1, pieces):
                misc_z(k, turn, z).start()
            got_m[turn, z] = own_m[place.mine()]

    def drain(late, turn):
        for step in reversed(range(1, bits + 1)):
            if late <= step:
                advance(jnp.int32(groups - 1 + late - step), step, turn)

    def few_copy(step):
        return pltpu.make_async_remote_copy(
            src_ref=few_total.at[step], dst_ref=few_got.at[step], send_sem=few_send.at[step],
            recv_sem=few_recv.at[step], device_id={"dp": place.partner(False, step)}, device_id_type=MESH,
        )

    def few_line(k, turn, source):
        return pltpu.make_async_remote_copy(
            src_ref=few_total.at[bits], dst_ref=few_z.at[turn, source], send_sem=fz_send.at[k],
            recv_sem=fz_recv.at[turn, source],
            device_id={"tensor": lax.rem(z + k, pieces)}, device_id_type=MESH,
        )

    def few_advance(step, turn):
        if step:
            few_copy(step - 1).wait_recv()
            few_total[step] = few_total[step - 1] + few_got[step - 1]
        if step < bits:
            few_copy(step).start()
        else:
            for k in range(1, pieces):
                few_line(k, turn, z).start()
            few_z[turn, z] = few_total[bits]

    def finish_few(turn):
        for n in range(1, pieces):
            few_line(n, turn, lax.rem(z + n, pieces)).wait_recv()
            misc_z(n, turn, lax.rem(z + n, pieces)).wait_recv()
        total, misc = few_z[turn, 0], got_m[turn, 0].astype(F32)
        for source in range(1, pieces):
            total = total + few_z[turn, source]
            misc = misc + got_m[turn, source].astype(F32)
        small_ref[LAYERS - 1 - turn] = total
        gm_ref[LAYERS - 1 - turn] = misc
        for step in range(bits):
            misc_copy(step).wait_send()
            few_copy(step).wait_send()
        for n in range(1, pieces):
            misc_z(n, turn, z).wait_send()
            few_line(n, turn, z).wait_send()

    def finish_group(group, turn):
        column = lax.div(group, pieces // 2)
        for half in range(2):

            @pl.when(quarter(group, half, pieces) == z)
            def _(half=half):
                total = own[(group,) + place.mine() + (slice(None), slice(None), pl.ds(half * LANES, LANES))]
                total = total.astype(F32)
                for n in range(1, pieces):
                    source = lax.rem(z + n, pieces)
                    pltpu.make_async_remote_copy(
                        src_ref=got_z.at[turn, source, column], dst_ref=got_z.at[turn, source, column],
                        send_sem=z_send.at[group, half], recv_sem=z_recv.at[turn, source, column],
                        device_id={"tensor": source}, device_id_type=MESH,
                    ).wait_recv()
                    total = total + got_z[turn, source, column].astype(F32)
                at = pl.multiple_of(column * LANES, LANES)
                gw_ref[LAYERS - 1 - turn, :, :, pl.ds(at, LANES)] = total

            @pl.when(quarter(group, half, pieces) != z)
            def _(half=half):
                z_copy(group, half, turn).wait_send()

            for step in range(bits):
                sum_copy(group, step, half).wait_send()

    def load(x, g):
        found = []
        for n in range(depth // GC):
            cols = pl.ds(n * GC, GC)
            found.append(pltpu.make_async_copy(x.at[:, cols], xs.at[n], load_sem.at[0, n]))
            if g is not None:
                found.append(pltpu.make_async_copy(g.at[:, cols], fs.at[n], load_sem.at[1, n]))
        return found

    def of_layer(pick):
        chosen = pick(0)
        for n in range(1, LAYERS):
            chosen = jnp.where(layer == n, pick(n), chosen)
        return chosen

    def out_weights():
        return of_layer(lambda n: side(weights[n][2:4], 0))

    def in_weights(which):
        return of_layer(lambda n: side(weights[n][:2], which))

    def taps():
        return jnp.concatenate([csw_ref[layer], csb_ref[pl.ds(layer, 1), :]], axis=0)

    def shared_conv():
        return conv(lambda k: shared_ref[pl.ds(HALO - k, tokens), :], keep_ref, taps(), tokens)

    @pl.when(jnp.logical_and(phase == 0, i == 0))
    def _():
        greet(place, z, pieces)

        @pl.when(z == pieces - 1)
        def _():
            incoming[...] = jnp.zeros(incoming.shape, BF)

        copies = [pltpu.make_async_copy(line_refs[LAYERS], gx_ref, next_sem)] + load(line_refs[LAYERS - 1], g_ref)
        for copy in copies:
            copy.start()
        for copy in copies:
            copy.wait()

    for turn in range(1, LAYERS):

        @pl.when(jnp.logical_and(phase == turn, i == 0))
        def _(turn=turn):
            copies = load(line_refs[LAYERS - 1 - turn], None)
            copies.append(pltpu.make_async_copy(gx_ref, mid_ref, next_sem))
            for copy in copies:
                copy.start()
            for n in range(depth // GC):
                fs[n] = gx_ref[:, n * GC : (n + 1) * GC]
            for copy in copies:
                copy.wait()
            copy = pltpu.make_async_copy(line_refs[LAYERS - turn], gx_ref, next_sem)
            copy.start()
            copy.wait()

    @pl.when(i == 0)
    def _():
        put_heads(rows_ref, heads_ref)
        dots = jnp.zeros((tokens, 1), F32)
        for k in range(depth // GC):
            cols = slice(k * GC, (k + 1) * GC)
            low = fs[k].astype(BF)
            gb[:, cols] = low
            gbt[cols, :] = low.T
            dots = dots + jnp.sum(low.astype(F32) * (gx_ref[:, cols] - xs[k]), axis=1, keepdims=True)
        r = r_ref[...]
        r2[...] = r * r * dots * (1.0 / inner)
        _, steps, _, summed, toward, reach, kept = step_terms(
            step_ref[...], heads_ref, carried_ref, tail_ref, kept_ref, tokens
        )
        put_sums(summed, col, row, groups, tokens)
        terms[0] = split2(steps)
        terms[1] = split2(toward)
        terms[2] = split2(reach)
        kept2 = split2(kept)
        for group in range(groups):
            ke[group] = dot_nn(kept2, spread(group))
        mixed = shared_conv()
        maps = mixed * sigmoid(mixed)
        for c in range(chunks):
            part = maps[c * CH : (c + 1) * CH]
            into, out = part[:, :STATE].astype(BF), part[:, STATE:]
            inb[c], outb[c], outbt[c] = into, out.astype(BF), out.T.astype(BF)
            crosst[c] = dot_nt(into, out.astype(BF))
        for ref in (gx_ref, gnorm, dct, dbt, dgt, sd, sp, sq, se):
            ref[...] = jnp.zeros(ref.shape, F32)

    @pl.when(i < groups)
    def _():
        group = i
        slot = lax.rem(group, skew + 1)
        gp = side_params((pa, pb))
        mixed = conv(lambda k: val_ref[0, pl.ds(HALO - k, tokens), :], keep_ref, gp, tokens)
        part = sigmoid(mixed)
        x = mixed * part
        xs[slot] = x
        fs[slot] = part + x * (1.0 - part)
        r = twice(r_ref[...])

        for turn in range(1, LAYERS):

            @pl.when(phase == turn)
            def _(turn=turn):
                finish_group(group, turn - 1)

        gm = dot_nn(gb[...], out_weights())
        scan = y_ref[0] + gp[6:7] * x
        gate = gate_ref[0]
        part = sigmoid(gate)
        silu = gate * part
        gated = scan * silu
        normal = gated * r
        own[(group,) + place.all + (2,)] = (
            dot_nn(gbt[...], (normal * gp[5:6]).astype(BF)).astype(BF).reshape(place.dims + (-1, GC))
        )
        ggated = r * gp[5:6] * gm - gated * twice(r2[...])
        dy = ggated * silu
        dys[slot] = dy.astype(BF)
        dgs[slot] = (ggated * scan * (part + silu * (1.0 - part))).astype(BF)
        small_ref[layer, pl.ds(group * 8, 8), :] = jnp.concatenate(
            [
                jnp.zeros((5, GC), F32),
                jnp.sum(gm * normal, axis=0, keepdims=True),
                jnp.sum(dy * x, axis=0, keepdims=True),
                jnp.zeros((1, GC), F32),
            ],
            axis=0,
        )
        spreader, collector = spread(group), collect(group)
        state = jnp.zeros((STATE, GC), F32)
        for c in reversed(range(chunks)):
            rows = pl.ds(c * CH, CH)
            reached = (dys[slot, rows, :].astype(F32) * dot_nn(terms[2, rows, :], spreader)).astype(BF)
            sp[rows, :] += dot_nn(split2(dys[slot, rows, :].astype(F32) * y_ref[0, rows, :]), collector)
            new = dot_nn(outbt[c], reached)
            state = ke[group, c : c + 1] * state + new
        fold[slot] = state

    for turn in range(1, LAYERS):
        for late in range(1, max(bits, skew) + 1):
            place_at = min(late, skew) - 1

            @pl.when(jnp.logical_and(phase == turn, i == place_at))
            def _(turn=turn, late=late):
                drain(late, turn - 1)
                if late <= bits:
                    few_advance(late, turn - 1)
                    misc_advance(late, turn - 1)

        @pl.when(jnp.logical_and(phase == turn, i == skew))
        def _(turn=turn):
            finish_few(turn - 1)

    j = i - back

    @pl.when(jnp.logical_and(j >= 0, j < groups))
    def _():
        @pl.when(z < pieces - 1)
        def _():
            state_copy(j).wait_recv()

        @pl.when(z > 0)
        def _():
            total = ke[j, 0:1]
            for c in range(1, chunks):
                total = total * ke[j, c : c + 1]
            outgoing[j] = (total * incoming[phase, j].astype(F32) + fold[lax.rem(j, skew + 1)]).astype(BF)
            state_copy(j).start()

    @pl.when(i >= skew)
    def _():
        group = i - skew
        slot = lax.rem(group, skew + 1)
        gp = side_params((qa, qb))
        spreader, collector = spread(group), collect(group)
        turn_sums(col, group)
        grad = incoming[phase, group].astype(F32)
        ends = [None] * chunks
        for c in reversed(range(chunks)):
            rows = pl.ds(c * CH, CH)
            low = grad.astype(BF)
            state = state_ref[0, c]
            ends[c] = jnp.sum(low.astype(F32) * state.astype(F32), axis=0, keepdims=True) * ke[group, c : c + 1]
            x = xs[slot, rows, :]
            dy = dys[slot, rows, :].astype(F32)
            steps = dot_nn(terms[0, rows, :], spreader)
            toward = dot_nn(terms[1, rows, :], spreader)
            reached = (dy * dot_nn(terms[2, rows, :], spreader)).astype(BF)
            grad = ke[group, c : c + 1] * grad + dot_nn(outbt[c], reached)
            sized = x * steps
            weighted = (sized * toward).astype(BF)
            later = dot_nn(inb[c], low) * toward
            dbt[c] += dot_nt(weighted, low)
            dct[c] += dot_nt(reached, state)
            parts = []
            cross = crosst[c]
            pairs_total = jnp.zeros((CH, CH), F32)
            for pair in range(HG // 2):
                at = slice(pair * LANES, (pair + 1) * LANES)
                dyp = dy[:, at]
                products = dot_nt(halves(sized[:, at]), dyp.astype(BF))
                decayed = []
                for n in range(2):
                    h = 2 * pair + n
                    across = row[group, h : h + 1, rows] - col[1, rows, h : h + 1]
                    decay = jnp.exp(jnp.minimum(across, biast_ref[c]))
                    decayed.append((cross * decay).astype(BF))
                    pairs_total = pairs_total + products[n * CH : (n + 1) * CH] * decay
                parts.append(dot_nn(jnp.concatenate(decayed, axis=1), halves(dyp)))
            dgt[c] += pairs_total
            within = jnp.concatenate(parts, axis=1)
            whole = within + later
            lowered = sized.astype(BF).astype(F32) * within
            sd[rows, :] += dot_nn(split2(whole * x), collector)
            sp[rows, :] -= dot_nn(split2(lowered), collector)
            sq[rows, :] += dot_nn(split2(sized * later), collector)
            dxd[rows, :] = (whole * steps + gp[6:7] * dy) * fs[slot, rows, :]
        for step in reversed(range(1, bits + 1)):
            advance(group - step, step, phase)
        ends.append(jnp.zeros((8 - chunks, GC), F32))
        se[...] += dot_nn(split2(jnp.concatenate(ends, axis=0)), collector)
        wide, sums = conv_back(
            dxd[...], lambda k: valb_ref[0, pl.ds(HALO - k, tokens), :], keep_ref, gp, tokens
        )
        small_ref[layer, pl.ds(group * 8, 8), :] += jnp.concatenate(sums + [jnp.zeros((3, GC), F32)], axis=0)
        wide = wide.astype(BF)
        dgate = dgs[slot]
        shape = place.dims + (-1, GC)
        own[(group,) + place.all + (0,)] = dot_nn(nxt[...], dgate).astype(BF).reshape(shape)
        own[(group,) + place.all + (1,)] = (
            (dot_nn(nxt[...], wide[HALO:]) + dot_nn(nht[...], wide[:HALO])).astype(BF).reshape(shape)
        )
        advance(group, 0, phase)
        back_wide = dot_nt(wide, in_weights(1))
        gnorm[...] += back_wide[:HALO]
        gx_ref[...] += back_wide[HALO:] + dot_nt(dgate, in_weights(0))

    @pl.when(i == groups + skew - 1)
    def _():
        for turn in range(LAYERS):

            @pl.when(phase == turn)
            def _(turn=turn):
                for copy in load(line_refs[LAYERS - 1 - turn], mid_ref if turn else g_ref):
                    copy.start()
                pltpu.make_async_copy(weights[LAYERS - 1 - turn][4], own_m, next_sem).start()

        upper = (iota2((CH, CH), 0) <= iota2((CH, CH), 1)).astype(F32)
        before = (iota2((CH, CH), 0) > iota2((CH, CH), 1)).astype(F32)
        raw, steps, rates, _, _, _, _ = step_terms(step_ref[...], heads_ref, carried_ref, tail_ref, kept_ref, tokens)
        drates, dmaps = [], []
        for c in range(chunks):
            rows = slice(c * CH, (c + 1) * CH)
            drates.append(dot_nn(upper, sp[rows, :], HI) + dot_nn(before, sq[rows, :], HI) + se[c : c + 1])
            low = dgt[c].astype(BF)
            into = dbt[c] + dot_nn(low, outb[c])
            out = dct[c] + dot_tn(low, inb[c])
            dmaps.append(jnp.concatenate([into, out], axis=1))
        drate = jnp.concatenate(drates, axis=0)
        dstep = (sd[...] - drate * heads_ref[1:2]) * sigmoid(raw)
        head_sums = jnp.concatenate(
            [jnp.sum(dstep, axis=0, keepdims=True), jnp.sum(drate * rates, axis=0, keepdims=True)], axis=1
        )
        mixed = shared_conv()
        part = sigmoid(mixed)
        dmixed = jnp.concatenate(dmaps, axis=0) * (part + mixed * part * (1.0 - part))
        wide, sums = conv_back(dmixed, lambda k: shared_ref[pl.ds(HALO - k, tokens), :], keep_ref, taps(), tokens)
        small_ref[layer, pl.ds(groups * 8, 8), :] = jnp.concatenate(sums + [jnp.zeros((3, 2 * STATE), F32)], axis=0)
        wide = wide.astype(BF)
        dstep = dstep.astype(BF)
        pltpu.make_async_copy(weights[0][4], own_m, next_sem).wait()
        back_wide = dot_nt(wide, own_m[..., : 2 * STATE].reshape(depth, 2 * STATE))
        gnorm[...] += back_wide[:HALO]

        @pl.when(z > 0)
        def _():
            halo_copy().start()

        gx_ref[...] += back_wide[HALO:] + dot_nt(dstep, own_m[..., 2 * STATE :].reshape(depth, LANES))
        at_end = phase == LAYERS - 1

        @pl.when(at_end)
        def _():
            drain(1, LAYERS - 1)

        misc = jnp.concatenate(
            [dot_nn(nxt[...], wide[HALO:]) + dot_nn(nht[...], wide[:HALO]), dot_nn(nxt[...], dstep)], axis=1
        )
        own_m[...] = misc.astype(BF).reshape(own_m.shape)
        misc_advance(0, phase)

        @pl.when(z < pieces - 1)
        def _():
            halo_copy().wait_recv()
            gx_ref[pl.ds(tokens - HALO, HALO), :] += hrecv[phase]

        for copy in load(line_refs[0], g_ref):
            copy.wait()
        blocks = [(k, slice(k * GC, (k + 1) * GC)) for k in range(depth // GC)]
        gain = gain_ref[pl.ds(layer, 1), :]
        power = inside = jnp.zeros((tokens, 1), F32)
        for k, cols in blocks:
            power = power + jnp.sum(xs[k] * xs[k], axis=1, keepdims=True)
            gained = gx_ref[:, cols] * gain[:, cols]
            inside = inside + jnp.sum(gained * xs[k], axis=1, keepdims=True)
        q = lax.rsqrt(power * (1.0 / depth) + EPS)
        inside = inside * (q * q * q) * (1.0 / depth)
        cuts = [jnp.sum(gx_ref[:, cols] * xs[k] * q, axis=0, keepdims=True) for k, cols in blocks]
        few_total[0, pl.ds(0, groups * 8 + 8), :] = small_ref[layer, pl.ds(0, groups * 8 + 8), :]
        few_total[0, pl.ds(groups * 8 + 8, 8), :] = jnp.concatenate(
            cuts + [head_sums, jnp.zeros((7 - len(cuts), GC), F32)], axis=0
        )
        few_advance(0, phase)
        for k, cols in blocks:
            gx_ref[:, cols] = fs[k] + q * (gx_ref[:, cols] * gain[:, cols]) - xs[k] * inside

        @pl.when(z > 0)
        def _():
            halo_copy().wait_send()
            for group in range(groups):
                state_copy(group).wait_send()

        @pl.when(at_end)
        def _():
            turn = LAYERS - 1
            misc_advance(1, turn)
            for step in range(2, bits + 1):
                drain(step, turn)
                few_advance(step - 1, turn)
                misc_advance(step, turn)
            few_advance(bits, turn)
            finish_few(turn)
            for group in range(groups):
                finish_group(jnp.int32(group), turn)


def whole(shape):
    return pl.BlockSpec(shape, lambda i: (0,) * len(shape), pipeline_mode=pl.Buffered(1))


def quarter(group, half, pieces):
    at = lax.rem(group, pieces // 2) if pieces > 2 else 0 * group
    return pieces - 1 - at if half else at


def group_specs(dims, wall):
    pieces, groups, _, skew = dims
    dp, _, _, share, _ = wall
    last = groups - 1

    def early(i):
        return jnp.minimum(i, last)

    def late(i):
        return jnp.maximum(i - skew, 0)

    def block(rows, at):
        return pl.BlockSpec((1, rows, GC), lambda i: (at(i), 0, 0))

    def both(make):
        return [make(0), make(1)]

    def column(i, at):
        return lax.div(at(i), pieces // 2)

    def pair(at):
        return both(
            lambda half: pl.BlockSpec(
                (dp, 1, 2, share, LANES), lambda i: (0, quarter(at(i), half, pieces), 0, 0, column(i, at))
            )
        )

    def single(at):
        return both(
            lambda half: pl.BlockSpec(
                (dp, 1, 1, share, LANES), lambda i: (0, quarter(at(i), half, pieces), 2, 0, column(i, at))
            )
        )

    def params(layer, at):
        return both(
            lambda half: pl.BlockSpec(
                (1, 1, 8, LANES), lambda i: (quarter(at(i), half, pieces), layer, 0, column(i, at))
            )
        )

    return early, late, block, pair, single, params


def side(refs, n):
    rows = refs[0].shape[0] * refs[0].shape[3]
    return jnp.concatenate([ref[:, 0, n].reshape(rows, LANES) for ref in refs], axis=1)


def side_params(refs):
    return jnp.concatenate([ref[0, 0] for ref in refs], axis=1)


def fixed(shape, place):
    return pl.BlockSpec(shape, lambda i: place, pipeline_mode=pl.Buffered(1))


def layer_forward(dims, bits, layer, x, gain, w, few, pack, csw, csb, masks, later, earlier):
    pieces, groups, tokens, skew = dims
    keep, bias, _, carried, tail, kept = masks
    chunks = tokens // CH
    depth = x.shape[1]
    ext = tokens + HALO
    slots = skew + 1
    early, late, _, pair, single, params = group_specs(dims, w.shape)

    def block(rows, at):
        return pl.BlockSpec((None, 1, rows, GC), lambda i: (layer, at(i), 0, 0))

    def mine(shape):
        return fixed((None,) + shape, (layer,) + (0,) * len(shape))

    anywhere = pl.BlockSpec(memory_space=pl.ANY)
    near = pl.BlockSpec(memory_space=pltpu.VMEM)
    gathers = later is not None
    cut = (2,) * bits
    buffers, sems = plane_scratch(pieces, bits, w.shape[3])
    if gathers:
        later_few, later = later
    first = 19 + 2 * gathers
    aliases = {first + k: 1 + k for k in range(len(earlier))}
    if gathers:
        aliases[20] = 11
    return pl.pallas_call(
        partial(forward_kernel, dims + (bits, layer, gathers)),
        grid=(groups + skew,),
        in_specs=[
            whole((tokens, depth)), whole(gain.shape), *pair(early), *single(late),
            whole(few.shape), *params(layer, early), *params(layer, late), fixed((pieces, 1, 8, 2 * LANES), (0, layer, 0, 0)),
            whole(csw.shape), whole(csb.shape),
            whole(keep.shape), whole(bias.shape), whole(carried.shape), whole(tail.shape), whole(kept.shape),
        ] + [near, anywhere] * gathers + [anywhere] * len(earlier),
        out_specs=[
            whole((tokens, depth)), mine((depth, tokens)), mine((depth, HALO)),
            block(tokens, early), block(ext, early), block(tokens, late),
            pl.BlockSpec((None, 1, chunks, STATE, GC), lambda i: (layer, late(i), 0, 0, 0)),
            mine((ext, 2 * STATE)), mine((tokens, LANES)), mine((tokens, LANES)),
        ] + [near, anywhere] * gathers,
        out_shape=[
            jax.ShapeDtypeStruct((tokens, depth), F32),
            jax.ShapeDtypeStruct((LAYERS, depth, tokens), BF),
            jax.ShapeDtypeStruct((LAYERS, depth, HALO), BF),
            jax.ShapeDtypeStruct((LAYERS, groups, tokens, GC), F32),
            jax.ShapeDtypeStruct((LAYERS, groups, ext, GC), F32),
            jax.ShapeDtypeStruct((LAYERS, groups, tokens, GC), F32),
            jax.ShapeDtypeStruct((LAYERS, groups, chunks, STATE, GC), BF),
            jax.ShapeDtypeStruct((LAYERS, ext, 2 * STATE), F32),
            jax.ShapeDtypeStruct((LAYERS, tokens, LANES), F32),
            jax.ShapeDtypeStruct((LAYERS, tokens, LANES), F32),
        ] + (
            [jax.ShapeDtypeStruct(cut + later_few.shape, BF), jax.ShapeDtypeStruct(later.shape, BF)]
            if gathers
            else []
        ),
        scratch_shapes=[
            pltpu.VMEM((ext, depth), BF),
            pltpu.VMEM((chunks, CH, STATE), BF),
            pltpu.VMEM((chunks, STATE, CH), BF),
            pltpu.VMEM((chunks, CH, STATE), BF),
            pltpu.VMEM((chunks, CH, CH), F32),
            pltpu.VMEM((2, tokens, LANES), F32),
            pltpu.VMEM((groups, 8, tokens), F32),
            pltpu.VMEM((3, tokens, 2 * LANES), BF),
            pltpu.VMEM((groups, 8, GC), F32),
            pltpu.VMEM((slots, tokens, GC), F32),
            pltpu.VMEM((slots, tokens, GC), F32),
            pltpu.VMEM((slots, tokens, GC), F32),
            pltpu.VMEM((slots, chunks, STATE, GC), F32),
            pltpu.VMEM((slots, STATE, GC), F32),
            pltpu.VMEM((groups, STATE, GC), BF),
            pltpu.VMEM((groups, STATE, GC), BF),
            pltpu.VMEM((tokens, depth), F32),
            pltpu.VMEM((tokens, LANES), F32),
            pltpu.VMEM((8, LANES), F32),
            pltpu.SemaphoreType.DMA,
            pltpu.SemaphoreType.DMA,
            pltpu.SemaphoreType.DMA((groups,)),
            pltpu.SemaphoreType.DMA((groups,)),
        ] + (buffers + sems if gathers else []),
        input_output_aliases=aliases,
        compiler_params=pltpu.CompilerParams(
            collective_id=layer, has_side_effects=True, vmem_limit_bytes=VMEM_LIMIT_FORWARD,
            dimension_semantics=("arbitrary",),
        ),
        name="layer_forward",
    )(
        x, gain, w, w, w, w, few, pack, pack, pack, pack, pack, csw, csb, keep, bias, carried, tail, kept,
        *([later_few, later] if gathers else []), *earlier,
    )


def layers_backward(dims, bits, g, line, gain, saved, weights, pack, csw, csb, masks):
    pieces, groups, tokens, skew = dims
    keep, _, biast, carried, tail, kept = masks
    nxt, nht, gate, val, y, states, shared, step_in, r = saved
    anywhere = pl.BlockSpec(memory_space=pl.ANY)
    chunks = tokens // CH
    depth = g.shape[1]
    wall = weights[0][0]
    _, _, _, share, wide = wall.shape
    ext = tokens + HALO
    slots = max(skew + 1, depth // GC)
    few_shape = (groups * 8 + 16, GC)
    halves_of = [(2,) * (bits - 1 - step) for step in range(bits)]
    steps = groups + skew
    early, late, *_ = group_specs(dims, wall.shape)

    def in_turn(layer, at):
        turn = LAYERS - 1 - layer
        return lambda ph, i: at(jnp.where(ph == turn, i, jnp.where(ph < turn, 0, steps - 1)))

    def block(rows, at):
        return pl.BlockSpec((None, 1, rows, GC), lambda ph, i: (LAYERS - 1 - ph, at(i), 0, 0))

    def of_layer(v):
        return pl.BlockSpec(
            (None,) + v.shape[1:], lambda ph, i: (LAYERS - 1 - ph,) + (0,) * (v.ndim - 1),
            pipeline_mode=pl.Buffered(1),
        )

    def weight_blocks(count, first, at):
        def spec(half):
            def place(ph, i):
                group = at(ph, i)
                return 0, quarter(group, half, pieces), first, 0, lax.div(group, pieces // 2)

            return pl.BlockSpec((wall.shape[0], 1, count, share, LANES), place)

        return [spec(half) for half in range(2)]

    def group_params(at):
        def spec(half):
            def place(ph, i):
                group = at(i)
                return quarter(group, half, pieces), LAYERS - 1 - ph, 0, lax.div(group, pieces // 2)

            return pl.BlockSpec((1, 1, 8, LANES), place)

        return [spec(half) for half in range(2)]

    def whole(shape):
        return pl.BlockSpec(shape, lambda ph, i: (0,) * len(shape), pipeline_mode=pl.Buffered(1))

    weight_specs, weight_args = [], []
    for layer in range(LAYERS):
        w, few = weights[layer]
        weight_specs += weight_blocks(2, 0, in_turn(layer, late)) + weight_blocks(1, 2, in_turn(layer, early)) + [anywhere]
        weight_args += [w, w, w, w, few]
    return pl.pallas_call(
        partial(backward_kernel, dims + (bits,)),
        grid=(LAYERS, steps),
        in_specs=[anywhere] * (LAYERS + 2) + weight_specs + [
            whole(gain.shape), of_layer(nxt), of_layer(nht), of_layer(r),
            *group_params(early), *group_params(late),
            pl.BlockSpec((pieces, 1, 8, 2 * LANES), lambda ph, i: (0, LAYERS - 1 - ph, 0, 0)),
            whole(csw.shape), whole(csb.shape),
            whole(keep.shape), whole(biast.shape), whole(carried.shape), whole(tail.shape), whole(kept.shape),
            block(tokens, early), block(ext, early), block(tokens, early), block(ext, late),
            pl.BlockSpec((None, 1, chunks, STATE, GC), lambda ph, i: (LAYERS - 1 - ph, late(i), 0, 0, 0)),
            of_layer(shared), of_layer(step_in),
        ],
        out_specs=[
            whole((tokens, depth)), whole((LAYERS, 3, share, wide)), whole((LAYERS, share, 2 * STATE + LANES)),
            whole((LAYERS,) + few_shape), anywhere,
        ],
        out_shape=[
            jax.ShapeDtypeStruct((tokens, depth), F32),
            jax.ShapeDtypeStruct((LAYERS, 3, share, wide), F32),
            jax.ShapeDtypeStruct((LAYERS, share, 2 * STATE + LANES), F32),
            jax.ShapeDtypeStruct((LAYERS,) + few_shape, F32),
            jax.ShapeDtypeStruct((tokens, depth), F32),
        ],
        scratch_shapes=[
            pltpu.VMEM((tokens, depth), BF),
            pltpu.VMEM((depth, tokens), BF),
            pltpu.VMEM((tokens, LANES), F32),
            pltpu.VMEM((chunks, CH, STATE), BF),
            pltpu.VMEM((chunks, CH, STATE), BF),
            pltpu.VMEM((chunks, STATE, CH), BF),
            pltpu.VMEM((chunks, CH, CH), F32),
            pltpu.VMEM((2, tokens, LANES), F32),
            pltpu.VMEM((groups, 8, tokens), F32),
            pltpu.VMEM((3, tokens, 2 * LANES), BF),
            pltpu.VMEM((groups, 8, GC), F32),
            pltpu.VMEM((slots, tokens, GC), BF),
            pltpu.VMEM((slots, tokens, GC), F32),
            pltpu.VMEM((slots, tokens, GC), F32),
            pltpu.VMEM((slots, tokens, GC), BF),
            pltpu.VMEM((slots, STATE, GC), F32),
            pltpu.VMEM((LAYERS, groups, STATE, GC), BF),
            pltpu.VMEM((groups, STATE, GC), BF),
            pltpu.VMEM((HALO, depth), F32),
            pltpu.VMEM((chunks, CH, STATE), F32),
            pltpu.VMEM((chunks, CH, STATE), F32),
            pltpu.VMEM((chunks, CH, CH), F32),
            pltpu.VMEM((tokens, LANES), F32),
            pltpu.VMEM((tokens, LANES), F32),
            pltpu.VMEM((tokens, LANES), F32),
            pltpu.VMEM((8, LANES), F32),
            pltpu.VMEM((tokens, GC), F32),
            pltpu.VMEM((LAYERS, HALO, depth), F32),
            pltpu.VMEM((groups,) + (2,) * bits + (3, share, GC), BF),
            pltpu.VMEM((2,) * bits + (share, 2 * STATE + LANES), BF),
            pltpu.VMEM((LAYERS, pieces, 2 * groups // pieces, 3, share, LANES), BF),
            pltpu.VMEM((LAYERS, pieces, share, 2 * STATE + LANES), BF),
            pltpu.SemaphoreType.DMA,
            pltpu.SemaphoreType.DMA((LAYERS,)),
            pltpu.SemaphoreType.DMA((groups,)),
            pltpu.SemaphoreType.DMA((LAYERS, groups)),
            pltpu.SemaphoreType.DMA((groups, bits, 2)),
            pltpu.SemaphoreType.DMA((groups, bits, 2)),
            pltpu.SemaphoreType.DMA((groups, 2)),
            pltpu.SemaphoreType.DMA((LAYERS, pieces, 2 * groups // pieces)),
            pltpu.SemaphoreType.DMA((bits,)),
            pltpu.SemaphoreType.DMA((bits,)),
            pltpu.SemaphoreType.DMA((pieces,)),
            pltpu.SemaphoreType.DMA((LAYERS, pieces)),
            pltpu.SemaphoreType.DMA,
            pltpu.SemaphoreType.DMA((2, depth // GC)),
            pltpu.VMEM((8, LANES), F32),
            pltpu.VMEM((bits + 1,) + few_shape, F32),
            pltpu.VMEM((bits,) + few_shape, F32),
            pltpu.VMEM((LAYERS, pieces) + few_shape, F32),
            pltpu.SemaphoreType.DMA((bits,)),
            pltpu.SemaphoreType.DMA((bits,)),
            pltpu.SemaphoreType.DMA((pieces,)),
            pltpu.SemaphoreType.DMA((LAYERS, pieces)),
            *[pltpu.VMEM((SLOTS,) + dims_left + (3, share, GC), BF) for dims_left in halves_of],
            *[pltpu.VMEM(dims_left + (share, 2 * STATE + LANES), BF) for dims_left in halves_of],
        ],
        compiler_params=pltpu.CompilerParams(
            collective_id=3, has_side_effects=True, vmem_limit_bytes=VMEM_LIMIT, dimension_semantics=("arbitrary", "arbitrary")
        ),
        name="layers_backward",
    )(
        g, *line, *weight_args, gain, nxt, nht, r, pack, pack, pack, pack, pack, csw, csb, keep, biast, carried, tail,
        kept, gate, val, y, val, states, shared, step_in,
    )


def near_first(z, pieces):
    table = [sorted(range(pieces), key=lambda k: (abs(k - at), k > at)) for at in range(pieces)]
    return [sum(jnp.where(z == at, table[at][p], 0) for at in range(pieces)) for p in range(pieces)]


class Line:
    def __init__(self, place, z, pieces, mine, wall, own_sem, z_send, z_recv):
        self.place, self.z, self.pieces, self.mine, self.wall = place, z, pieces, mine, wall
        self.z_send, self.z_recv = z_send, z_recv
        self.order = near_first(z, pieces)
        self.own = pltpu.make_async_copy(mine, wall.at[place.mine() + (z,)], own_sem)

    def z_copy(self, zi, up):
        src = self.mine if zi is self.z else self.wall.at[self.place.mine() + (zi,)]
        return pltpu.make_async_remote_copy(
            src_ref=src, dst_ref=self.wall.at[self.place.mine() + (zi,)], send_sem=self.z_send.at[int(up), zi],
            recv_sem=self.z_recv.at[zi], device_id={"tensor": self.z + (1 if up else -1)}, device_id_type=MESH,
        )

    def pass_on(self, zi, act):
        z, last = self.z, self.pieces - 1

        @pl.when(jnp.logical_and(zi <= z, z < last))
        def _():
            act(self.z_copy(zi, True))

        @pl.when(jnp.logical_and(zi >= z, z > 0))
        def _():
            act(self.z_copy(zi, False))

    def start(self):
        self.pass_on(self.z, lambda copy: copy.start())
        self.own.start()

    def arrive(self, p):
        zi = self.order[p]
        pltpu.make_async_remote_copy(
            src_ref=self.mine, dst_ref=self.wall.at[self.place.mine() + (zi,)], send_sem=self.z_send.at[0, zi],
            recv_sem=self.z_recv.at[zi], device_id={"tensor": zi}, device_id_type=MESH,
        ).wait_recv()
        self.pass_on(zi, lambda copy: copy.start())

    def finish(self):
        for p in range(self.pieces):
            self.pass_on(self.order[p], lambda copy: copy.wait_send())


class Plane:
    def __init__(self, place, z, pieces, mine, wall, few, few_z, few_all, *sems):
        self.place, self.z, self.pieces, self.bits = place, z, pieces, place.bits
        self.mine, self.wall, self.few, self.few_z, self.few_all = mine, wall, few, few_z, few_all
        self.d_send, self.d_recv, self.t_send, self.t_recv, self.f_send, self.f_recv = sems
        wide = wall.shape[-1]
        self.cols = [pl.ds(0, wide // 2), pl.ds(wide // 2, wide // 2)]
        self.few_cols = [pl.ds(0, 2 * STATE), pl.ds(2 * STATE, LANES)]
        self.order = near_first(z, pieces)
        rest = list(range(1, self.bits))
        self.paths = [rest + [0], rest[::-1] + [0]]

    def d_copy(self, p, half, step):
        path = self.paths[half]
        cols = (slice(None), slice(None), self.cols[half])
        ref = self.wall.at[self.place.along(path[:step]) + (self.order[p],) + cols]
        return pltpu.make_async_remote_copy(
            src_ref=self.mine.at[cols] if self.mine is not None and p + step == 0 else ref, dst_ref=ref,
            send_sem=self.d_send.at[p, half, step], recv_sem=self.d_recv.at[p, half, step],
            device_id={"dp": self.place.flip(path[step])}, device_id_type=MESH,
        )

    def line_copy(self, k):
        return pltpu.make_async_remote_copy(
            src_ref=self.few.at[:, self.few_cols[1]], dst_ref=self.few_z.at[self.z], send_sem=self.t_send.at[k],
            recv_sem=self.t_recv.at[k], device_id={"tensor": lax.rem(self.z + k, self.pieces)}, device_id_type=MESH,
        )

    def few_copy(self, half, step):
        path = self.paths[half]
        ref = self.few_all.at[self.place.along(path[:step]) + (slice(None), self.few_cols[half])]
        return pltpu.make_async_remote_copy(
            src_ref=ref, dst_ref=ref, send_sem=self.f_send.at[half, step], recv_sem=self.f_recv.at[half, step],
            device_id={"dp": self.place.flip(path[step])}, device_id_type=MESH,
        )

    def few_event(self, step):
        if step == 0:
            total = self.few[:, self.few_cols[1]]
            for k in range(1, self.pieces):
                self.line_copy(k).wait_recv()
                total = total + self.few_z[lax.rem(self.z + self.pieces - k, self.pieces)]
            self.few_all[self.place.mine()] = jnp.concatenate([self.few[:, self.few_cols[0]], total], axis=1)
        for half in range(2):
            if step:
                self.few_copy(half, step - 1).wait_recv()
            if step < self.bits:
                self.few_copy(half, step).start()

    def start(self, p):
        for half in range(2):
            self.d_copy(p, half, 0).start()

    def start_few(self):
        for k in range(1, self.pieces):
            self.line_copy(k).start()

    def double(self, p, step):
        for half in range(2):
            self.d_copy(p, half, step - 1).wait_recv()
            if step < self.bits:
                self.d_copy(p, half, step).start()

    def finish(self):
        for p in range(self.pieces):
            for half in range(2):
                for step in range(self.bits):
                    self.d_copy(p, half, step).wait_send()
        for k in range(1, self.pieces):
            self.line_copy(k).wait_send()
        for half in range(2):
            for step in range(self.bits):
                self.few_copy(half, step).wait_send()


def greet(place, z, pieces):
    barrier = pltpu.get_barrier_semaphore()
    for b in range(place.bits):
        pl.semaphore_signal(barrier, inc=1, device_id={"dp": place.flip(b)}, device_id_type=MESH)
    for k in range(1, pieces):
        pl.semaphore_signal(barrier, inc=1, device_id={"tensor": lax.rem(z + k, pieces)}, device_id_type=MESH)
    pl.semaphore_wait(barrier, place.bits + pieces - 1)


def write_masks(z, tokens, starts_ref, keep_ref, bias_ref, biast_ref, carried_ref, tail_ref, kept_ref):
    first = z * tokens

    def label(position):
        total = None
        for k in range(starts_ref.shape[1]):
            term = jnp.where(position >= starts_ref[0, k], 1.0, 0.0)
            total = term if total is None else total + term
        return total

    def same(a, b):
        return jnp.where(a == b, 1.0, 0.0)

    for c in range(tokens // CH):
        begin = first + c * CH
        down = iota2((CH, LANES), 0) + begin
        across = iota2((CH, LANES), 1) + begin
        own, other = label(down), label(across)
        rows = pl.ds(c * CH, CH)
        for k in range(1, 4):
            keep_ref[k - 1, rows, :] = same(label(down - k), own)
        equal = own == other
        bias_ref[c] = jnp.where(equal, jnp.where(down >= across, 0.0, NEG), NEG)
        biast_ref[c] = jnp.where(equal, jnp.where(down <= across, 0.0, NEG), NEG)
        flat = jnp.zeros((CH, LANES), jnp.int32) + begin
        before, final = label(flat - 1), label(flat + (CH - 1))
        carried_ref[rows, :] = same(own, before)
        tail_ref[rows, :] = same(own, final)
        kept_ref[pl.ds(c, 1), :] = same(final, before)[:1]
    kept_ref[pl.ds(tokens // CH, 8 - tokens // CH), :] = jnp.zeros((8 - tokens // CH, LANES), F32)


def gather_kernel(
    dims, starts, tokens_ref, cotangent_ref, cvw, cvb, gate_gain, skip, bias_in, decay, bc, dt, mine, later,
    wall, wall_later, x_all, g_all, few_out, few_later, pack_out, keep, bias, biast, carried, tail, kept,
    x_wide, g_wide, pack, pack_all, few, few_z, few_all, wide_sem, pk_send, pk_recv, *sems,
):
    pieces, tokens, bits = dims
    place = Place(bits)
    z = lax.axis_index("tensor")
    greet(place, z, pieces)
    line = Line(place, z, pieces, mine, wall, *sems[:3])
    line_later = Line(place, z, pieces, later, wall_later, *sems[3:6])
    plane = Plane(place, z, pieces, mine, wall, few, few_z, few_all, *sems[6:])

    heads = skip.shape[1]
    upper_half = z >= pieces // 2
    first = HG * jnp.where(upper_half, pieces - 1 - z, z) + jnp.where(upper_half, HG // 2, 0)

    def lane_of(head):
        return first + HG * (pieces // 2) * (head // 2) + head % 2

    def spot(ref, layer):
        lane = iota2((1, LANES), 1)
        total = jnp.zeros((1, LANES), F32)
        for head in range(heads):
            total = jnp.where(lane == lane_of(head), ref[layer : layer + 1, head : head + 1], total)
        return total

    low, high = iota2((heads, LANES), 0), iota2((heads, LANES), 1)
    chosen = (lane_of(0) + HG * (pieces // 2) * (low // 2) + low % 2 == high).astype(F32).astype(BF)
    for layer in range(LAYERS):
        wide = jnp.concatenate([bc[layer], dot_nn(dt[layer], chosen).astype(BF)], axis=1)
        if layer == 0:
            few[...] = wide
        else:
            few_later[...] = wide
    plane.start(0)
    line.start()
    plane.start_few()
    channel = iota2((1, cvb.shape[1]), 1) // HD
    for layer in range(LAYERS):
        skips = jnp.zeros(channel.shape, F32)
        for head in range(heads):
            skips = jnp.where(channel == head, skip[layer : layer + 1, head : head + 1], skips)
        own = slice(layer, layer + 1)
        rest = jnp.zeros((1, cvb.shape[1] - 2 * LANES), F32)
        tail_row = jnp.concatenate([spot(bias_in, layer), spot(decay, layer), rest], axis=1)
        pack[layer] = jnp.concatenate([cvw[layer], cvb[own], gate_gain[own], skips, tail_row], axis=0)

    def pack_copy(k):
        return pltpu.make_async_remote_copy(
            src_ref=pack, dst_ref=pack_all.at[z], send_sem=pk_send.at[k], recv_sem=pk_recv.at[k],
            device_id={"tensor": lax.rem(z + k, pieces)}, device_id_type=MESH,
        )

    for k in range(1, pieces):
        pack_copy(k).start()
    pack_all[z] = pack[...]
    wides = []
    for k, (narrow, wide, out) in enumerate(((tokens_ref, x_wide, x_all), (cotangent_ref, g_wide, g_all))):
        wide[...] = narrow[...].astype(F32)
        wides.append(pltpu.make_async_copy(wide, out, wide_sem.at[k]))
        wides[k].start()
    write_masks(z, tokens, starts, keep, bias, biast, carried, tail, kept)

    def arrive(p):
        line.arrive(p)
        plane.start(p)
        if p == min(2, pieces - 1):
            line_later.start()

    def double(p, step):
        if p == 0 and step == 1:
            line.own.wait()
        plane.double(p, step)

    events = []
    for p in range(pieces):
        if p:
            events.append((10.0 * p, partial(arrive, p)))
            events.append((10.0 * (2 + p) + 5.0, partial(line_later.arrive, p)))
        for step in range(1, bits + 1):
            late = 0.0 if step < bits - 1 else 0.8
            events.append((10.0 * p + 9.5 * step + late, partial(double, p, step)))
    for step in range(bits + 1):
        events.append((5.0 + 8.0 * step, partial(plane.few_event, step)))
    for _, act in sorted(events, key=lambda event: event[0]):
        act()
    line_later.own.wait()
    line.finish()
    line_later.finish()
    plane.finish()
    for copy in wides:
        copy.wait()
    for k in range(1, pieces):
        pack_copy(k).wait()
    few_out[...] = few_all[...]
    pack_out[...] = pack_all[...]


def line_sems(pieces):
    dma = pltpu.SemaphoreType.DMA
    return [dma, dma((2, pieces)), dma((pieces,))]


def plane_scratch(pieces, bits, share):
    dma = pltpu.SemaphoreType.DMA
    return [pltpu.VMEM((pieces, share, LANES), BF), pltpu.VMEM((2,) * bits + (share, 2 * STATE + LANES), BF)], [
        dma((pieces, 2, bits)), dma((pieces, 2, bits)), dma((pieces,)), dma((pieces,)), dma((2, bits)), dma((2, bits)),
    ]


def gather_first(dims, starts, x, g, params, bc, dt, share, later):
    pieces, tokens, bits = dims
    cut = (2,) * bits
    chunks = tokens // CH
    dma = pltpu.SemaphoreType.DMA
    anywhere = pl.BlockSpec(memory_space=pl.ANY)
    near = pl.BlockSpec(memory_space=pltpu.VMEM)
    buffers, sems = plane_scratch(pieces, bits, share.shape[1])
    pack = (LAYERS, 8, params[1].shape[1])
    few = (share.shape[1], 2 * STATE + LANES)
    return pl.pallas_call(
        partial(gather_kernel, dims),
        in_specs=[pl.BlockSpec(memory_space=pltpu.SMEM)] + [near] * 10 + [anywhere] * 2,
        out_specs=[anywhere] * 4 + [near] * 9,
        out_shape=[
            jax.ShapeDtypeStruct(cut + (pieces,) + share.shape, BF),
            jax.ShapeDtypeStruct(cut + (pieces,) + share.shape, BF),
            jax.ShapeDtypeStruct(x.shape, F32),
            jax.ShapeDtypeStruct(g.shape, F32),
            jax.ShapeDtypeStruct(cut + few, BF),
            jax.ShapeDtypeStruct(few, BF),
            jax.ShapeDtypeStruct((pieces,) + pack, F32),
            jax.ShapeDtypeStruct((3, tokens, LANES), F32),
            jax.ShapeDtypeStruct((chunks, CH, CH), F32),
            jax.ShapeDtypeStruct((chunks, CH, CH), F32),
            jax.ShapeDtypeStruct((tokens, LANES), F32),
            jax.ShapeDtypeStruct((tokens, LANES), F32),
            jax.ShapeDtypeStruct((8, LANES), F32),
        ],
        scratch_shapes=[
            pltpu.VMEM(x.shape, F32), pltpu.VMEM(g.shape, F32), pltpu.VMEM(pack, F32), pltpu.VMEM((pieces,) + pack, F32),
            pltpu.VMEM(few, BF),
        ] + buffers + [dma((2,)), dma((pieces,)), dma((pieces,))] + line_sems(pieces) * 2 + sems,
        compiler_params=pltpu.CompilerParams(collective_id=2, has_side_effects=True, vmem_limit_bytes=VMEM_LIMIT),
        name="gather_first",
    )(starts, x, g, *params, bc, dt, share, later)


def local(
    tokens, gate_value_weight, w_bc, w_dt, w_out, norm_gain, conv_value_w, conv_value_b, conv_shared_w, conv_shared_b,
    step_bias, decay_log, skip_gain, gate_gain, starts, cotangent,
):
    pieces, dp = lax.axis_size("tensor"), lax.axis_size("dp")
    z = lax.axis_index("tensor")
    bits = (dp - 1).bit_length()
    count, depth = tokens.shape
    own = conv_value_b.shape[1]
    few = step_bias.shape[1]
    groups = pieces * own // GC
    dims = (pieces, groups, count, pieces - 1)

    shares = [
        jnp.concatenate([jnp.swapaxes(gate_value_weight[layer], 0, 1), w_out[layer][None]], axis=0)
        for layer in range(LAYERS)
    ]
    wall, wall_later, x, grad, few_all, few_later, pack, *masks = gather_first(
        (pieces, count, bits), starts, tokens, cotangent,
        (conv_value_w, conv_value_b, gate_gain, skip_gain, step_bias, decay_log), w_bc, w_dt, *shares,
    )
    line, saved, weights = [x], [], []
    for layer in range(LAYERS):
        weights.append((wall.reshape((dp,) + wall.shape[bits:]), few_all))
        later = (few_later, wall_later) if layer + 1 < LAYERS else None
        x, *saved = layer_forward(
            dims, bits, layer, x, norm_gain, *weights[-1], pack, conv_shared_w, conv_shared_b, masks, later, saved
        )
        if later is not None:
            *saved, few_all, wall = saved
        line.append(x)
    upper_half = z >= pieces // 2
    at = jnp.where(upper_half, pieces - 1 - z, z)

    def own_heads(v):
        v = v[..., : pieces * few].reshape(v.shape[:-1] + (few // 2, pieces // 2, 2, 2))
        v = lax.dynamic_index_in_dim(v, at, axis=v.ndim - 3, keepdims=False)
        v = lax.dynamic_index_in_dim(v, upper_half.astype(jnp.int32), axis=v.ndim - 2, keepdims=False)
        return v.reshape(v.shape[:-2] + (few,))

    grad, gw, gm, small, _ = layers_backward(
        dims, bits, grad, line, norm_gain, saved, weights, pack, conv_shared_w, conv_shared_b, masks
    )
    rows = small[:, : groups * 8].reshape(LAYERS, 2 * groups // pieces, pieces // 2, 8, 2, LANES)
    rows = lax.dynamic_index_in_dim(rows, at, axis=2, keepdims=False)
    rows = lax.dynamic_index_in_dim(rows, upper_half.astype(jnp.int32), axis=3, keepdims=False)
    rows = jnp.swapaxes(rows, 1, 2).reshape(LAYERS, 8, own)
    gcs = small[:, groups * 8 : groups * 8 + 8]
    ends = small[:, groups * 8 + 8 :]
    cuts = depth // GC
    gheads = own_heads(ends[:, cuts].reshape(LAYERS, 2, LANES))
    return (
        x.astype(BF), grad, jnp.swapaxes(gw[:, :2], 1, 2), gm[:, :, : 2 * STATE], own_heads(gm[:, :, 2 * STATE :]),
        gw[:, 2], ends[:, :cuts].reshape(LAYERS, depth),
        rows[:, :4], rows[:, 4], gcs[:, :4], gcs[:, 4], gheads[:, 0], gheads[:, 1],
        jnp.sum(rows[:, 6].reshape(LAYERS, few, HD), axis=2), rows[:, 5],
    )


def solution(mesh):
    in_specs = (
        P(("dp", "tensor"), None),
        P(None, "dp", None, "tensor"),
        P(None, "dp", None),
        P(None, "dp", "tensor"),
        P(None, "dp", "tensor"),
        P(),
        P(None, None, "tensor"),
        P(None, "tensor"),
        P(),
        P(),
        P(None, "tensor"),
        P(None, "tensor"),
        P(None, "tensor"),
        P(None, "tensor"),
        P("dp", None),
        P(("dp", "tensor"), None),
    )
    out_specs = (
        P(("dp", "tensor"), None),
        P(("dp", "tensor"), None),
        P(None, "dp", None, "tensor"),
        P(None, "dp", None),
        P(None, "dp", "tensor"),
        P(None, "dp", "tensor"),
        P(),
        P(None, None, "tensor"),
        P(None, "tensor"),
        P(),
        P(),
        P(None, "tensor"),
        P(None, "tensor"),
        P(None, "tensor"),
        P(None, "tensor"),
    )
    return jax.shard_map(local, mesh=mesh, in_specs=in_specs, out_specs=out_specs, check_vma=False)
```

```python
from functools import partial

import jax
import jax.numpy as jnp
from jax import lax
from jax.experimental import pallas as pl
from jax.experimental.pallas import tpu as pltpu
from jax.sharding import PartitionSpec as P

LAYERS = 2
EPS = 1e-05
HALO = 16
CH = 128
TILE = 64
GC = 256
HD = 64
HG = GC // HD
LANES = 128
STATE = 128
NEG = -1e30
SLOTS = 2
VMEM_LIMIT = 60 * 1024 * 1024
VMEM_LIMIT_FORWARD = 62 * 1024 * 1024
MESH = pl.DeviceIdType.MESH
HI = lax.Precision.HIGHEST
F32 = jnp.float32
BF = jnp.bfloat16


def dot_nn(a, b, precision=None):
    return lax.dot_general(a, b, (((1,), (0,)), ((), ())), precision=precision, preferred_element_type=F32)


def dot_nt(a, b):
    return lax.dot_general(a, b, (((1,), (1,)), ((), ())), preferred_element_type=F32)


def dot_tn(a, b):
    return lax.dot_general(a, b, (((0,), (0,)), ((), ())), preferred_element_type=F32)


def sigmoid(v):
    return 0.5 * jnp.tanh(0.5 * v) + 0.5


def twice(v):
    return jnp.concatenate([v, v], axis=1)


def split2(v):
    high = v.astype(BF)
    return jnp.concatenate([high, (v - high.astype(F32)).astype(BF)], axis=1)


def iota2(shape, dim):
    return lax.broadcasted_iota(jnp.int32, shape, dim)


def spread(group):
    row = iota2((2 * LANES, GC), 0) % LANES
    head = iota2((2 * LANES, GC), 1) // HD + group * HG
    return (row == head).astype(F32).astype(BF)


def collect(group):
    head = (iota2((2 * GC, LANES), 0) % GC) // HD + group * HG
    return (head == iota2((2 * GC, LANES), 1)).astype(F32).astype(BF)


def conv(load, keep_ref, weights, tokens):
    return conv_rows(load, keep_ref, weights, pl.ds(0, tokens))


def conv_rows(load, keep_ref, weights, rows):
    total = weights[4:5] + weights[0:1] * load(0)
    for k in range(1, 4):
        total = total + weights[k : k + 1] * (load(k) * twice(keep_ref[k - 1, rows, :]))
    return total


def tiles(tokens):
    return range(0, tokens, TILE)


def conv_back(grad, load, keep_ref, weights, tokens):
    rows = []
    total = None
    for k in range(4):
        part = grad if k == 0 else grad * twice(keep_ref[k - 1])
        rows.append(jnp.sum(part * load(k), axis=0, keepdims=True))
        wide = jnp.concatenate([jnp.zeros((HALO, grad.shape[1]), F32), weights[k : k + 1] * part], axis=0)
        if k:
            wide = pltpu.roll(wide, tokens + HALO - k, 0)
        total = wide if total is None else total + wide
    rows.append(jnp.sum(grad, axis=0, keepdims=True))
    return total, rows


def step_terms(step_in, heads_ref, carried_ref, tail_ref, kept_ref, tokens):
    chunks = tokens // CH
    raw = step_in + heads_ref[0:1]
    steps = jnp.maximum(raw, 0.0) + jnp.log1p(jnp.exp(-jnp.abs(raw)))
    rates = -steps * heads_ref[1:2]
    lower = (iota2((CH, CH), 0) >= iota2((CH, CH), 1)).astype(F32)
    sums, toward, kept = [], [], []
    for c in range(chunks):
        summed = dot_nn(lower, rates[c * CH : (c + 1) * CH], HI)
        last = summed[CH - 1 : CH]
        sums.append(summed)
        toward.append(jnp.exp(last - summed))
        kept.append(jnp.exp(last) * kept_ref[c : c + 1])
    kept.append(jnp.zeros((8 - chunks, LANES), F32))
    summed = jnp.concatenate(sums, axis=0)
    toward = jnp.concatenate(toward, axis=0) * tail_ref[...]
    reach = jnp.exp(summed) * carried_ref[...]
    return raw, steps, rates, summed, toward, reach, jnp.concatenate(kept, axis=0)


def put_sums(summed, col_ref, row_ref, groups, tokens):
    for c in range(tokens // CH):
        turned = summed[c * CH : (c + 1) * CH].T
        for group in range(groups):
            row_ref[group, 0:HG, c * CH : (c + 1) * CH] = turned[group * HG : (group + 1) * HG]
    col_ref[0] = summed


def turn_sums(col_ref, group):
    col_ref[1] = pltpu.roll(col_ref[0], lax.rem(LANES - group * HG, LANES), 1)


def put_heads(rows_ref, heads_ref):
    total = rows_ref[0, 0, 7:8, :]
    for k in range(1, rows_ref.shape[0]):
        total = total + rows_ref[k, 0, 7:8, :]
    heads_ref[...] = jnp.concatenate(
        [total[:, :LANES], jnp.exp(total[:, LANES:]), jnp.zeros((6, LANES), F32)], axis=0
    )


def shared_taps(csw_ref, csb_ref, layer):
    return jnp.concatenate([csw_ref[layer], csb_ref[layer : layer + 1]], axis=0)


def halves(v):
    first = iota2(v.shape, 1) < HD
    return jnp.concatenate([jnp.where(first, v, 0.0), jnp.where(first, 0.0, v)], axis=0).astype(BF)


def forward_kernel(
    dims,
    x_ref, gain_ref, wa, wb, oa, ob, few_ref, pa, pb, qa, qb, rows_ref, csw_ref, csb_ref,
    keep_ref, bias_ref, carried_ref, tail_ref, kept_ref, *rest,
):
    pieces, groups, tokens, skew, bits, layer, gathers = dims
    if gathers:
        few_mine, _, *rest = rest
    if layer:
        rest = rest[9:]
    next_ref, nxt_ref, nht_ref, gate_ref, val_ref, y_ref, state_ref, shared_ref, step_ref, r_ref, *rest = rest
    if gathers:
        few_out, wall_ref, *rest = rest
    nx, inb, inbt, outb, cross, col, row, terms, ke, intra, xs, gs, fresh, fold, *rest = rest
    incoming, outgoing, branch, squares, heads_ref, halo_send, halo_recv, send, recv, *rest = rest
    if gathers:
        few_z, few_all, *rest = rest
    place = Place(bits)
    chunks = tokens // CH
    i = pl.program_id(0)
    z = lax.axis_index("tensor")
    right, left = jnp.minimum(z + 1, pieces - 1), jnp.maximum(z - 1, 0)

    def halo_copy():
        return pltpu.make_async_remote_copy(
            src_ref=nx.at[pl.ds(tokens, HALO)], dst_ref=nx.at[pl.ds(0, HALO)],
            send_sem=halo_send, recv_sem=halo_recv, device_id={"tensor": right}, device_id_type=MESH,
        )

    def state_copy(group):
        return pltpu.make_async_remote_copy(
            src_ref=outgoing.at[group], dst_ref=incoming.at[group],
            send_sem=send.at[group], recv_sem=recv.at[group], device_id={"tensor": right}, device_id_type=MESH,
        )

    plan = [[] for _ in range(groups + skew)]
    if gathers:
        plane = Plane(place, z, pieces, None, wall_ref, few_mine, few_z, few_all, *rest)
        for step in range(1, bits + 1):
            for p in range(pieces):
                plan[min(4 * step + p - 2, groups + skew - 1)].append(partial(plane.double, p, step))
        for step in range(bits + 1):
            plan[min(2 * step + 1, groups + skew - 1)].append(partial(plane.few_event, step))

    @pl.when(i == 0)
    def _():
        greet(place, z, pieces)
        x = x_ref[...]
        scale = lax.rsqrt(jnp.mean(x * x, axis=1, keepdims=True) + EPS)
        nx[pl.ds(HALO, tokens), :] = (x * scale * gain_ref[layer : layer + 1]).astype(BF)
        put_heads(rows_ref, heads_ref)

        @pl.when(z < pieces - 1)
        def _():
            halo_copy().start()

        if gathers:
            for p in range(pieces):
                plane.start(p)
            plane.start_few()

        @pl.when(z == 0)
        def _():
            nx[pl.ds(0, HALO), :] = jnp.zeros((HALO, nx.shape[1]), BF)
            incoming[...] = jnp.zeros(incoming.shape, BF)

        depth = nx.shape[1]
        step_in = dot_nn(nx[pl.ds(HALO, tokens), :], few_ref[..., 2 * STATE :].reshape(depth, LANES))
        step_ref[...] = step_in
        _, steps, _, summed, toward, reach, kept = step_terms(
            step_in, heads_ref, carried_ref, tail_ref, kept_ref, tokens
        )
        put_sums(summed, col, row, groups, tokens)
        terms[0] = split2(steps)
        terms[1] = split2(toward)
        terms[2] = split2(reach)
        kept2 = split2(kept)
        for group in range(groups):
            ke[group] = dot_nn(kept2, spread(group))

        @pl.when(z > 0)
        def _():
            halo_copy().wait_recv()

        shared_ref[...] = dot_nn(nx[...], few_ref[..., : 2 * STATE].reshape(depth, 2 * STATE))
        taps = shared_taps(csw_ref, csb_ref, layer)
        mixed = conv(lambda k: shared_ref[pl.ds(HALO - k, tokens), :], keep_ref, taps, tokens)
        maps = mixed * sigmoid(mixed)
        for c in range(chunks):
            part = maps[c * CH : (c + 1) * CH]
            into, out = part[:, :STATE], part[:, STATE:].astype(BF)
            inb[c], outb[c], inbt[c] = into.astype(BF), out, into.T.astype(BF)
            cross[c] = dot_nt(out, into.astype(BF))
        branch[...] = jnp.zeros(branch.shape, F32)
        squares[...] = jnp.zeros(squares.shape, F32)

    @pl.when(i < groups)
    def _():
        depth = nx.shape[1]
        group = i
        slot = lax.rem(group, skew + 1)
        gate_ref[0] = dot_nn(nx[pl.ds(HALO, tokens), :], side((wa, wb), 0))
        val_ref[0] = dot_nn(nx[...], side((wa, wb), 1))
        gp = side_params((pa, pb))
        for start in tiles(tokens):
            rows = pl.ds(start, TILE)
            mixed = conv_rows(lambda k: val_ref[0, pl.ds(HALO + start - k, TILE), :], keep_ref, gp, rows)
            xs[slot, rows, :] = mixed * sigmoid(mixed)
            gate = gate_ref[0, rows, :]
            gs[slot, rows, :] = gate * sigmoid(gate)
        turn_sums(col, group)
        spreader = spread(group)
        state = jnp.zeros((STATE, GC), F32)
        for c in range(chunks):
            rows = pl.ds(c * CH, CH)
            sized = xs[slot, rows, :] * dot_nn(terms[0, rows, :], spreader)
            weighted = (sized * dot_nn(terms[1, rows, :], spreader)).astype(BF)
            new = dot_nn(inbt[c], weighted)
            fresh[slot, c] = new
            state = ke[group, c : c + 1] * state + new
            for pair in range(HG // 2):
                lanes = pl.ds(pair * LANES, LANES)
                decayed = []
                for j in (2 * pair, 2 * pair + 1):
                    across = col[1, rows, j : j + 1] - row[group, j : j + 1, rows]
                    decayed.append((cross[c] * jnp.exp(jnp.minimum(across, bias_ref[c]))).astype(BF))
                blocks = halves(sized[:, pair * LANES : (pair + 1) * LANES])
                intra[slot, rows, lanes] = dot_nn(jnp.concatenate(decayed, axis=1), blocks)
        fold[slot] = state

    j = i - z

    @pl.when(jnp.logical_and(j >= 0, j < groups))
    def _():
        @pl.when(z > 0)
        def _():
            state_copy(j).wait_recv()

        @pl.when(z < pieces - 1)
        def _():
            total = ke[j, 0:1]
            for c in range(1, chunks):
                total = total * ke[j, c : c + 1]
            outgoing[j] = (total * incoming[j].astype(F32) + fold[lax.rem(j, skew + 1)]).astype(BF)
            state_copy(j).start()

    @pl.when(i >= skew)
    def _():
        group = i - skew
        slot = lax.rem(group, skew + 1)
        depth = nx.shape[1]
        spreader = spread(group)
        gp = side_params((qa, qb))
        state = incoming[group].astype(F32)
        for c in range(chunks):
            rows = pl.ds(c * CH, CH)
            low = state.astype(BF)
            state_ref[0, c] = low
            y = intra[slot, rows, :] + dot_nn(outb[c], low) * dot_nn(terms[2, rows, :], spreader)
            y_ref[0, rows, :] = y
            gated = (y + gp[6:7] * xs[slot, rows, :]) * gs[slot, rows, :]
            squares[rows, :] += jnp.sum(gated * gated, axis=1, keepdims=True)
            intra[slot, rows, :] = gated * gp[5:6]
            if c < chunks - 1:
                state = ke[group, c : c + 1] * state + fresh[slot, c]
        branch[...] += dot_nt(intra[slot].astype(BF), side((oa, ob), 0))

    for step, acts in enumerate(plan):
        if acts:

            @pl.when(i == step)
            def _(acts=acts):
                for act in acts:
                    act()

    @pl.when(i == groups + skew - 1)
    def _():
        inner = groups * GC
        factor = lax.rsqrt(squares[...] * (1.0 / inner) + EPS)
        r_ref[...] = factor
        next_ref[...] = x_ref[...] + branch[...] * factor[:, 0:1]
        nxt_ref[...] = nx[pl.ds(HALO, tokens), :].T
        nht_ref[...] = nx[pl.ds(0, HALO), :].T
        if gathers:
            plane.finish()
            few_out[...] = few_all[...]

        @pl.when(z < pieces - 1)
        def _():
            halo_copy().wait_send()
            for group in range(groups):
                state_copy(group).wait_send()


class Place:
    def __init__(self, bits):
        self.bits = bits
        self.index = lax.axis_index("dp")
        self.bit = [lax.rem(self.index // (1 << b), 2) for b in range(bits)]
        self.dims = (2,) * bits
        self.all = (slice(None),) * bits

    def flip(self, b):
        return self.index + (1 << b) * (1 - 2 * self.bit[b])

    def along(self, done):
        return tuple(slice(None) if b in done else self.bit[b] for b in reversed(range(self.bits)))

    def order(self, odd):
        rest = list(range(1, self.bits))
        return [0] + (rest[::-1] if odd else rest)

    def partner(self, odd, step):
        return self.flip(self.order(odd)[step])

    def region(self, odd, step, keep):
        order = self.order(odd)
        at = []
        for b in reversed(range(self.bits)):
            if b in order[:step]:
                at.append(self.bit[b])
            elif b == order[step]:
                at.append(self.bit[b] if keep else 1 - self.bit[b])
            else:
                at.append(slice(None))
        return tuple(at)

    def mine(self):
        return tuple(self.bit[b] for b in reversed(range(self.bits)))


def backward_kernel(
    dims,
    g_ref, *refs,
):
    pieces, groups, tokens, skew, bits = dims
    line_refs, refs = refs[: LAYERS + 1], refs[LAYERS + 1 :]
    weights, refs = [refs[5 * n : 5 * n + 5] for n in range(LAYERS)], refs[5 * LAYERS :]
    gain_ref, nxt, nht, r_ref, pa, pb, qa, qb, rows_ref, *refs = refs
    csw_ref, csb_ref, keep_ref, biast_ref, carried_ref, tail_ref, kept_ref, *refs = refs
    gate_ref, val_ref, y_ref, valb_ref, state_ref, shared_ref, step_ref, *refs = refs
    gx_ref, gw_ref, go_ref, gm_ref, rows_ref_out, small_ref, mid_ref, *refs = refs
    gb, gbt, r2, inb, outb, outbt, crosst, col, row, terms, ke, *refs = refs
    dys, xs, fs, dgs, fold, incoming, outgoing, gnorm, dct, dbt, dgt, sd, sp, sq, se, dxd, turned, hrecv, *refs = refs
    own, own_m, got_z, got_m, halo_send, halo_recv, send, recv, sum_send, sum_recv, z_send, z_recv, *refs = refs
    msum_send, msum_recv, mz_send, mz_recv, next_sem, load_sem, heads_ref, *refs = refs
    rows_now, row_total, row_got, row_z, map_total, map_got, map_z, end_total, end_got, end_z, *refs = refs
    few_send, few_recv, fz_send, fz_recv, *got = refs
    chunks = tokens // CH
    phase, i = pl.program_id(0), pl.program_id(1)
    layer = LAYERS - 1 - phase
    z = lax.axis_index("tensor")
    right, left = jnp.minimum(z + 1, pieces - 1), jnp.maximum(z - 1, 0)
    back = pieces - 1 - z
    depth = gb.shape[1]
    inner = groups * GC

    def halo_copy():
        return pltpu.make_async_remote_copy(
            src_ref=gnorm, dst_ref=hrecv.at[phase], send_sem=halo_send, recv_sem=halo_recv.at[phase],
            device_id={"tensor": left}, device_id_type=MESH,
        )

    def state_copy(group):
        return pltpu.make_async_remote_copy(
            src_ref=outgoing.at[group], dst_ref=incoming.at[phase, group],
            send_sem=send.at[group], recv_sem=recv.at[phase, group], device_id={"tensor": left}, device_id_type=MESH,
        )

    place = Place(bits)
    parts, parts_m = got[:bits], got[bits:]

    def part(step, group, half):
        return lax.rem(group, SLOTS), half

    def held(step, group, half, keep):
        return (group, half) + place.region(half, step, keep)

    def put_gradient(group, which, value):
        rows = own.shape[-2] // 3
        for half in range(2):
            cut = value[:, half * LANES : (half + 1) * LANES].astype(BF).reshape(place.dims + (rows, LANES))
            own[(group, half) + place.all + (pl.ds(which * rows, rows),)] = cut

    def sum_copy(group, step, half):
        return pltpu.make_async_remote_copy(
            src_ref=own.at[held(step, group, half, False)], dst_ref=parts[step].at[part(step, group, half)],
            send_sem=sum_send.at[group, step, half], recv_sem=sum_recv.at[group, step, half],
            device_id={"dp": place.partner(half, step)}, device_id_type=MESH,
        )

    def z_copy(group, half, turn):
        column = lax.div(group, pieces // 2)
        return pltpu.make_async_remote_copy(
            src_ref=own.at[(group, half) + place.mine()],
            dst_ref=got_z.at[turn, z, column], send_sem=z_send.at[group, half], recv_sem=z_recv.at[turn, z, column],
            device_id={"tensor": quarter(group, half, pieces)}, device_id_type=MESH,
        )

    def advance(group, step, turn):
        @pl.when(jnp.logical_and(group >= 0, group < groups))
        def _():
            for half in range(2):
                if step:
                    sum_copy(group, step - 1, half).wait_recv()
                    at = held(step - 1, group, half, True)
                    own[at] = own[at] + parts[step - 1][part(step - 1, group, half)]
                if step < bits:
                    sum_copy(group, step, half).start()
                if step == bits:

                    @pl.when(quarter(group, half, pieces) != z)
                    def _(half=half):
                        z_copy(group, half, turn).start()

    def misc_copy(step):
        return pltpu.make_async_remote_copy(
            src_ref=own_m.at[place.region(False, step, False)], dst_ref=parts_m[step],
            send_sem=msum_send.at[step], recv_sem=msum_recv.at[step],
            device_id={"dp": place.partner(False, step)}, device_id_type=MESH,
        )

    def misc_z(k, turn, source):
        return pltpu.make_async_remote_copy(
            src_ref=own_m.at[place.mine()], dst_ref=got_m.at[turn, source], send_sem=mz_send.at[k],
            recv_sem=mz_recv.at[turn, source],
            device_id={"tensor": lax.rem(z + k, pieces)}, device_id_type=MESH,
        )

    def misc_advance(step, turn):
        if step:
            misc_copy(step - 1).wait_recv()
            at = place.region(False, step - 1, True)
            own_m[at] = own_m[at] + parts_m[step - 1][...]
        if step < bits:
            misc_copy(step).start()
        else:
            for k in range(1, pieces):
                misc_z(k, turn, z).start()
            got_m[turn, z] = own_m[place.mine()]

    def drain(late, turn):
        for step in reversed(range(1, bits + 1)):
            if late <= step:
                advance(jnp.int32(groups - 1 + late - step), step, turn)

    def put_rows(group, rows, adds):
        rows = jnp.concatenate(rows, axis=0)
        at = lax.rem(group, pieces // 2), pl.ds(pl.multiple_of(lax.div(group, pieces // 2) * 8, 8), 8)
        for half in range(2):
            cut = rows[:, half * LANES : (half + 1) * LANES]
            if adds:
                cut = cut + rows_now[at[0], half, at[1], :]
            rows_now[at[0], half, at[1], :] = cut

    def quarter_of(at):
        upper_half = at >= pieces // 2
        return jnp.where(upper_half, pieces - 1 - at, at), jnp.where(upper_half, 1, 0)

    def few_copies(step, early):
        refs = [(row_total, row_got), (map_total, map_got)] if early else [(end_total, end_got)]
        first = 0 if early else 2
        return [
            pltpu.make_async_remote_copy(
                src_ref=total.at[step], dst_ref=other.at[step], send_sem=few_send.at[first + n, step],
                recv_sem=few_recv.at[first + n, step], device_id={"dp": place.partner(False, step)}, device_id_type=MESH,
            )
            for n, (total, other) in enumerate(refs)
        ]

    def few_lines(k, turn, source, early):
        target = lax.rem(z + k, pieces)
        pairs = [(end_total.at[bits], end_z)]
        if early:
            pairs = [(row_total.at[(bits,) + quarter_of(target)], row_z), (map_total.at[bits], map_z)]
        first = 0 if early else 2
        return [
            pltpu.make_async_remote_copy(
                src_ref=ref, dst_ref=other.at[turn, source], send_sem=fz_send.at[first + n, k],
                recv_sem=fz_recv.at[turn, first + n, source], device_id={"tensor": target}, device_id_type=MESH,
            )
            for n, (ref, other) in enumerate(pairs)
        ]

    def few_advance(step, turn, early):
        if step:
            for copy in few_copies(step - 1, early):
                copy.wait_recv()
            for total, other in [(row_total, row_got), (map_total, map_got)] if early else [(end_total, end_got)]:
                total[step] = total[step - 1] + other[step - 1]
        if step < bits:
            for copy in few_copies(step, early):
                copy.start()
        else:
            for k in range(1, pieces):
                for copy in few_lines(k, turn, z, early):
                    copy.start()
            if early:
                row_z[turn, z] = row_total[(bits,) + quarter_of(z)]
                map_z[turn, z] = map_total[bits]
            else:
                end_z[turn, z] = end_total[bits]

    def finish_few(turn):
        for n in range(1, pieces):
            source = lax.rem(z + n, pieces)
            for copy in few_lines(n, turn, source, True) + few_lines(n, turn, source, False):
                copy.wait_recv()
            misc_z(n, turn, source).wait_recv()
        misc = got_m[turn, 0].astype(F32)
        sums = [ref[turn, 0] for ref in (row_z, map_z, end_z)]
        for source in range(1, pieces):
            sums = [total + ref[turn, source] for total, ref in zip(sums, (row_z, map_z, end_z))]
            misc = misc + got_m[turn, source].astype(F32)
        layer_done = LAYERS - 1 - turn
        rows_ref_out[layer_done] = sums[0]
        small_ref[layer_done, pl.ds(0, 8), :] = sums[1]
        small_ref[layer_done, pl.ds(8, 8), :] = sums[2]
        gm_ref[layer_done] = misc
        for step in range(bits):
            misc_copy(step).wait_send()
            for copy in few_copies(step, True) + few_copies(step, False):
                copy.wait_send()
        for n in range(1, pieces):
            misc_z(n, turn, z).wait_send()
            for copy in few_lines(n, turn, z, True) + few_lines(n, turn, z, False):
                copy.wait_send()

    def finish_group(group, turn):
        column = lax.div(group, pieces // 2)
        for half in range(2):

            @pl.when(quarter(group, half, pieces) == z)
            def _(half=half):
                total = own[(group, half) + place.mine()].astype(F32)
                for n in range(1, pieces):
                    source = lax.rem(z + n, pieces)
                    pltpu.make_async_remote_copy(
                        src_ref=got_z.at[turn, source, column], dst_ref=got_z.at[turn, source, column],
                        send_sem=z_send.at[group, half], recv_sem=z_recv.at[turn, source, column],
                        device_id={"tensor": source}, device_id_type=MESH,
                    ).wait_recv()
                    total = total + got_z[turn, source, column].astype(F32)
                at = pl.multiple_of(column * LANES, LANES)
                total = total.reshape(3, -1, LANES)
                gw_ref[LAYERS - 1 - turn, :, :, pl.ds(at, LANES)] = total[:2]
                go_ref[LAYERS - 1 - turn, :, pl.ds(at, LANES)] = total[2]

            @pl.when(quarter(group, half, pieces) != z)
            def _(half=half):
                z_copy(group, half, turn).wait_send()

            for step in range(bits):
                sum_copy(group, step, half).wait_send()

    def load(x, g):
        found = []
        for n in range(depth // GC):
            cols = pl.ds(n * GC, GC)
            found.append(pltpu.make_async_copy(x.at[:, cols], xs.at[n], load_sem.at[0, n]))
            if g is not None:
                found.append(pltpu.make_async_copy(g.at[:, cols], fs.at[n], load_sem.at[1, n]))
        return found

    def of_layer(pick):
        chosen = pick(0)
        for n in range(1, LAYERS):
            chosen = jnp.where(layer == n, pick(n), chosen)
        return chosen

    def out_weights():
        return of_layer(lambda n: side(weights[n][2:4], 0))

    def in_weights(which):
        return of_layer(lambda n: side(weights[n][:2], which))

    def taps():
        return jnp.concatenate([csw_ref[layer], csb_ref[pl.ds(layer, 1), :]], axis=0)

    def shared_conv():
        return conv(lambda k: shared_ref[pl.ds(HALO - k, tokens), :], keep_ref, taps(), tokens)

    @pl.when(jnp.logical_and(phase == 0, i == 0))
    def _():
        greet(place, z, pieces)

        @pl.when(z == pieces - 1)
        def _():
            incoming[...] = jnp.zeros(incoming.shape, BF)

        copies = [pltpu.make_async_copy(line_refs[LAYERS], gx_ref, next_sem)] + load(line_refs[LAYERS - 1], g_ref)
        for copy in copies:
            copy.start()
        for copy in copies:
            copy.wait()

    for turn in range(1, LAYERS):

        @pl.when(jnp.logical_and(phase == turn, i == 0))
        def _(turn=turn):
            copies = load(line_refs[LAYERS - 1 - turn], None)
            copies.append(pltpu.make_async_copy(gx_ref, mid_ref, next_sem))
            for copy in copies:
                copy.start()
            for n in range(depth // GC):
                fs[n] = gx_ref[:, n * GC : (n + 1) * GC]
            for copy in copies:
                copy.wait()
            copy = pltpu.make_async_copy(line_refs[LAYERS - turn], gx_ref, next_sem)
            copy.start()
            copy.wait()

    @pl.when(i == 0)
    def _():
        put_heads(rows_ref, heads_ref)
        dots = jnp.zeros((tokens, 1), F32)
        for k in range(depth // GC):
            cols = slice(k * GC, (k + 1) * GC)
            low = fs[k].astype(BF)
            gb[:, cols] = low
            gbt[cols, :] = low.T
            dots = dots + jnp.sum(low.astype(F32) * (gx_ref[:, cols] - xs[k]), axis=1, keepdims=True)
        r = r_ref[...]
        r2[...] = r * r * dots * (1.0 / inner)
        _, steps, _, summed, toward, reach, kept = step_terms(
            step_ref[...], heads_ref, carried_ref, tail_ref, kept_ref, tokens
        )
        put_sums(summed, col, row, groups, tokens)
        terms[0] = split2(steps)
        terms[1] = split2(toward)
        terms[2] = split2(reach)
        kept2 = split2(kept)
        for group in range(groups):
            ke[group] = dot_nn(kept2, spread(group))
        mixed = shared_conv()
        maps = mixed * sigmoid(mixed)
        for c in range(chunks):
            part = maps[c * CH : (c + 1) * CH]
            into, out = part[:, :STATE].astype(BF), part[:, STATE:]
            inb[c], outb[c], outbt[c] = into, out.astype(BF), out.T.astype(BF)
            crosst[c] = dot_nt(into, out.astype(BF))
        for ref in (gx_ref, gnorm, dct, dbt, dgt, sd, sp, sq, se):
            ref[...] = jnp.zeros(ref.shape, F32)

    @pl.when(i < groups)
    def _():
        group = i
        slot = lax.rem(group, skew + 1)
        gp = side_params((pa, pb))

        for turn in range(1, LAYERS):

            @pl.when(phase == turn)
            def _(turn=turn):
                finish_group(group, turn - 1)

        dxd[...] = dot_nn(gb[...], out_weights())
        gain_sum = skip_sum = jnp.zeros((1, GC), F32)
        for start in tiles(tokens):
            rows = pl.ds(start, TILE)
            mixed = conv_rows(lambda k: val_ref[0, pl.ds(HALO + start - k, TILE), :], keep_ref, gp, rows)
            part = sigmoid(mixed)
            x = mixed * part
            xs[slot, rows, :] = x
            fs[slot, rows, :] = part + x * (1.0 - part)
            r = twice(r_ref[rows, :])
            gm = dxd[rows, :]
            scan = y_ref[0, rows, :] + gp[6:7] * x
            gate = gate_ref[0, rows, :]
            part = sigmoid(gate)
            silu = gate * part
            gated = scan * silu
            normal = gated * r
            turned[rows, :] = (normal * gp[5:6]).astype(BF)
            ggated = r * gp[5:6] * gm - gated * twice(r2[rows, :])
            dy = ggated * silu
            dys[slot, rows, :] = dy.astype(BF)
            dgs[slot, rows, :] = (ggated * scan * (part + silu * (1.0 - part))).astype(BF)
            gain_sum = gain_sum + jnp.sum(gm * normal, axis=0, keepdims=True)
            skip_sum = skip_sum + jnp.sum(dy * x, axis=0, keepdims=True)
        put_gradient(group, 2, dot_nn(gbt[...], turned[...]))
        put_rows(group, [jnp.zeros((5, GC), F32), gain_sum, skip_sum, jnp.zeros((1, GC), F32)], False)
        spreader, collector = spread(group), collect(group)
        state = jnp.zeros((STATE, GC), F32)
        for c in reversed(range(chunks)):
            rows = pl.ds(c * CH, CH)
            reached = (dys[slot, rows, :].astype(F32) * dot_nn(terms[2, rows, :], spreader)).astype(BF)
            sp[rows, :] += dot_nn(split2(dys[slot, rows, :].astype(F32) * y_ref[0, rows, :]), collector)
            new = dot_nn(outbt[c], reached)
            state = ke[group, c : c + 1] * state + new
        fold[slot] = state

    for turn in range(1, LAYERS):
        for late in range(1, max(bits, skew) + 1):
            place_at = min(late, skew) - 1

            @pl.when(jnp.logical_and(phase == turn, i == place_at))
            def _(turn=turn, late=late):
                drain(late, turn - 1)
                if late <= bits:
                    few_advance(late, turn - 1, True)
                    few_advance(late, turn - 1, False)
                    misc_advance(late, turn - 1)

        @pl.when(jnp.logical_and(phase == turn, i == skew))
        def _(turn=turn):
            finish_few(turn - 1)

    j = i - back

    @pl.when(jnp.logical_and(j >= 0, j < groups))
    def _():
        @pl.when(z < pieces - 1)
        def _():
            state_copy(j).wait_recv()

        @pl.when(z > 0)
        def _():
            total = ke[j, 0:1]
            for c in range(1, chunks):
                total = total * ke[j, c : c + 1]
            outgoing[j] = (total * incoming[phase, j].astype(F32) + fold[lax.rem(j, skew + 1)]).astype(BF)
            state_copy(j).start()

    @pl.when(i >= skew)
    def _():
        group = i - skew
        slot = lax.rem(group, skew + 1)
        gp = side_params((qa, qb))
        spreader, collector = spread(group), collect(group)
        turn_sums(col, group)
        grad = incoming[phase, group].astype(F32)
        ends = [None] * chunks
        for c in reversed(range(chunks)):
            rows = pl.ds(c * CH, CH)
            low = grad.astype(BF)
            state = state_ref[0, c]
            ends[c] = jnp.sum(low.astype(F32) * state.astype(F32), axis=0, keepdims=True) * ke[group, c : c + 1]
            x = xs[slot, rows, :]
            dy = dys[slot, rows, :].astype(F32)
            steps = dot_nn(terms[0, rows, :], spreader)
            toward = dot_nn(terms[1, rows, :], spreader)
            reached = (dy * dot_nn(terms[2, rows, :], spreader)).astype(BF)
            grad = ke[group, c : c + 1] * grad + dot_nn(outbt[c], reached)
            sized = x * steps
            weighted = (sized * toward).astype(BF)
            later = dot_nn(inb[c], low) * toward
            dbt[c] += dot_nt(weighted, low)
            dct[c] += dot_nt(reached, state)
            parts = []
            cross = crosst[c]
            pairs_total = jnp.zeros((CH, CH), F32)
            for pair in range(HG // 2):
                at = slice(pair * LANES, (pair + 1) * LANES)
                dyp = dy[:, at]
                products = dot_nt(halves(sized[:, at]), dyp.astype(BF))
                decayed = []
                for n in range(2):
                    h = 2 * pair + n
                    across = row[group, h : h + 1, rows] - col[1, rows, h : h + 1]
                    decay = jnp.exp(jnp.minimum(across, biast_ref[c]))
                    decayed.append((cross * decay).astype(BF))
                    pairs_total = pairs_total + products[n * CH : (n + 1) * CH] * decay
                parts.append(dot_nn(jnp.concatenate(decayed, axis=1), halves(dyp)))
            dgt[c] += pairs_total
            within = jnp.concatenate(parts, axis=1)
            whole = within + later
            lowered = sized.astype(BF).astype(F32) * within
            sd[rows, :] += dot_nn(split2(whole * x), collector)
            sp[rows, :] -= dot_nn(split2(lowered), collector)
            sq[rows, :] += dot_nn(split2(sized * later), collector)
            dxd[rows, :] = (whole * steps + gp[6:7] * dy) * fs[slot, rows, :]
        for step in reversed(range(1, bits + 1)):
            advance(group - step, step, phase)
        ends.append(jnp.zeros((8 - chunks, GC), F32))
        se[...] += dot_nn(split2(jnp.concatenate(ends, axis=0)), collector)
        wide, sums = conv_back(
            dxd[...], lambda k: valb_ref[0, pl.ds(HALO - k, tokens), :], keep_ref, gp, tokens
        )
        put_rows(group, sums + [jnp.zeros((3, GC), F32)], True)
        wide = wide.astype(BF)
        dgate = dgs[slot]
        put_gradient(group, 0, dot_nn(nxt[...], dgate))
        put_gradient(group, 1, dot_nn(nxt[...], wide[HALO:]) + dot_nn(nht[...], wide[:HALO]))
        advance(group, 0, phase)
        both = jnp.concatenate([in_weights(0), in_weights(1)], axis=1)
        gnorm[...] += dot_nt(wide[:HALO], both[:, GC:])
        gx_ref[...] += dot_nt(jnp.concatenate([dgate, wide[HALO:]], axis=1), both)

    @pl.when(i == groups + skew - 1)
    def _():
        for turn in range(LAYERS):

            @pl.when(phase == turn)
            def _(turn=turn):
                for copy in load(line_refs[LAYERS - 1 - turn], mid_ref if turn else g_ref):
                    copy.start()
                pltpu.make_async_copy(weights[LAYERS - 1 - turn][4], own_m, next_sem).start()

        upper = (iota2((CH, CH), 0) <= iota2((CH, CH), 1)).astype(F32)
        before = (iota2((CH, CH), 0) > iota2((CH, CH), 1)).astype(F32)
        raw, steps, rates, _, _, _, _ = step_terms(step_ref[...], heads_ref, carried_ref, tail_ref, kept_ref, tokens)
        drates, dmaps = [], []
        for c in range(chunks):
            rows = slice(c * CH, (c + 1) * CH)
            drates.append(dot_nn(upper, sp[rows, :], HI) + dot_nn(before, sq[rows, :], HI) + se[c : c + 1])
            low = dgt[c].astype(BF)
            into = dbt[c] + dot_nn(low, outb[c])
            out = dct[c] + dot_tn(low, inb[c])
            dmaps.append(jnp.concatenate([into, out], axis=1))
        drate = jnp.concatenate(drates, axis=0)
        dstep = (sd[...] - drate * heads_ref[1:2]) * sigmoid(raw)
        head_sums = jnp.concatenate(
            [jnp.sum(dstep, axis=0, keepdims=True), jnp.sum(drate * rates, axis=0, keepdims=True)], axis=1
        )
        mixed = shared_conv()
        part = sigmoid(mixed)
        dmixed = jnp.concatenate(dmaps, axis=0) * (part + mixed * part * (1.0 - part))
        wide, sums = conv_back(dmixed, lambda k: shared_ref[pl.ds(HALO - k, tokens), :], keep_ref, taps(), tokens)
        row_total[0] = rows_now[...]
        map_total[0] = jnp.concatenate(sums + [jnp.zeros((3, 2 * STATE), F32)], axis=0)
        few_advance(0, phase, True)
        wide = wide.astype(BF)
        dstep = dstep.astype(BF)
        pltpu.make_async_copy(weights[0][4], own_m, next_sem).wait()
        back_wide = dot_nt(wide, own_m[..., : 2 * STATE].reshape(depth, 2 * STATE))
        gnorm[...] += back_wide[:HALO]

        @pl.when(z > 0)
        def _():
            halo_copy().start()

        gx_ref[...] += back_wide[HALO:] + dot_nt(dstep, own_m[..., 2 * STATE :].reshape(depth, LANES))
        at_end = phase == LAYERS - 1

        @pl.when(at_end)
        def _():
            drain(1, LAYERS - 1)

        misc = jnp.concatenate(
            [dot_nn(nxt[...], wide[HALO:]) + dot_nn(nht[...], wide[:HALO]), dot_nn(nxt[...], dstep)], axis=1
        )
        own_m[...] = misc.astype(BF).reshape(own_m.shape)
        misc_advance(0, phase)

        @pl.when(z < pieces - 1)
        def _():
            halo_copy().wait_recv()
            gx_ref[pl.ds(tokens - HALO, HALO), :] += hrecv[phase]

        for copy in load(line_refs[0], g_ref):
            copy.wait()
        blocks = [(k, slice(k * GC, (k + 1) * GC)) for k in range(depth // GC)]
        gain = gain_ref[pl.ds(layer, 1), :]
        power = inside = jnp.zeros((tokens, 1), F32)
        for k, cols in blocks:
            power = power + jnp.sum(xs[k] * xs[k], axis=1, keepdims=True)
            gained = gx_ref[:, cols] * gain[:, cols]
            inside = inside + jnp.sum(gained * xs[k], axis=1, keepdims=True)
        q = lax.rsqrt(power * (1.0 / depth) + EPS)
        inside = inside * (q * q * q) * (1.0 / depth)
        cuts = [jnp.sum(gx_ref[:, cols] * xs[k] * q, axis=0, keepdims=True) for k, cols in blocks]
        end_total[0] = jnp.concatenate(cuts + [head_sums, jnp.zeros((7 - len(cuts), GC), F32)], axis=0)
        few_advance(0, phase, False)
        for k, cols in blocks:
            gx_ref[:, cols] = fs[k] + q * (gx_ref[:, cols] * gain[:, cols]) - xs[k] * inside

        @pl.when(z > 0)
        def _():
            halo_copy().wait_send()
            for group in range(groups):
                state_copy(group).wait_send()

        @pl.when(at_end)
        def _():
            turn = LAYERS - 1
            few_advance(1, turn, True)
            misc_advance(1, turn)
            for step in range(2, bits + 1):
                drain(step, turn)
                few_advance(step, turn, True)
                few_advance(step - 1, turn, False)
                misc_advance(step, turn)
            few_advance(bits, turn, False)
            finish_few(turn)
            for group in range(groups):
                finish_group(jnp.int32(group), turn)


def whole(shape):
    return pl.BlockSpec(shape, lambda i: (0,) * len(shape), pipeline_mode=pl.Buffered(1))


def quarter(group, half, pieces):
    at = lax.rem(group, pieces // 2) if pieces > 2 else 0 * group
    return pieces - 1 - at if half else at


def group_specs(dims, wall):
    pieces, groups, _, skew = dims
    dp, _, _, share, _ = wall
    last = groups - 1

    def early(i):
        return jnp.minimum(i, last)

    def late(i):
        return jnp.maximum(i - skew, 0)

    def block(rows, at):
        return pl.BlockSpec((1, rows, GC), lambda i: (at(i), 0, 0))

    def both(make):
        return [make(0), make(1)]

    def column(i, at):
        return lax.div(at(i), pieces // 2)

    def pair(at):
        return both(
            lambda half: pl.BlockSpec(
                (dp, 1, 2, share, LANES), lambda i: (0, quarter(at(i), half, pieces), 0, 0, column(i, at))
            )
        )

    def single(at):
        return both(
            lambda half: pl.BlockSpec(
                (dp, 1, 1, share, LANES), lambda i: (0, quarter(at(i), half, pieces), 2, 0, column(i, at))
            )
        )

    def params(layer, at):
        return both(
            lambda half: pl.BlockSpec(
                (1, 1, 8, LANES), lambda i: (quarter(at(i), half, pieces), layer, 0, column(i, at))
            )
        )

    return early, late, block, pair, single, params


def side(refs, n):
    rows = refs[0].shape[0] * refs[0].shape[3]
    return jnp.concatenate([ref[:, 0, n].reshape(rows, LANES) for ref in refs], axis=1)


def side_params(refs):
    return jnp.concatenate([ref[0, 0] for ref in refs], axis=1)


def fixed(shape, place):
    return pl.BlockSpec(shape, lambda i: place, pipeline_mode=pl.Buffered(1))


def layer_forward(dims, bits, layer, x, gain, w, few, pack, csw, csb, masks, later, earlier):
    pieces, groups, tokens, skew = dims
    keep, bias, _, carried, tail, kept = masks
    chunks = tokens // CH
    depth = x.shape[1]
    ext = tokens + HALO
    slots = skew + 1
    early, late, _, pair, single, params = group_specs(dims, w.shape)

    def block(rows, at):
        return pl.BlockSpec((None, 1, rows, GC), lambda i: (layer, at(i), 0, 0))

    def mine(shape):
        return fixed((None,) + shape, (layer,) + (0,) * len(shape))

    anywhere = pl.BlockSpec(memory_space=pl.ANY)
    near = pl.BlockSpec(memory_space=pltpu.VMEM)
    gathers = later is not None
    cut = (2,) * bits
    buffers, sems = plane_scratch(pieces, bits, w.shape[3])
    if gathers:
        later_few, later = later
    first = 19 + 2 * gathers
    aliases = {first + k: 1 + k for k in range(len(earlier))}
    if gathers:
        aliases[20] = 11
    return pl.pallas_call(
        partial(forward_kernel, dims + (bits, layer, gathers)),
        grid=(groups + skew,),
        in_specs=[
            whole((tokens, depth)), whole(gain.shape), *pair(early), *single(late),
            whole(few.shape), *params(layer, early), *params(layer, late), fixed((pieces, 1, 8, 2 * LANES), (0, layer, 0, 0)),
            whole(csw.shape), whole(csb.shape),
            whole(keep.shape), whole(bias.shape), whole(carried.shape), whole(tail.shape), whole(kept.shape),
        ] + [near, anywhere] * gathers + [anywhere] * len(earlier),
        out_specs=[
            whole((tokens, depth)), mine((depth, tokens)), mine((depth, HALO)),
            block(tokens, early), block(ext, early), block(tokens, late),
            pl.BlockSpec((None, 1, chunks, STATE, GC), lambda i: (layer, late(i), 0, 0, 0)),
            mine((ext, 2 * STATE)), mine((tokens, LANES)), mine((tokens, LANES)),
        ] + [near, anywhere] * gathers,
        out_shape=[
            jax.ShapeDtypeStruct((tokens, depth), F32),
            jax.ShapeDtypeStruct((LAYERS, depth, tokens), BF),
            jax.ShapeDtypeStruct((LAYERS, depth, HALO), BF),
            jax.ShapeDtypeStruct((LAYERS, groups, tokens, GC), F32),
            jax.ShapeDtypeStruct((LAYERS, groups, ext, GC), F32),
            jax.ShapeDtypeStruct((LAYERS, groups, tokens, GC), F32),
            jax.ShapeDtypeStruct((LAYERS, groups, chunks, STATE, GC), BF),
            jax.ShapeDtypeStruct((LAYERS, ext, 2 * STATE), F32),
            jax.ShapeDtypeStruct((LAYERS, tokens, LANES), F32),
            jax.ShapeDtypeStruct((LAYERS, tokens, LANES), F32),
        ] + (
            [jax.ShapeDtypeStruct(cut + later_few.shape, BF), jax.ShapeDtypeStruct(later.shape, BF)]
            if gathers
            else []
        ),
        scratch_shapes=[
            pltpu.VMEM((ext, depth), BF),
            pltpu.VMEM((chunks, CH, STATE), BF),
            pltpu.VMEM((chunks, STATE, CH), BF),
            pltpu.VMEM((chunks, CH, STATE), BF),
            pltpu.VMEM((chunks, CH, CH), F32),
            pltpu.VMEM((2, tokens, LANES), F32),
            pltpu.VMEM((groups, 8, tokens), F32),
            pltpu.VMEM((3, tokens, 2 * LANES), BF),
            pltpu.VMEM((groups, 8, GC), F32),
            pltpu.VMEM((slots, tokens, GC), F32),
            pltpu.VMEM((slots, tokens, GC), F32),
            pltpu.VMEM((slots, tokens, GC), F32),
            pltpu.VMEM((slots, chunks, STATE, GC), F32),
            pltpu.VMEM((slots, STATE, GC), F32),
            pltpu.VMEM((groups, STATE, GC), BF),
            pltpu.VMEM((groups, STATE, GC), BF),
            pltpu.VMEM((tokens, depth), F32),
            pltpu.VMEM((tokens, LANES), F32),
            pltpu.VMEM((8, LANES), F32),
            pltpu.SemaphoreType.DMA,
            pltpu.SemaphoreType.DMA,
            pltpu.SemaphoreType.DMA((groups,)),
            pltpu.SemaphoreType.DMA((groups,)),
        ] + (buffers + sems if gathers else []),
        input_output_aliases=aliases,
        compiler_params=pltpu.CompilerParams(
            collective_id=layer, has_side_effects=True, vmem_limit_bytes=VMEM_LIMIT_FORWARD,
            dimension_semantics=("arbitrary",),
        ),
        name="layer_forward",
    )(
        x, gain, w, w, w, w, few, pack, pack, pack, pack, pack, csw, csb, keep, bias, carried, tail, kept,
        *([later_few, later] if gathers else []), *earlier,
    )


def layers_backward(dims, bits, g, line, gain, saved, weights, pack, csw, csb, masks):
    pieces, groups, tokens, skew = dims
    keep, _, biast, carried, tail, kept = masks
    nxt, nht, gate, val, y, states, shared, step_in, r = saved
    anywhere = pl.BlockSpec(memory_space=pl.ANY)
    chunks = tokens // CH
    depth = g.shape[1]
    wall = weights[0][0]
    _, _, _, share, wide = wall.shape
    ext = tokens + HALO
    slots = max(skew + 1, depth // GC)
    columns = 2 * groups // pieces
    row_shape = (pieces // 2, 2, columns * 8, LANES)
    few_shape = (8, GC)
    halves_of = [(2,) * (bits - 1 - step) for step in range(bits)]
    steps = groups + skew
    early, late, *_ = group_specs(dims, wall.shape)

    def in_turn(layer, at):
        turn = LAYERS - 1 - layer
        return lambda ph, i: at(jnp.where(ph == turn, i, jnp.where(ph < turn, 0, steps - 1)))

    def block(rows, at):
        return pl.BlockSpec((None, 1, rows, GC), lambda ph, i: (LAYERS - 1 - ph, at(i), 0, 0))

    def of_layer(v):
        return pl.BlockSpec(
            (None,) + v.shape[1:], lambda ph, i: (LAYERS - 1 - ph,) + (0,) * (v.ndim - 1),
            pipeline_mode=pl.Buffered(1),
        )

    def weight_blocks(count, first, at):
        def spec(half):
            def place(ph, i):
                group = at(ph, i)
                return 0, quarter(group, half, pieces), first, 0, lax.div(group, pieces // 2)

            return pl.BlockSpec((wall.shape[0], 1, count, share, LANES), place)

        return [spec(half) for half in range(2)]

    def group_params(at):
        def spec(half):
            def place(ph, i):
                group = at(i)
                return quarter(group, half, pieces), LAYERS - 1 - ph, 0, lax.div(group, pieces // 2)

            return pl.BlockSpec((1, 1, 8, LANES), place)

        return [spec(half) for half in range(2)]

    def whole(shape):
        return pl.BlockSpec(shape, lambda ph, i: (0,) * len(shape), pipeline_mode=pl.Buffered(1))

    weight_specs, weight_args = [], []
    for layer in range(LAYERS):
        w, few = weights[layer]
        weight_specs += weight_blocks(2, 0, in_turn(layer, late)) + weight_blocks(1, 2, in_turn(layer, early)) + [anywhere]
        weight_args += [w, w, w, w, few]
    return pl.pallas_call(
        partial(backward_kernel, dims + (bits,)),
        grid=(LAYERS, steps),
        in_specs=[anywhere] * (LAYERS + 2) + weight_specs + [
            whole(gain.shape), of_layer(nxt), of_layer(nht), of_layer(r),
            *group_params(early), *group_params(late),
            pl.BlockSpec((pieces, 1, 8, 2 * LANES), lambda ph, i: (0, LAYERS - 1 - ph, 0, 0)),
            whole(csw.shape), whole(csb.shape),
            whole(keep.shape), whole(biast.shape), whole(carried.shape), whole(tail.shape), whole(kept.shape),
            block(tokens, early), block(ext, early), block(tokens, early), block(ext, late),
            pl.BlockSpec((None, 1, chunks, STATE, GC), lambda ph, i: (LAYERS - 1 - ph, late(i), 0, 0, 0)),
            of_layer(shared), of_layer(step_in),
        ],
        out_specs=[
            whole((tokens, depth)), whole((LAYERS, 2, share, wide)), whole((LAYERS, share, wide)),
            whole((LAYERS, share, 2 * STATE + LANES)),
            whole((LAYERS, columns * 8, LANES)), whole((LAYERS, 16, GC)), anywhere,
        ],
        out_shape=[
            jax.ShapeDtypeStruct((tokens, depth), F32),
            jax.ShapeDtypeStruct((LAYERS, 2, share, wide), F32),
            jax.ShapeDtypeStruct((LAYERS, share, wide), F32),
            jax.ShapeDtypeStruct((LAYERS, share, 2 * STATE + LANES), F32),
            jax.ShapeDtypeStruct((LAYERS, columns * 8, LANES), F32),
            jax.ShapeDtypeStruct((LAYERS, 16, GC), F32),
            jax.ShapeDtypeStruct((tokens, depth), F32),
        ],
        scratch_shapes=[
            pltpu.VMEM((tokens, depth), BF),
            pltpu.VMEM((depth, tokens), BF),
            pltpu.VMEM((tokens, LANES), F32),
            pltpu.VMEM((chunks, CH, STATE), BF),
            pltpu.VMEM((chunks, CH, STATE), BF),
            pltpu.VMEM((chunks, STATE, CH), BF),
            pltpu.VMEM((chunks, CH, CH), F32),
            pltpu.VMEM((2, tokens, LANES), F32),
            pltpu.VMEM((groups, 8, tokens), F32),
            pltpu.VMEM((3, tokens, 2 * LANES), BF),
            pltpu.VMEM((groups, 8, GC), F32),
            pltpu.VMEM((slots, tokens, GC), BF),
            pltpu.VMEM((slots, tokens, GC), F32),
            pltpu.VMEM((slots, tokens, GC), F32),
            pltpu.VMEM((slots, tokens, GC), BF),
            pltpu.VMEM((slots, STATE, GC), F32),
            pltpu.VMEM((LAYERS, groups, STATE, GC), BF),
            pltpu.VMEM((groups, STATE, GC), BF),
            pltpu.VMEM((HALO, depth), F32),
            pltpu.VMEM((chunks, CH, STATE), F32),
            pltpu.VMEM((chunks, CH, STATE), F32),
            pltpu.VMEM((chunks, CH, CH), F32),
            pltpu.VMEM((tokens, LANES), F32),
            pltpu.VMEM((tokens, LANES), F32),
            pltpu.VMEM((tokens, LANES), F32),
            pltpu.VMEM((8, LANES), F32),
            pltpu.VMEM((tokens, GC), F32),
            pltpu.VMEM((tokens, GC), BF),
            pltpu.VMEM((LAYERS, HALO, depth), F32),
            pltpu.VMEM((groups, 2) + (2,) * bits + (3 * share, LANES), BF),
            pltpu.VMEM((2,) * bits + (share, 2 * STATE + LANES), BF),
            pltpu.VMEM((LAYERS, pieces, 2 * groups // pieces, 3 * share, LANES), BF),
            pltpu.VMEM((LAYERS, pieces, share, 2 * STATE + LANES), BF),
            pltpu.SemaphoreType.DMA,
            pltpu.SemaphoreType.DMA((LAYERS,)),
            pltpu.SemaphoreType.DMA((groups,)),
            pltpu.SemaphoreType.DMA((LAYERS, groups)),
            pltpu.SemaphoreType.DMA((groups, bits, 2)),
            pltpu.SemaphoreType.DMA((groups, bits, 2)),
            pltpu.SemaphoreType.DMA((groups, 2)),
            pltpu.SemaphoreType.DMA((LAYERS, pieces, 2 * groups // pieces)),
            pltpu.SemaphoreType.DMA((bits,)),
            pltpu.SemaphoreType.DMA((bits,)),
            pltpu.SemaphoreType.DMA((pieces,)),
            pltpu.SemaphoreType.DMA((LAYERS, pieces)),
            pltpu.SemaphoreType.DMA,
            pltpu.SemaphoreType.DMA((2, depth // GC)),
            pltpu.VMEM((8, LANES), F32),
            pltpu.VMEM(row_shape, F32),
            pltpu.VMEM((bits + 1,) + row_shape, F32),
            pltpu.VMEM((bits,) + row_shape, F32),
            pltpu.VMEM((LAYERS, pieces) + row_shape[2:], F32),
            pltpu.VMEM((bits + 1,) + few_shape, F32),
            pltpu.VMEM((bits,) + few_shape, F32),
            pltpu.VMEM((LAYERS, pieces) + few_shape, F32),
            pltpu.VMEM((bits + 1,) + few_shape, F32),
            pltpu.VMEM((bits,) + few_shape, F32),
            pltpu.VMEM((LAYERS, pieces) + few_shape, F32),
            pltpu.SemaphoreType.DMA((3, bits)),
            pltpu.SemaphoreType.DMA((3, bits)),
            pltpu.SemaphoreType.DMA((3, pieces)),
            pltpu.SemaphoreType.DMA((LAYERS, 3, pieces)),
            *[pltpu.VMEM((SLOTS, 2) + dims_left + (3 * share, LANES), BF) for dims_left in halves_of],
            *[pltpu.VMEM(dims_left + (share, 2 * STATE + LANES), BF) for dims_left in halves_of],
        ],
        compiler_params=pltpu.CompilerParams(
            collective_id=3, has_side_effects=True, vmem_limit_bytes=VMEM_LIMIT, dimension_semantics=("arbitrary", "arbitrary")
        ),
        name="layers_backward",
    )(
        g, *line, *weight_args, gain, nxt, nht, r, pack, pack, pack, pack, pack, csw, csb, keep, biast, carried, tail,
        kept, gate, val, y, val, states, shared, step_in,
    )


def near_first(z, pieces):
    table = [sorted(range(pieces), key=lambda k: (abs(k - at), k > at)) for at in range(pieces)]
    return [sum(jnp.where(z == at, table[at][p], 0) for at in range(pieces)) for p in range(pieces)]


class Line:
    def __init__(self, place, z, pieces, mine, wall, own_sem, z_send, z_recv):
        self.place, self.z, self.pieces, self.mine, self.wall = place, z, pieces, mine, wall
        self.z_send, self.z_recv = z_send, z_recv
        self.order = near_first(z, pieces)
        self.own = pltpu.make_async_copy(mine, wall.at[place.mine() + (z,)], own_sem)

    def z_copy(self, zi, up):
        src = self.mine if zi is self.z else self.wall.at[self.place.mine() + (zi,)]
        return pltpu.make_async_remote_copy(
            src_ref=src, dst_ref=self.wall.at[self.place.mine() + (zi,)], send_sem=self.z_send.at[int(up), zi],
            recv_sem=self.z_recv.at[zi], device_id={"tensor": self.z + (1 if up else -1)}, device_id_type=MESH,
        )

    def pass_on(self, zi, act):
        z, last = self.z, self.pieces - 1

        @pl.when(jnp.logical_and(zi <= z, z < last))
        def _():
            act(self.z_copy(zi, True))

        @pl.when(jnp.logical_and(zi >= z, z > 0))
        def _():
            act(self.z_copy(zi, False))

    def start(self):
        self.pass_on(self.z, lambda copy: copy.start())
        self.own.start()

    def arrive(self, p):
        zi = self.order[p]
        pltpu.make_async_remote_copy(
            src_ref=self.mine, dst_ref=self.wall.at[self.place.mine() + (zi,)], send_sem=self.z_send.at[0, zi],
            recv_sem=self.z_recv.at[zi], device_id={"tensor": zi}, device_id_type=MESH,
        ).wait_recv()
        self.pass_on(zi, lambda copy: copy.start())

    def finish(self):
        for p in range(self.pieces):
            self.pass_on(self.order[p], lambda copy: copy.wait_send())


class Plane:
    def __init__(self, place, z, pieces, mine, wall, few, few_z, few_all, *sems):
        self.place, self.z, self.pieces, self.bits = place, z, pieces, place.bits
        self.mine, self.wall, self.few, self.few_z, self.few_all = mine, wall, few, few_z, few_all
        self.d_send, self.d_recv, self.t_send, self.t_recv, self.f_send, self.f_recv = sems
        wide = wall.shape[-1]
        self.cols = [pl.ds(0, wide // 2), pl.ds(wide // 2, wide // 2)]
        self.few_cols = [pl.ds(0, 2 * STATE), pl.ds(2 * STATE, LANES)]
        self.order = near_first(z, pieces)
        rest = list(range(1, self.bits))
        self.paths = [rest + [0], rest[::-1] + [0]]

    def d_copy(self, p, half, step):
        path = self.paths[half]
        cols = (slice(None), slice(None), self.cols[half])
        ref = self.wall.at[self.place.along(path[:step]) + (self.order[p],) + cols]
        return pltpu.make_async_remote_copy(
            src_ref=self.mine.at[cols] if self.mine is not None and p + step == 0 else ref, dst_ref=ref,
            send_sem=self.d_send.at[p, half, step], recv_sem=self.d_recv.at[p, half, step],
            device_id={"dp": self.place.flip(path[step])}, device_id_type=MESH,
        )

    def line_copy(self, k):
        return pltpu.make_async_remote_copy(
            src_ref=self.few.at[:, self.few_cols[1]], dst_ref=self.few_z.at[self.z], send_sem=self.t_send.at[k],
            recv_sem=self.t_recv.at[k], device_id={"tensor": lax.rem(self.z + k, self.pieces)}, device_id_type=MESH,
        )

    def few_copy(self, half, step):
        path = self.paths[half]
        ref = self.few_all.at[self.place.along(path[:step]) + (slice(None), self.few_cols[half])]
        return pltpu.make_async_remote_copy(
            src_ref=ref, dst_ref=ref, send_sem=self.f_send.at[half, step], recv_sem=self.f_recv.at[half, step],
            device_id={"dp": self.place.flip(path[step])}, device_id_type=MESH,
        )

    def few_event(self, step):
        if step == 0:
            total = self.few[:, self.few_cols[1]]
            for k in range(1, self.pieces):
                self.line_copy(k).wait_recv()
                total = total + self.few_z[lax.rem(self.z + self.pieces - k, self.pieces)]
            self.few_all[self.place.mine()] = jnp.concatenate([self.few[:, self.few_cols[0]], total], axis=1)
        for half in range(2):
            if step:
                self.few_copy(half, step - 1).wait_recv()
            if step < self.bits:
                self.few_copy(half, step).start()

    def start(self, p):
        for half in range(2):
            self.d_copy(p, half, 0).start()

    def start_few(self):
        for k in range(1, self.pieces):
            self.line_copy(k).start()

    def double(self, p, step):
        for half in range(2):
            self.d_copy(p, half, step - 1).wait_recv()
            if step < self.bits:
                self.d_copy(p, half, step).start()

    def finish(self):
        for p in range(self.pieces):
            for half in range(2):
                for step in range(self.bits):
                    self.d_copy(p, half, step).wait_send()
        for k in range(1, self.pieces):
            self.line_copy(k).wait_send()
        for half in range(2):
            for step in range(self.bits):
                self.few_copy(half, step).wait_send()


def greet(place, z, pieces):
    barrier = pltpu.get_barrier_semaphore()
    for b in range(place.bits):
        pl.semaphore_signal(barrier, inc=1, device_id={"dp": place.flip(b)}, device_id_type=MESH)
    for k in range(1, pieces):
        pl.semaphore_signal(barrier, inc=1, device_id={"tensor": lax.rem(z + k, pieces)}, device_id_type=MESH)
    pl.semaphore_wait(barrier, place.bits + pieces - 1)


def write_masks(z, tokens, starts_ref, keep_ref, bias_ref, biast_ref, carried_ref, tail_ref, kept_ref):
    first = z * tokens

    def label(position):
        total = None
        for k in range(starts_ref.shape[1]):
            term = jnp.where(position >= starts_ref[0, k], 1.0, 0.0)
            total = term if total is None else total + term
        return total

    def same(a, b):
        return jnp.where(a == b, 1.0, 0.0)

    for c in range(tokens // CH):
        begin = first + c * CH
        down = iota2((CH, LANES), 0) + begin
        across = iota2((CH, LANES), 1) + begin
        own, other = label(down), label(across)
        rows = pl.ds(c * CH, CH)
        for k in range(1, 4):
            keep_ref[k - 1, rows, :] = same(label(down - k), own)
        equal = own == other
        bias_ref[c] = jnp.where(equal, jnp.where(down >= across, 0.0, NEG), NEG)
        biast_ref[c] = jnp.where(equal, jnp.where(down <= across, 0.0, NEG), NEG)
        flat = jnp.zeros((CH, LANES), jnp.int32) + begin
        before, final = label(flat - 1), label(flat + (CH - 1))
        carried_ref[rows, :] = same(own, before)
        tail_ref[rows, :] = same(own, final)
        kept_ref[pl.ds(c, 1), :] = same(final, before)[:1]
    kept_ref[pl.ds(tokens // CH, 8 - tokens // CH), :] = jnp.zeros((8 - tokens // CH, LANES), F32)


def gather_kernel(
    dims, starts, tokens_ref, cotangent_ref, cvw, cvb, gate_gain, skip, bias_in, decay, bc, dt, mine, later,
    wall, wall_later, x_all, g_all, few_out, few_later, pack_out, keep, bias, biast, carried, tail, kept,
    x_wide, g_wide, pack, pack_all, few, few_z, few_all, wide_sem, pk_send, pk_recv, *sems,
):
    pieces, tokens, bits = dims
    place = Place(bits)
    z = lax.axis_index("tensor")
    greet(place, z, pieces)
    line = Line(place, z, pieces, mine, wall, *sems[:3])
    line_later = Line(place, z, pieces, later, wall_later, *sems[3:6])
    plane = Plane(place, z, pieces, mine, wall, few, few_z, few_all, *sems[6:])

    heads = skip.shape[1]
    upper_half = z >= pieces // 2
    first = HG * jnp.where(upper_half, pieces - 1 - z, z) + jnp.where(upper_half, HG // 2, 0)

    def lane_of(head):
        return first + HG * (pieces // 2) * (head // 2) + head % 2

    def spot(ref, layer):
        lane = iota2((1, LANES), 1)
        total = jnp.zeros((1, LANES), F32)
        for head in range(heads):
            total = jnp.where(lane == lane_of(head), ref[layer : layer + 1, head : head + 1], total)
        return total

    low, high = iota2((heads, LANES), 0), iota2((heads, LANES), 1)
    chosen = (lane_of(0) + HG * (pieces // 2) * (low // 2) + low % 2 == high).astype(F32).astype(BF)
    for layer in range(LAYERS):
        wide = jnp.concatenate([bc[layer], dot_nn(dt[layer], chosen).astype(BF)], axis=1)
        if layer == 0:
            few[...] = wide
        else:
            few_later[...] = wide
    plane.start(0)
    line.start()
    plane.start_few()
    channel = iota2((1, cvb.shape[1]), 1) // HD
    for layer in range(LAYERS):
        skips = jnp.zeros(channel.shape, F32)
        for head in range(heads):
            skips = jnp.where(channel == head, skip[layer : layer + 1, head : head + 1], skips)
        own = slice(layer, layer + 1)
        rest = jnp.zeros((1, cvb.shape[1] - 2 * LANES), F32)
        tail_row = jnp.concatenate([spot(bias_in, layer), spot(decay, layer), rest], axis=1)
        pack[layer] = jnp.concatenate([cvw[layer], cvb[own], gate_gain[own], skips, tail_row], axis=0)

    def pack_copy(k):
        return pltpu.make_async_remote_copy(
            src_ref=pack, dst_ref=pack_all.at[z], send_sem=pk_send.at[k], recv_sem=pk_recv.at[k],
            device_id={"tensor": lax.rem(z + k, pieces)}, device_id_type=MESH,
        )

    for k in range(1, pieces):
        pack_copy(k).start()
    pack_all[z] = pack[...]
    wides = []
    for k, (narrow, wide, out) in enumerate(((tokens_ref, x_wide, x_all), (cotangent_ref, g_wide, g_all))):
        wide[...] = narrow[...].astype(F32)
        wides.append(pltpu.make_async_copy(wide, out, wide_sem.at[k]))
        wides[k].start()
    write_masks(z, tokens, starts, keep, bias, biast, carried, tail, kept)

    def arrive(p):
        line.arrive(p)
        plane.start(p)
        if p == min(2, pieces - 1):
            line_later.start()

    def double(p, step):
        if p == 0 and step == 1:
            line.own.wait()
        plane.double(p, step)

    events = []
    for p in range(pieces):
        if p:
            events.append((10.0 * p, partial(arrive, p)))
            events.append((10.0 * (2 + p) + 5.0, partial(line_later.arrive, p)))
        for step in range(1, bits + 1):
            late = 0.0 if step < bits - 1 else 0.8
            events.append((10.0 * p + 9.5 * step + late, partial(double, p, step)))
    for step in range(bits + 1):
        events.append((12.0 + 10.0 * step, partial(plane.few_event, step)))
    for _, act in sorted(events, key=lambda event: event[0]):
        act()
    line_later.own.wait()
    line.finish()
    line_later.finish()
    plane.finish()
    for copy in wides:
        copy.wait()
    for k in range(1, pieces):
        pack_copy(k).wait()
    few_out[...] = few_all[...]
    pack_out[...] = pack_all[...]


def line_sems(pieces):
    dma = pltpu.SemaphoreType.DMA
    return [dma, dma((2, pieces)), dma((pieces,))]


def plane_scratch(pieces, bits, share):
    dma = pltpu.SemaphoreType.DMA
    return [pltpu.VMEM((pieces, share, LANES), BF), pltpu.VMEM((2,) * bits + (share, 2 * STATE + LANES), BF)], [
        dma((pieces, 2, bits)), dma((pieces, 2, bits)), dma((pieces,)), dma((pieces,)), dma((2, bits)), dma((2, bits)),
    ]


def gather_first(dims, starts, x, g, params, bc, dt, share, later):
    pieces, tokens, bits = dims
    cut = (2,) * bits
    chunks = tokens // CH
    dma = pltpu.SemaphoreType.DMA
    anywhere = pl.BlockSpec(memory_space=pl.ANY)
    near = pl.BlockSpec(memory_space=pltpu.VMEM)
    buffers, sems = plane_scratch(pieces, bits, share.shape[1])
    pack = (LAYERS, 8, params[1].shape[1])
    few = (share.shape[1], 2 * STATE + LANES)
    return pl.pallas_call(
        partial(gather_kernel, dims),
        in_specs=[pl.BlockSpec(memory_space=pltpu.SMEM)] + [near] * 12,
        out_specs=[anywhere] * 4 + [near] * 9,
        out_shape=[
            jax.ShapeDtypeStruct(cut + (pieces,) + share.shape, BF),
            jax.ShapeDtypeStruct(cut + (pieces,) + share.shape, BF),
            jax.ShapeDtypeStruct(x.shape, F32),
            jax.ShapeDtypeStruct(g.shape, F32),
            jax.ShapeDtypeStruct(cut + few, BF),
            jax.ShapeDtypeStruct(few, BF),
            jax.ShapeDtypeStruct((pieces,) + pack, F32),
            jax.ShapeDtypeStruct((3, tokens, LANES), F32),
            jax.ShapeDtypeStruct((chunks, CH, CH), F32),
            jax.ShapeDtypeStruct((chunks, CH, CH), F32),
            jax.ShapeDtypeStruct((tokens, LANES), F32),
            jax.ShapeDtypeStruct((tokens, LANES), F32),
            jax.ShapeDtypeStruct((8, LANES), F32),
        ],
        scratch_shapes=[
            pltpu.VMEM(x.shape, F32), pltpu.VMEM(g.shape, F32), pltpu.VMEM(pack, F32), pltpu.VMEM((pieces,) + pack, F32),
            pltpu.VMEM(few, BF),
        ] + buffers + [dma((2,)), dma((pieces,)), dma((pieces,))] + line_sems(pieces) * 2 + sems,
        compiler_params=pltpu.CompilerParams(collective_id=2, has_side_effects=True, vmem_limit_bytes=VMEM_LIMIT),
        name="gather_first",
    )(starts, x, g, *params, bc, dt, share, later)


def local(
    tokens, gate_value_weight, w_bc, w_dt, w_out, norm_gain, conv_value_w, conv_value_b, conv_shared_w, conv_shared_b,
    step_bias, decay_log, skip_gain, gate_gain, starts, cotangent,
):
    pieces, dp = lax.axis_size("tensor"), lax.axis_size("dp")
    z = lax.axis_index("tensor")
    bits = (dp - 1).bit_length()
    count, depth = tokens.shape
    own = conv_value_b.shape[1]
    few = step_bias.shape[1]
    groups = pieces * own // GC
    dims = (pieces, groups, count, pieces - 1)

    shares = [
        jnp.concatenate([jnp.swapaxes(gate_value_weight[layer], 0, 1), w_out[layer][None]], axis=0)
        for layer in range(LAYERS)
    ]
    wall, wall_later, x, grad, few_all, few_later, pack, *masks = gather_first(
        (pieces, count, bits), starts, tokens, cotangent,
        (conv_value_w, conv_value_b, gate_gain, skip_gain, step_bias, decay_log), w_bc, w_dt, *shares,
    )
    line, saved, weights = [x], [], []
    for layer in range(LAYERS):
        weights.append((wall.reshape((dp,) + wall.shape[bits:]), few_all))
        later = (few_later, wall_later) if layer + 1 < LAYERS else None
        x, *saved = layer_forward(
            dims, bits, layer, x, norm_gain, *weights[-1], pack, conv_shared_w, conv_shared_b, masks, later, saved
        )
        if later is not None:
            *saved, few_all, wall = saved
        line.append(x)
    upper_half = z >= pieces // 2
    at = jnp.where(upper_half, pieces - 1 - z, z)

    def own_heads(v):
        v = v[..., : pieces * few].reshape(v.shape[:-1] + (few // 2, pieces // 2, 2, 2))
        v = lax.dynamic_index_in_dim(v, at, axis=v.ndim - 3, keepdims=False)
        v = lax.dynamic_index_in_dim(v, upper_half.astype(jnp.int32), axis=v.ndim - 2, keepdims=False)
        return v.reshape(v.shape[:-2] + (few,))

    grad, gw, go, gm, rows, small, _ = layers_backward(
        dims, bits, grad, line, norm_gain, saved, weights, pack, conv_shared_w, conv_shared_b, masks
    )
    rows = jnp.swapaxes(rows.reshape(LAYERS, -1, 8, LANES), 1, 2).reshape(LAYERS, 8, own)
    gcs, ends = small[:, :8], small[:, 8:]
    cuts = depth // GC
    gheads = own_heads(ends[:, cuts].reshape(LAYERS, 2, LANES))
    return (
        x.astype(BF), grad, jnp.swapaxes(gw, 1, 2), gm[:, :, : 2 * STATE], own_heads(gm[:, :, 2 * STATE :]),
        go, ends[:, :cuts].reshape(LAYERS, depth),
        rows[:, :4], rows[:, 4], gcs[:, :4], gcs[:, 4], gheads[:, 0], gheads[:, 1],
        jnp.sum(rows[:, 6].reshape(LAYERS, few, HD), axis=2), rows[:, 5],
    )


def solution(mesh):
    in_specs = (
        P(("dp", "tensor"), None),
        P(None, "dp", None, "tensor"),
        P(None, "dp", None),
        P(None, "dp", "tensor"),
        P(None, "dp", "tensor"),
        P(),
        P(None, None, "tensor"),
        P(None, "tensor"),
        P(),
        P(),
        P(None, "tensor"),
        P(None, "tensor"),
        P(None, "tensor"),
        P(None, "tensor"),
        P("dp", None),
        P(("dp", "tensor"), None),
    )
    out_specs = (
        P(("dp", "tensor"), None),
        P(("dp", "tensor"), None),
        P(None, "dp", None, "tensor"),
        P(None, "dp", None),
        P(None, "dp", "tensor"),
        P(None, "dp", "tensor"),
        P(),
        P(None, None, "tensor"),
        P(None, "tensor"),
        P(),
        P(),
        P(None, "tensor"),
        P(None, "tensor"),
        P(None, "tensor"),
        P(None, "tensor"),
    )
    return jax.shard_map(local, mesh=mesh, in_specs=in_specs, out_specs=out_specs, check_vma=False)
```

```python
from functools import partial

import jax
import jax.numpy as jnp
from jax import lax
from jax.experimental import pallas as pl
from jax.experimental.pallas import tpu as pltpu
from jax.sharding import PartitionSpec as P

LAYERS = 2
EPS = 1e-05
HALO = 16
CH = 128
TILE = 64
GC = 256
HD = 64
HG = GC // HD
LANES = 128
STATE = 128
NEG = -1e30
SLOTS = 2
VMEM_LIMIT = 60 * 1024 * 1024
VMEM_LIMIT_FORWARD = 62 * 1024 * 1024
MESH = pl.DeviceIdType.MESH
HI = lax.Precision.HIGHEST
F32 = jnp.float32
BF = jnp.bfloat16


def dot_nn(a, b, precision=None):
    return lax.dot_general(a, b, (((1,), (0,)), ((), ())), precision=precision, preferred_element_type=F32)


def dot_nt(a, b):
    return lax.dot_general(a, b, (((1,), (1,)), ((), ())), preferred_element_type=F32)


def dot_tn(a, b):
    return lax.dot_general(a, b, (((0,), (0,)), ((), ())), preferred_element_type=F32)


def sigmoid(v):
    return 0.5 * jnp.tanh(0.5 * v) + 0.5


def twice(v):
    return jnp.concatenate([v, v], axis=1)


def split2(v):
    high = v.astype(BF)
    return jnp.concatenate([high, (v - high.astype(F32)).astype(BF)], axis=1)


def iota2(shape, dim):
    return lax.broadcasted_iota(jnp.int32, shape, dim)


def spread(group):
    row = iota2((2 * LANES, GC), 0) % LANES
    head = iota2((2 * LANES, GC), 1) // HD + group * HG
    return (row == head).astype(F32).astype(BF)


def collect(group):
    head = (iota2((2 * GC, LANES), 0) % GC) // HD + group * HG
    return (head == iota2((2 * GC, LANES), 1)).astype(F32).astype(BF)


def conv(load, keep_ref, weights, tokens):
    return conv_rows(load, keep_ref, weights, pl.ds(0, tokens))


def conv_rows(load, keep_ref, weights, rows):
    total = weights[4:5] + weights[0:1] * load(0)
    for k in range(1, 4):
        total = total + weights[k : k + 1] * (load(k) * twice(keep_ref[k - 1, rows, :]))
    return total


def tiles(tokens):
    return range(0, tokens, TILE)


def conv_back(grad, load, keep_ref, weights, tokens):
    rows = []
    total = None
    for k in range(4):
        part = grad if k == 0 else grad * twice(keep_ref[k - 1])
        rows.append(jnp.sum(part * load(k), axis=0, keepdims=True))
        wide = jnp.concatenate([jnp.zeros((HALO, grad.shape[1]), F32), weights[k : k + 1] * part], axis=0)
        if k:
            wide = pltpu.roll(wide, tokens + HALO - k, 0)
        total = wide if total is None else total + wide
    rows.append(jnp.sum(grad, axis=0, keepdims=True))
    return total, rows


def step_terms(step_in, heads_ref, carried_ref, tail_ref, kept_ref, tokens):
    chunks = tokens // CH
    raw = step_in + heads_ref[0:1]
    steps = jnp.maximum(raw, 0.0) + jnp.log1p(jnp.exp(-jnp.abs(raw)))
    rates = -steps * heads_ref[1:2]
    lower = (iota2((CH, CH), 0) >= iota2((CH, CH), 1)).astype(F32)
    sums, toward, kept = [], [], []
    for c in range(chunks):
        summed = dot_nn(lower, rates[c * CH : (c + 1) * CH], HI)
        last = summed[CH - 1 : CH]
        sums.append(summed)
        toward.append(jnp.exp(last - summed))
        kept.append(jnp.exp(last) * kept_ref[c : c + 1])
    kept.append(jnp.zeros((8 - chunks, LANES), F32))
    summed = jnp.concatenate(sums, axis=0)
    toward = jnp.concatenate(toward, axis=0) * tail_ref[...]
    reach = jnp.exp(summed) * carried_ref[...]
    return raw, steps, rates, summed, toward, reach, jnp.concatenate(kept, axis=0)


def put_sums(summed, col_ref, row_ref, groups, tokens):
    for c in range(tokens // CH):
        turned = summed[c * CH : (c + 1) * CH].T
        for group in range(groups):
            row_ref[group, 0:HG, c * CH : (c + 1) * CH] = turned[group * HG : (group + 1) * HG]
    col_ref[0] = summed


def turn_sums(col_ref, group):
    col_ref[1] = pltpu.roll(col_ref[0], lax.rem(LANES - group * HG, LANES), 1)


def put_heads(rows_ref, heads_ref):
    total = rows_ref[0, 0, 7:8, :]
    for k in range(1, rows_ref.shape[0]):
        total = total + rows_ref[k, 0, 7:8, :]
    heads_ref[...] = jnp.concatenate(
        [total[:, :LANES], jnp.exp(total[:, LANES:]), jnp.zeros((6, LANES), F32)], axis=0
    )


def shared_taps(csw_ref, csb_ref, layer):
    return jnp.concatenate([csw_ref[layer], csb_ref[layer : layer + 1]], axis=0)


def halves(v):
    first = iota2(v.shape, 1) < HD
    return jnp.concatenate([jnp.where(first, v, 0.0), jnp.where(first, 0.0, v)], axis=0).astype(BF)


def forward_kernel(
    dims,
    x_ref, gain_ref, wa, wb, oa, ob, few_ref, pa, pb, qa, qb, rows_ref, csw_ref, csb_ref,
    keep_ref, bias_ref, carried_ref, tail_ref, kept_ref, *rest,
):
    pieces, groups, tokens, skew, bits, layer, gathers = dims
    if gathers:
        few_mine, _, *rest = rest
    if layer:
        rest = rest[9:]
    next_ref, nxt_ref, nht_ref, gate_ref, val_ref, y_ref, state_ref, shared_ref, step_ref, r_ref, *rest = rest
    if gathers:
        few_out, wall_ref, *rest = rest
    nx, inb, inbt, outb, cross, col, row, terms, ke, intra, xs, gs, fresh, fold, *rest = rest
    incoming, outgoing, branch, squares, heads_ref, halo_send, halo_recv, send, recv, *rest = rest
    if gathers:
        few_z, few_all, *rest = rest
    place = Place(bits)
    chunks = tokens // CH
    i = pl.program_id(0)
    z = lax.axis_index("tensor")
    right, left = jnp.minimum(z + 1, pieces - 1), jnp.maximum(z - 1, 0)

    def halo_copy():
        return pltpu.make_async_remote_copy(
            src_ref=nx.at[pl.ds(tokens, HALO)], dst_ref=nx.at[pl.ds(0, HALO)],
            send_sem=halo_send, recv_sem=halo_recv, device_id={"tensor": right}, device_id_type=MESH,
        )

    def state_copy(group):
        return pltpu.make_async_remote_copy(
            src_ref=outgoing.at[group], dst_ref=incoming.at[group],
            send_sem=send.at[group], recv_sem=recv.at[group], device_id={"tensor": right}, device_id_type=MESH,
        )

    plan = [[] for _ in range(groups + skew)]
    if gathers:
        plane = Plane(place, z, pieces, None, wall_ref, few_mine, few_z, few_all, *rest)
        for step in range(1, bits + 1):
            for p in range(pieces):
                plan[min(4 * step + p - 2, groups + skew - 1)].append(partial(plane.double, p, step))
        for step in range(bits + 1):
            plan[min(2 * step + 1, groups + skew - 1)].append(partial(plane.few_event, step))

    @pl.when(i == 0)
    def _():
        greet(place, z, pieces)
        x = x_ref[...]
        scale = lax.rsqrt(jnp.mean(x * x, axis=1, keepdims=True) + EPS)
        nx[pl.ds(HALO, tokens), :] = (x * scale * gain_ref[layer : layer + 1]).astype(BF)
        put_heads(rows_ref, heads_ref)

        @pl.when(z < pieces - 1)
        def _():
            halo_copy().start()

        if gathers:
            for p in range(pieces):
                plane.start(p)
            plane.start_few()

        @pl.when(z == 0)
        def _():
            nx[pl.ds(0, HALO), :] = jnp.zeros((HALO, nx.shape[1]), BF)
            incoming[...] = jnp.zeros(incoming.shape, BF)

        depth = nx.shape[1]
        step_in = dot_nn(nx[pl.ds(HALO, tokens), :], few_ref[..., 2 * STATE :].reshape(depth, LANES))
        step_ref[...] = step_in
        _, steps, _, summed, toward, reach, kept = step_terms(
            step_in, heads_ref, carried_ref, tail_ref, kept_ref, tokens
        )
        put_sums(summed, col, row, groups, tokens)
        terms[0] = split2(steps)
        terms[1] = split2(toward)
        terms[2] = split2(reach)
        kept2 = split2(kept)
        for group in range(groups):
            ke[group] = dot_nn(kept2, spread(group))

        @pl.when(z > 0)
        def _():
            halo_copy().wait_recv()

        shared_ref[...] = dot_nn(nx[...], few_ref[..., : 2 * STATE].reshape(depth, 2 * STATE))
        taps = shared_taps(csw_ref, csb_ref, layer)
        mixed = conv(lambda k: shared_ref[pl.ds(HALO - k, tokens), :], keep_ref, taps, tokens)
        maps = mixed * sigmoid(mixed)
        for c in range(chunks):
            part = maps[c * CH : (c + 1) * CH]
            into, out = part[:, :STATE], part[:, STATE:].astype(BF)
            inb[c], outb[c], inbt[c] = into.astype(BF), out, into.T.astype(BF)
            cross[c] = dot_nt(out, into.astype(BF))
        branch[...] = jnp.zeros(branch.shape, F32)
        squares[...] = jnp.zeros(squares.shape, F32)

    @pl.when(i < groups)
    def _():
        depth = nx.shape[1]
        group = i
        slot = lax.rem(group, skew + 1)
        gate_ref[0] = dot_nn(nx[pl.ds(HALO, tokens), :], side((wa, wb), 0))
        val_ref[0] = dot_nn(nx[...], side((wa, wb), 1))
        gp = side_params((pa, pb))
        for start in tiles(tokens):
            rows = pl.ds(start, TILE)
            mixed = conv_rows(lambda k: val_ref[0, pl.ds(HALO + start - k, TILE), :], keep_ref, gp, rows)
            xs[slot, rows, :] = mixed * sigmoid(mixed)
            gate = gate_ref[0, rows, :]
            gs[slot, rows, :] = gate * sigmoid(gate)
        turn_sums(col, group)
        spreader = spread(group)
        state = jnp.zeros((STATE, GC), F32)
        for c in range(chunks):
            rows = pl.ds(c * CH, CH)
            sized = xs[slot, rows, :] * dot_nn(terms[0, rows, :], spreader)
            weighted = (sized * dot_nn(terms[1, rows, :], spreader)).astype(BF)
            new = dot_nn(inbt[c], weighted)
            fresh[slot, c] = new
            state = ke[group, c : c + 1] * state + new
            for pair in range(HG // 2):
                lanes = pl.ds(pair * LANES, LANES)
                decayed = []
                for j in (2 * pair, 2 * pair + 1):
                    across = col[1, rows, j : j + 1] - row[group, j : j + 1, rows]
                    decayed.append((cross[c] * jnp.exp(jnp.minimum(across, bias_ref[c]))).astype(BF))
                blocks = halves(sized[:, pair * LANES : (pair + 1) * LANES])
                intra[slot, rows, lanes] = dot_nn(jnp.concatenate(decayed, axis=1), blocks)
        fold[slot] = state

    j = i - z

    @pl.when(jnp.logical_and(j >= 0, j < groups))
    def _():
        @pl.when(z > 0)
        def _():
            state_copy(j).wait_recv()

        @pl.when(z < pieces - 1)
        def _():
            total = ke[j, 0:1]
            for c in range(1, chunks):
                total = total * ke[j, c : c + 1]
            outgoing[j] = (total * incoming[j].astype(F32) + fold[lax.rem(j, skew + 1)]).astype(BF)
            state_copy(j).start()

    @pl.when(i >= skew)
    def _():
        group = i - skew
        slot = lax.rem(group, skew + 1)
        depth = nx.shape[1]
        spreader = spread(group)
        gp = side_params((qa, qb))
        state = incoming[group].astype(F32)
        for c in range(chunks):
            rows = pl.ds(c * CH, CH)
            low = state.astype(BF)
            state_ref[0, c] = low
            y = intra[slot, rows, :] + dot_nn(outb[c], low) * dot_nn(terms[2, rows, :], spreader)
            y_ref[0, rows, :] = y
            gated = (y + gp[6:7] * xs[slot, rows, :]) * gs[slot, rows, :]
            squares[rows, :] += jnp.sum(gated * gated, axis=1, keepdims=True)
            intra[slot, rows, :] = gated * gp[5:6]
            if c < chunks - 1:
                state = ke[group, c : c + 1] * state + fresh[slot, c]
        branch[...] += dot_nt(intra[slot].astype(BF), side((oa, ob), 0))

    for step, acts in enumerate(plan):
        if acts:

            @pl.when(i == step)
            def _(acts=acts):
                for act in acts:
                    act()

    @pl.when(i == groups + skew - 1)
    def _():
        inner = groups * GC
        factor = lax.rsqrt(squares[...] * (1.0 / inner) + EPS)
        r_ref[...] = factor
        next_ref[...] = x_ref[...] + branch[...] * factor[:, 0:1]
        nxt_ref[...] = nx[pl.ds(HALO, tokens), :].T
        nht_ref[...] = nx[pl.ds(0, HALO), :].T
        if gathers:
            plane.finish()
            few_out[...] = few_all[...]

        @pl.when(z < pieces - 1)
        def _():
            halo_copy().wait_send()
            for group in range(groups):
                state_copy(group).wait_send()


class Place:
    def __init__(self, bits):
        self.bits = bits
        self.index = lax.axis_index("dp")
        self.bit = [lax.rem(self.index // (1 << b), 2) for b in range(bits)]
        self.dims = (2,) * bits
        self.all = (slice(None),) * bits

    def flip(self, b):
        return self.index + (1 << b) * (1 - 2 * self.bit[b])

    def along(self, done):
        return tuple(slice(None) if b in done else self.bit[b] for b in reversed(range(self.bits)))

    def order(self, odd):
        rest = list(range(1, self.bits))
        return [0] + (rest[::-1] if odd else rest)

    def partner(self, odd, step):
        return self.flip(self.order(odd)[step])

    def region(self, odd, step, keep):
        order = self.order(odd)
        at = []
        for b in reversed(range(self.bits)):
            if b in order[:step]:
                at.append(self.bit[b])
            elif b == order[step]:
                at.append(self.bit[b] if keep else 1 - self.bit[b])
            else:
                at.append(slice(None))
        return tuple(at)

    def mine(self):
        return tuple(self.bit[b] for b in reversed(range(self.bits)))


def backward_kernel(
    dims,
    g_ref, *refs,
):
    pieces, groups, tokens, skew, bits = dims
    line_refs, refs = refs[: LAYERS + 1], refs[LAYERS + 1 :]
    weights, refs = [refs[5 * n : 5 * n + 5] for n in range(LAYERS)], refs[5 * LAYERS :]
    gain_ref, nxt, nht, r_ref, pa, pb, qa, qb, rows_ref, *refs = refs
    csw_ref, csb_ref, keep_ref, biast_ref, carried_ref, tail_ref, kept_ref, *refs = refs
    gate_ref, val_ref, y_ref, valb_ref, state_ref, shared_ref, step_ref, *refs = refs
    gx_ref, gw_ref, go_ref, gm_ref, rows_ref_out, small_ref, mid_ref, *refs = refs
    gb, gbt, r2, inb, outb, outbt, crosst, col, row, terms, ke, *refs = refs
    dys, xs, fs, dgs, fold, incoming, outgoing, gnorm, dct, dbt, dgt, sd, sp, sq, se, dxd, turned, hrecv, *refs = refs
    own, own_m, got_z, got_m, halo_send, halo_recv, send, recv, sum_send, sum_recv, z_send, z_recv, *refs = refs
    msum_send, msum_recv, mz_send, mz_recv, next_sem, load_sem, heads_ref, *refs = refs
    rows_now, row_total, row_got, row_z, map_total, map_got, map_z, end_total, end_got, end_z, *refs = refs
    few_send, few_recv, fz_send, fz_recv, *got = refs
    chunks = tokens // CH
    phase, i = pl.program_id(0), pl.program_id(1)
    layer = LAYERS - 1 - phase
    z = lax.axis_index("tensor")
    right, left = jnp.minimum(z + 1, pieces - 1), jnp.maximum(z - 1, 0)
    back = pieces - 1 - z
    depth = gb.shape[1]
    inner = groups * GC

    def halo_copy():
        return pltpu.make_async_remote_copy(
            src_ref=gnorm, dst_ref=hrecv.at[phase], send_sem=halo_send, recv_sem=halo_recv.at[phase],
            device_id={"tensor": left}, device_id_type=MESH,
        )

    def state_copy(group):
        return pltpu.make_async_remote_copy(
            src_ref=outgoing.at[group], dst_ref=incoming.at[phase, group],
            send_sem=send.at[group], recv_sem=recv.at[phase, group], device_id={"tensor": left}, device_id_type=MESH,
        )

    place = Place(bits)
    parts, parts_m = got[:bits], got[bits:]

    def part(step, group, half):
        return lax.rem(group, SLOTS), half

    def held(step, group, half, keep):
        return (group, half) + place.region(half, step, keep)

    def put_gradient(group, which, value):
        rows = own.shape[-2] // 3
        for half in range(2):
            cut = value[:, half * LANES : (half + 1) * LANES].astype(BF).reshape(place.dims + (rows, LANES))
            own[(group, half) + place.all + (pl.ds(which * rows, rows),)] = cut

    def sum_copy(group, step, half):
        return pltpu.make_async_remote_copy(
            src_ref=own.at[held(step, group, half, False)], dst_ref=parts[step].at[part(step, group, half)],
            send_sem=sum_send.at[group, step, half], recv_sem=sum_recv.at[group, step, half],
            device_id={"dp": place.partner(half, step)}, device_id_type=MESH,
        )

    def z_copy(group, half, turn):
        column = lax.div(group, pieces // 2)
        return pltpu.make_async_remote_copy(
            src_ref=own.at[(group, half) + place.mine()],
            dst_ref=got_z.at[turn, z, column], send_sem=z_send.at[group, half], recv_sem=z_recv.at[turn, z, column],
            device_id={"tensor": quarter(group, half, pieces)}, device_id_type=MESH,
        )

    def advance(group, step, turn):
        @pl.when(jnp.logical_and(group >= 0, group < groups))
        def _():
            for half in range(2):
                if step:
                    sum_copy(group, step - 1, half).wait_recv()
                    at = held(step - 1, group, half, True)
                    own[at] = own[at] + parts[step - 1][part(step - 1, group, half)]
                if step < bits:
                    sum_copy(group, step, half).start()
                if step == bits:

                    @pl.when(quarter(group, half, pieces) != z)
                    def _(half=half):
                        z_copy(group, half, turn).start()

    def misc_copy(step):
        return pltpu.make_async_remote_copy(
            src_ref=own_m.at[place.region(False, step, False)], dst_ref=parts_m[step],
            send_sem=msum_send.at[step], recv_sem=msum_recv.at[step],
            device_id={"dp": place.partner(False, step)}, device_id_type=MESH,
        )

    def misc_z(k, turn, source):
        return pltpu.make_async_remote_copy(
            src_ref=own_m.at[place.mine()], dst_ref=got_m.at[turn, source], send_sem=mz_send.at[k],
            recv_sem=mz_recv.at[turn, source],
            device_id={"tensor": lax.rem(z + k, pieces)}, device_id_type=MESH,
        )

    def misc_advance(step, turn):
        if step:
            misc_copy(step - 1).wait_recv()
            at = place.region(False, step - 1, True)
            own_m[at] = own_m[at] + parts_m[step - 1][...]
        if step < bits:
            misc_copy(step).start()
        else:
            for k in range(1, pieces):
                misc_z(k, turn, z).start()
            got_m[turn, z] = own_m[place.mine()]

    def drain(late, turn):
        for step in reversed(range(1, bits + 1)):
            if late <= step:
                advance(jnp.int32(groups - 1 + late - step), step, turn)

    def put_rows(group, rows, adds):
        rows = jnp.concatenate(rows, axis=0)
        at = lax.rem(group, pieces // 2), pl.ds(pl.multiple_of(lax.div(group, pieces // 2) * 8, 8), 8)
        for half in range(2):
            cut = rows[:, half * LANES : (half + 1) * LANES]
            if adds:
                cut = cut + rows_now[at[0], half, at[1], :]
            rows_now[at[0], half, at[1], :] = cut

    def quarter_of(at):
        upper_half = at >= pieces // 2
        return jnp.where(upper_half, pieces - 1 - at, at), jnp.where(upper_half, 1, 0)

    def few_copies(step, early):
        refs = [(row_total, row_got), (map_total, map_got)] if early else [(end_total, end_got)]
        first = 0 if early else 2
        return [
            pltpu.make_async_remote_copy(
                src_ref=total.at[step], dst_ref=other.at[step], send_sem=few_send.at[first + n, step],
                recv_sem=few_recv.at[first + n, step], device_id={"dp": place.partner(False, step)}, device_id_type=MESH,
            )
            for n, (total, other) in enumerate(refs)
        ]

    def few_lines(k, turn, source, early):
        target = lax.rem(z + k, pieces)
        pairs = [(end_total.at[bits], end_z)]
        if early:
            pairs = [(row_total.at[(bits,) + quarter_of(target)], row_z), (map_total.at[bits], map_z)]
        first = 0 if early else 2
        return [
            pltpu.make_async_remote_copy(
                src_ref=ref, dst_ref=other.at[turn, source], send_sem=fz_send.at[first + n, k],
                recv_sem=fz_recv.at[turn, first + n, source], device_id={"tensor": target}, device_id_type=MESH,
            )
            for n, (ref, other) in enumerate(pairs)
        ]

    def few_advance(step, turn, early):
        if step:
            for copy in few_copies(step - 1, early):
                copy.wait_recv()
            for total, other in [(row_total, row_got), (map_total, map_got)] if early else [(end_total, end_got)]:
                total[step] = total[step - 1] + other[step - 1]
        if step < bits:
            for copy in few_copies(step, early):
                copy.start()
        else:
            for k in range(1, pieces):
                for copy in few_lines(k, turn, z, early):
                    copy.start()
            if early:
                row_z[turn, z] = row_total[(bits,) + quarter_of(z)]
                map_z[turn, z] = map_total[bits]
            else:
                end_z[turn, z] = end_total[bits]

    def finish_few(turn):
        for n in range(1, pieces):
            source = lax.rem(z + n, pieces)
            for copy in few_lines(n, turn, source, True) + few_lines(n, turn, source, False):
                copy.wait_recv()
            misc_z(n, turn, source).wait_recv()
        misc = got_m[turn, 0].astype(F32)
        sums = [ref[turn, 0] for ref in (row_z, map_z, end_z)]
        for source in range(1, pieces):
            sums = [total + ref[turn, source] for total, ref in zip(sums, (row_z, map_z, end_z))]
            misc = misc + got_m[turn, source].astype(F32)
        layer_done = LAYERS - 1 - turn
        rows_ref_out[layer_done] = sums[0]
        small_ref[layer_done, pl.ds(0, 8), :] = sums[1]
        small_ref[layer_done, pl.ds(8, 8), :] = sums[2]
        gm_ref[layer_done] = misc
        for step in range(bits):
            misc_copy(step).wait_send()
            for copy in few_copies(step, True) + few_copies(step, False):
                copy.wait_send()
        for n in range(1, pieces):
            misc_z(n, turn, z).wait_send()
            for copy in few_lines(n, turn, z, True) + few_lines(n, turn, z, False):
                copy.wait_send()

    def finish_group(group, turn):
        column = lax.div(group, pieces // 2)
        for half in range(2):

            @pl.when(quarter(group, half, pieces) == z)
            def _(half=half):
                total = own[(group, half) + place.mine()].astype(F32)
                for n in range(1, pieces):
                    source = lax.rem(z + n, pieces)
                    pltpu.make_async_remote_copy(
                        src_ref=got_z.at[turn, source, column], dst_ref=got_z.at[turn, source, column],
                        send_sem=z_send.at[group, half], recv_sem=z_recv.at[turn, source, column],
                        device_id={"tensor": source}, device_id_type=MESH,
                    ).wait_recv()
                    total = total + got_z[turn, source, column].astype(F32)
                at = pl.multiple_of(column * LANES, LANES)
                total = total.reshape(3, -1, LANES)
                gw_ref[LAYERS - 1 - turn, :, :, pl.ds(at, LANES)] = total[:2]
                go_ref[LAYERS - 1 - turn, :, pl.ds(at, LANES)] = total[2]

            @pl.when(quarter(group, half, pieces) != z)
            def _(half=half):
                z_copy(group, half, turn).wait_send()

            for step in range(bits):
                sum_copy(group, step, half).wait_send()

    def load(x, g):
        found = []
        for n in range(depth // GC):
            cols = pl.ds(n * GC, GC)
            found.append(pltpu.make_async_copy(x.at[:, cols], xs.at[n], load_sem.at[0, n]))
            if g is not None:
                found.append(pltpu.make_async_copy(g.at[:, cols], fs.at[n], load_sem.at[1, n]))
        return found

    def of_layer(pick):
        chosen = pick(0)
        for n in range(1, LAYERS):
            chosen = jnp.where(layer == n, pick(n), chosen)
        return chosen

    def out_weights():
        return of_layer(lambda n: side(weights[n][2:4], 0))

    def in_weights(which):
        return of_layer(lambda n: side(weights[n][:2], which))

    def taps():
        return jnp.concatenate([csw_ref[layer], csb_ref[pl.ds(layer, 1), :]], axis=0)

    def shared_conv():
        return conv(lambda k: shared_ref[pl.ds(HALO - k, tokens), :], keep_ref, taps(), tokens)

    @pl.when(jnp.logical_and(phase == 0, i == 0))
    def _():
        greet(place, z, pieces)

        @pl.when(z == pieces - 1)
        def _():
            incoming[...] = jnp.zeros(incoming.shape, BF)

        copies = [pltpu.make_async_copy(line_refs[LAYERS], gx_ref, next_sem)] + load(line_refs[LAYERS - 1], g_ref)
        for copy in copies:
            copy.start()
        for copy in copies:
            copy.wait()

    for turn in range(1, LAYERS):

        @pl.when(jnp.logical_and(phase == turn, i == 0))
        def _(turn=turn):
            copies = load(line_refs[LAYERS - 1 - turn], None)
            copies.append(pltpu.make_async_copy(gx_ref, mid_ref, next_sem))
            for copy in copies:
                copy.start()
            for n in range(depth // GC):
                fs[n] = gx_ref[:, n * GC : (n + 1) * GC]
            for copy in copies:
                copy.wait()
            copy = pltpu.make_async_copy(line_refs[LAYERS - turn], gx_ref, next_sem)
            copy.start()
            copy.wait()

    @pl.when(i == 0)
    def _():
        put_heads(rows_ref, heads_ref)
        dots = jnp.zeros((tokens, 1), F32)
        for k in range(depth // GC):
            cols = slice(k * GC, (k + 1) * GC)
            low = fs[k].astype(BF)
            gb[:, cols] = low
            gbt[cols, :] = low.T
            dots = dots + jnp.sum(low.astype(F32) * (gx_ref[:, cols] - xs[k]), axis=1, keepdims=True)
        r = r_ref[...]
        r2[...] = r * r * dots * (1.0 / inner)
        _, steps, _, summed, toward, reach, kept = step_terms(
            step_ref[...], heads_ref, carried_ref, tail_ref, kept_ref, tokens
        )
        put_sums(summed, col, row, groups, tokens)
        terms[0] = split2(steps)
        terms[1] = split2(toward)
        terms[2] = split2(reach)
        kept2 = split2(kept)
        for group in range(groups):
            ke[group] = dot_nn(kept2, spread(group))
        mixed = shared_conv()
        maps = mixed * sigmoid(mixed)
        for c in range(chunks):
            part = maps[c * CH : (c + 1) * CH]
            into, out = part[:, :STATE].astype(BF), part[:, STATE:]
            inb[c], outb[c], outbt[c] = into, out.astype(BF), out.T.astype(BF)
            crosst[c] = dot_nt(into, out.astype(BF))
        for ref in (gx_ref, gnorm, dct, dbt, dgt, sd, sp, sq, se):
            ref[...] = jnp.zeros(ref.shape, F32)

    @pl.when(i < groups)
    def _():
        group = i
        slot = lax.rem(group, skew + 1)
        gp = side_params((pa, pb))

        for turn in range(1, LAYERS):

            @pl.when(phase == turn)
            def _(turn=turn):
                finish_group(group, turn - 1)

        dxd[...] = dot_nn(gb[...], out_weights())
        gain_sum = skip_sum = jnp.zeros((1, GC), F32)
        for start in tiles(tokens):
            rows = pl.ds(start, TILE)
            mixed = conv_rows(lambda k: val_ref[0, pl.ds(HALO + start - k, TILE), :], keep_ref, gp, rows)
            part = sigmoid(mixed)
            x = mixed * part
            xs[slot, rows, :] = x
            fs[slot, rows, :] = part + x * (1.0 - part)
            r = twice(r_ref[rows, :])
            gm = dxd[rows, :]
            scan = y_ref[0, rows, :] + gp[6:7] * x
            gate = gate_ref[0, rows, :]
            part = sigmoid(gate)
            silu = gate * part
            gated = scan * silu
            normal = gated * r
            turned[rows, :] = (normal * gp[5:6]).astype(BF)
            ggated = r * gp[5:6] * gm - gated * twice(r2[rows, :])
            dy = ggated * silu
            dys[slot, rows, :] = dy.astype(BF)
            dgs[slot, rows, :] = (ggated * scan * (part + silu * (1.0 - part))).astype(BF)
            gain_sum = gain_sum + jnp.sum(gm * normal, axis=0, keepdims=True)
            skip_sum = skip_sum + jnp.sum(dy * x, axis=0, keepdims=True)
        put_gradient(group, 2, dot_nn(gbt[...], turned[...]))
        put_rows(group, [jnp.zeros((5, GC), F32), gain_sum, skip_sum, jnp.zeros((1, GC), F32)], False)
        spreader, collector = spread(group), collect(group)
        state = jnp.zeros((STATE, GC), F32)
        for c in reversed(range(chunks)):
            rows = pl.ds(c * CH, CH)
            reached = (dys[slot, rows, :].astype(F32) * dot_nn(terms[2, rows, :], spreader)).astype(BF)
            sp[rows, :] += dot_nn(split2(dys[slot, rows, :].astype(F32) * y_ref[0, rows, :]), collector)
            new = dot_nn(outbt[c], reached)
            state = ke[group, c : c + 1] * state + new
        fold[slot] = state

    for turn in range(1, LAYERS):
        for late in range(1, max(bits, skew) + 1):
            place_at = min(late, skew) - 1

            @pl.when(jnp.logical_and(phase == turn, i == place_at))
            def _(turn=turn, late=late):
                drain(late, turn - 1)
                if late <= bits:
                    few_advance(late, turn - 1, True)
                    few_advance(late, turn - 1, False)
                    misc_advance(late, turn - 1)

        @pl.when(jnp.logical_and(phase == turn, i == skew))
        def _(turn=turn):
            finish_few(turn - 1)

    j = i - back

    @pl.when(jnp.logical_and(j >= 0, j < groups))
    def _():
        @pl.when(z < pieces - 1)
        def _():
            state_copy(j).wait_recv()

        @pl.when(z > 0)
        def _():
            total = ke[j, 0:1]
            for c in range(1, chunks):
                total = total * ke[j, c : c + 1]
            outgoing[j] = (total * incoming[phase, j].astype(F32) + fold[lax.rem(j, skew + 1)]).astype(BF)
            state_copy(j).start()

    @pl.when(i >= skew)
    def _():
        group = i - skew
        slot = lax.rem(group, skew + 1)
        gp = side_params((qa, qb))
        spreader, collector = spread(group), collect(group)
        turn_sums(col, group)
        grad = incoming[phase, group].astype(F32)
        ends = [None] * chunks
        for c in reversed(range(chunks)):
            rows = pl.ds(c * CH, CH)
            low = grad.astype(BF)
            state = state_ref[0, c]
            ends[c] = jnp.sum(low.astype(F32) * state.astype(F32), axis=0, keepdims=True) * ke[group, c : c + 1]
            x = xs[slot, rows, :]
            dy = dys[slot, rows, :].astype(F32)
            steps = dot_nn(terms[0, rows, :], spreader)
            toward = dot_nn(terms[1, rows, :], spreader)
            reached = (dy * dot_nn(terms[2, rows, :], spreader)).astype(BF)
            grad = ke[group, c : c + 1] * grad + dot_nn(outbt[c], reached)
            sized = x * steps
            weighted = (sized * toward).astype(BF)
            later = dot_nn(inb[c], low) * toward
            dbt[c] += dot_nt(weighted, low)
            dct[c] += dot_nt(reached, state)
            parts = []
            cross = crosst[c]
            pairs_total = jnp.zeros((CH, CH), F32)
            for pair in range(HG // 2):
                at = slice(pair * LANES, (pair + 1) * LANES)
                dyp = dy[:, at]
                products = dot_nt(halves(sized[:, at]), dyp.astype(BF))
                decayed = []
                for n in range(2):
                    h = 2 * pair + n
                    across = row[group, h : h + 1, rows] - col[1, rows, h : h + 1]
                    decay = jnp.exp(jnp.minimum(across, biast_ref[c]))
                    decayed.append((cross * decay).astype(BF))
                    pairs_total = pairs_total + products[n * CH : (n + 1) * CH] * decay
                parts.append(dot_nn(jnp.concatenate(decayed, axis=1), halves(dyp)))
            dgt[c] += pairs_total
            within = jnp.concatenate(parts, axis=1)
            whole = within + later
            lowered = sized.astype(BF).astype(F32) * within
            sd[rows, :] += dot_nn(split2(whole * x), collector)
            sp[rows, :] -= dot_nn(split2(lowered), collector)
            sq[rows, :] += dot_nn((sized * later).astype(BF), collector[:GC])
            dxd[rows, :] = (whole * steps + gp[6:7] * dy) * fs[slot, rows, :]
        for step in reversed(range(1, bits + 1)):
            advance(group - step, step, phase)
        ends.append(jnp.zeros((8 - chunks, GC), F32))
        se[...] += dot_nn(split2(jnp.concatenate(ends, axis=0)), collector)
        wide, sums = conv_back(
            dxd[...], lambda k: valb_ref[0, pl.ds(HALO - k, tokens), :], keep_ref, gp, tokens
        )
        put_rows(group, sums + [jnp.zeros((3, GC), F32)], True)
        wide = wide.astype(BF)
        dgate = dgs[slot]
        put_gradient(group, 0, dot_nn(nxt[...], dgate))
        put_gradient(group, 1, dot_nn(nxt[...], wide[HALO:]) + dot_nn(nht[...], wide[:HALO]))
        advance(group, 0, phase)
        both = jnp.concatenate([in_weights(0), in_weights(1)], axis=1)
        gnorm[...] += dot_nt(wide[:HALO], both[:, GC:])
        gx_ref[...] += dot_nt(jnp.concatenate([dgate, wide[HALO:]], axis=1), both)

    @pl.when(i == groups + skew - 1)
    def _():
        for turn in range(LAYERS):

            @pl.when(phase == turn)
            def _(turn=turn):
                for copy in load(line_refs[LAYERS - 1 - turn], mid_ref if turn else g_ref):
                    copy.start()
                pltpu.make_async_copy(weights[LAYERS - 1 - turn][4], own_m, next_sem).start()

        upper = (iota2((CH, CH), 0) <= iota2((CH, CH), 1)).astype(F32)
        before = (iota2((CH, CH), 0) > iota2((CH, CH), 1)).astype(F32)
        raw, steps, rates, _, _, _, _ = step_terms(step_ref[...], heads_ref, carried_ref, tail_ref, kept_ref, tokens)
        drates, dmaps = [], []
        for c in range(chunks):
            rows = slice(c * CH, (c + 1) * CH)
            drates.append(dot_nn(upper, sp[rows, :], HI) + dot_nn(before, sq[rows, :], HI) + se[c : c + 1])
            low = dgt[c].astype(BF)
            into = dbt[c] + dot_nn(low, outb[c])
            out = dct[c] + dot_tn(low, inb[c])
            dmaps.append(jnp.concatenate([into, out], axis=1))
        drate = jnp.concatenate(drates, axis=0)
        dstep = (sd[...] - drate * heads_ref[1:2]) * sigmoid(raw)
        head_sums = jnp.concatenate(
            [jnp.sum(dstep, axis=0, keepdims=True), jnp.sum(drate * rates, axis=0, keepdims=True)], axis=1
        )
        mixed = shared_conv()
        part = sigmoid(mixed)
        dmixed = jnp.concatenate(dmaps, axis=0) * (part + mixed * part * (1.0 - part))
        wide, sums = conv_back(dmixed, lambda k: shared_ref[pl.ds(HALO - k, tokens), :], keep_ref, taps(), tokens)
        row_total[0] = rows_now[...]
        map_total[0] = jnp.concatenate(sums + [jnp.zeros((3, 2 * STATE), F32)], axis=0)
        few_advance(0, phase, True)
        wide = wide.astype(BF)
        dstep = dstep.astype(BF)
        pltpu.make_async_copy(weights[0][4], own_m, next_sem).wait()
        back_wide = dot_nt(wide, own_m[..., : 2 * STATE].reshape(depth, 2 * STATE))
        gnorm[...] += back_wide[:HALO]

        @pl.when(z > 0)
        def _():
            halo_copy().start()

        gx_ref[...] += back_wide[HALO:] + dot_nt(dstep, own_m[..., 2 * STATE :].reshape(depth, LANES))
        at_end = phase == LAYERS - 1

        @pl.when(at_end)
        def _():
            drain(1, LAYERS - 1)

        misc = jnp.concatenate(
            [dot_nn(nxt[...], wide[HALO:]) + dot_nn(nht[...], wide[:HALO]), dot_nn(nxt[...], dstep)], axis=1
        )
        own_m[...] = misc.astype(BF).reshape(own_m.shape)
        misc_advance(0, phase)

        @pl.when(z < pieces - 1)
        def _():
            halo_copy().wait_recv()
            gx_ref[pl.ds(tokens - HALO, HALO), :] += hrecv[phase]

        for copy in load(line_refs[0], g_ref):
            copy.wait()
        blocks = [(k, slice(k * GC, (k + 1) * GC)) for k in range(depth // GC)]
        gain = gain_ref[pl.ds(layer, 1), :]
        power = inside = jnp.zeros((tokens, 1), F32)
        for k, cols in blocks:
            power = power + jnp.sum(xs[k] * xs[k], axis=1, keepdims=True)
            gained = gx_ref[:, cols] * gain[:, cols]
            inside = inside + jnp.sum(gained * xs[k], axis=1, keepdims=True)
        q = lax.rsqrt(power * (1.0 / depth) + EPS)
        inside = inside * (q * q * q) * (1.0 / depth)
        cuts = [jnp.sum(gx_ref[:, cols] * xs[k] * q, axis=0, keepdims=True) for k, cols in blocks]
        end_total[0] = jnp.concatenate(cuts + [head_sums, jnp.zeros((7 - len(cuts), GC), F32)], axis=0)
        few_advance(0, phase, False)
        for k, cols in blocks:
            gx_ref[:, cols] = fs[k] + q * (gx_ref[:, cols] * gain[:, cols]) - xs[k] * inside

        @pl.when(z > 0)
        def _():
            halo_copy().wait_send()
            for group in range(groups):
                state_copy(group).wait_send()

        @pl.when(at_end)
        def _():
            turn = LAYERS - 1
            few_advance(1, turn, True)
            misc_advance(1, turn)
            for step in range(2, bits + 1):
                drain(step, turn)
                few_advance(step, turn, True)
                few_advance(step - 1, turn, False)
                misc_advance(step, turn)
            few_advance(bits, turn, False)
            for group in range(groups - 2):
                finish_group(jnp.int32(group), turn)
            finish_few(turn)
            for group in range(groups - 2, groups):
                finish_group(jnp.int32(group), turn)


def whole(shape):
    return pl.BlockSpec(shape, lambda i: (0,) * len(shape), pipeline_mode=pl.Buffered(1))


def quarter(group, half, pieces):
    at = lax.rem(group, pieces // 2) if pieces > 2 else 0 * group
    return pieces - 1 - at if half else at


def group_specs(dims, wall):
    pieces, groups, _, skew = dims
    dp, _, _, share, _ = wall
    last = groups - 1

    def early(i):
        return jnp.minimum(i, last)

    def late(i):
        return jnp.maximum(i - skew, 0)

    def block(rows, at):
        return pl.BlockSpec((1, rows, GC), lambda i: (at(i), 0, 0))

    def both(make):
        return [make(0), make(1)]

    def column(i, at):
        return lax.div(at(i), pieces // 2)

    def pair(at):
        return both(
            lambda half: pl.BlockSpec(
                (dp, 1, 2, share, LANES), lambda i: (0, quarter(at(i), half, pieces), 0, 0, column(i, at))
            )
        )

    def single(at):
        return both(
            lambda half: pl.BlockSpec(
                (dp, 1, 1, share, LANES), lambda i: (0, quarter(at(i), half, pieces), 2, 0, column(i, at))
            )
        )

    def params(layer, at):
        return both(
            lambda half: pl.BlockSpec(
                (1, 1, 8, LANES), lambda i: (quarter(at(i), half, pieces), layer, 0, column(i, at))
            )
        )

    return early, late, block, pair, single, params


def side(refs, n):
    rows = refs[0].shape[0] * refs[0].shape[3]
    return jnp.concatenate([ref[:, 0, n].reshape(rows, LANES) for ref in refs], axis=1)


def side_params(refs):
    return jnp.concatenate([ref[0, 0] for ref in refs], axis=1)


def fixed(shape, place):
    return pl.BlockSpec(shape, lambda i: place, pipeline_mode=pl.Buffered(1))


def layer_forward(dims, bits, layer, x, gain, w, few, pack, csw, csb, masks, later, earlier):
    pieces, groups, tokens, skew = dims
    keep, bias, _, carried, tail, kept = masks
    chunks = tokens // CH
    depth = x.shape[1]
    ext = tokens + HALO
    slots = skew + 1
    early, late, _, pair, single, params = group_specs(dims, w.shape)

    def block(rows, at):
        return pl.BlockSpec((None, 1, rows, GC), lambda i: (layer, at(i), 0, 0))

    def mine(shape):
        return fixed((None,) + shape, (layer,) + (0,) * len(shape))

    anywhere = pl.BlockSpec(memory_space=pl.ANY)
    near = pl.BlockSpec(memory_space=pltpu.VMEM)
    gathers = later is not None
    cut = (2,) * bits
    buffers, sems = plane_scratch(pieces, bits, w.shape[3])
    if gathers:
        later_few, later = later
    first = 19 + 2 * gathers
    aliases = {first + k: 1 + k for k in range(len(earlier))}
    if gathers:
        aliases[20] = 11
    return pl.pallas_call(
        partial(forward_kernel, dims + (bits, layer, gathers)),
        grid=(groups + skew,),
        in_specs=[
            whole((tokens, depth)), whole(gain.shape), *pair(early), *single(late),
            whole(few.shape), *params(layer, early), *params(layer, late), fixed((pieces, 1, 8, 2 * LANES), (0, layer, 0, 0)),
            whole(csw.shape), whole(csb.shape),
            whole(keep.shape), whole(bias.shape), whole(carried.shape), whole(tail.shape), whole(kept.shape),
        ] + [near, anywhere] * gathers + [anywhere] * len(earlier),
        out_specs=[
            whole((tokens, depth)), mine((depth, tokens)), mine((depth, HALO)),
            block(tokens, early), block(ext, early), block(tokens, late),
            pl.BlockSpec((None, 1, chunks, STATE, GC), lambda i: (layer, late(i), 0, 0, 0)),
            mine((ext, 2 * STATE)), mine((tokens, LANES)), mine((tokens, LANES)),
        ] + [near, anywhere] * gathers,
        out_shape=[
            jax.ShapeDtypeStruct((tokens, depth), F32),
            jax.ShapeDtypeStruct((LAYERS, depth, tokens), BF),
            jax.ShapeDtypeStruct((LAYERS, depth, HALO), BF),
            jax.ShapeDtypeStruct((LAYERS, groups, tokens, GC), F32),
            jax.ShapeDtypeStruct((LAYERS, groups, ext, GC), F32),
            jax.ShapeDtypeStruct((LAYERS, groups, tokens, GC), F32),
            jax.ShapeDtypeStruct((LAYERS, groups, chunks, STATE, GC), BF),
            jax.ShapeDtypeStruct((LAYERS, ext, 2 * STATE), F32),
            jax.ShapeDtypeStruct((LAYERS, tokens, LANES), F32),
            jax.ShapeDtypeStruct((LAYERS, tokens, LANES), F32),
        ] + (
            [jax.ShapeDtypeStruct(cut + later_few.shape, BF), jax.ShapeDtypeStruct(later.shape, BF)]
            if gathers
            else []
        ),
        scratch_shapes=[
            pltpu.VMEM((ext, depth), BF),
            pltpu.VMEM((chunks, CH, STATE), BF),
            pltpu.VMEM((chunks, STATE, CH), BF),
            pltpu.VMEM((chunks, CH, STATE), BF),
            pltpu.VMEM((chunks, CH, CH), F32),
            pltpu.VMEM((2, tokens, LANES), F32),
            pltpu.VMEM((groups, 8, tokens), F32),
            pltpu.VMEM((3, tokens, 2 * LANES), BF),
            pltpu.VMEM((groups, 8, GC), F32),
            pltpu.VMEM((slots, tokens, GC), F32),
            pltpu.VMEM((slots, tokens, GC), F32),
            pltpu.VMEM((slots, tokens, GC), F32),
            pltpu.VMEM((slots, chunks, STATE, GC), F32),
            pltpu.VMEM((slots, STATE, GC), F32),
            pltpu.VMEM((groups, STATE, GC), BF),
            pltpu.VMEM((groups, STATE, GC), BF),
            pltpu.VMEM((tokens, depth), F32),
            pltpu.VMEM((tokens, LANES), F32),
            pltpu.VMEM((8, LANES), F32),
            pltpu.SemaphoreType.DMA,
            pltpu.SemaphoreType.DMA,
            pltpu.SemaphoreType.DMA((groups,)),
            pltpu.SemaphoreType.DMA((groups,)),
        ] + (buffers + sems if gathers else []),
        input_output_aliases=aliases,
        compiler_params=pltpu.CompilerParams(
            collective_id=layer, has_side_effects=True, vmem_limit_bytes=VMEM_LIMIT_FORWARD,
            dimension_semantics=("arbitrary",),
        ),
        name="layer_forward",
    )(
        x, gain, w, w, w, w, few, pack, pack, pack, pack, pack, csw, csb, keep, bias, carried, tail, kept,
        *([later_few, later] if gathers else []), *earlier,
    )


def layers_backward(dims, bits, g, line, gain, saved, weights, pack, csw, csb, masks):
    pieces, groups, tokens, skew = dims
    keep, _, biast, carried, tail, kept = masks
    nxt, nht, gate, val, y, states, shared, step_in, r = saved
    anywhere = pl.BlockSpec(memory_space=pl.ANY)
    chunks = tokens // CH
    depth = g.shape[1]
    wall = weights[0][0]
    _, _, _, share, wide = wall.shape
    ext = tokens + HALO
    slots = max(skew + 1, depth // GC)
    columns = 2 * groups // pieces
    row_shape = (pieces // 2, 2, columns * 8, LANES)
    few_shape = (8, GC)
    halves_of = [(2,) * (bits - 1 - step) for step in range(bits)]
    steps = groups + skew
    early, late, *_ = group_specs(dims, wall.shape)

    def in_turn(layer, at):
        turn = LAYERS - 1 - layer
        return lambda ph, i: at(jnp.where(ph == turn, i, jnp.where(ph < turn, 0, steps - 1)))

    def block(rows, at):
        return pl.BlockSpec((None, 1, rows, GC), lambda ph, i: (LAYERS - 1 - ph, at(i), 0, 0))

    def of_layer(v):
        return pl.BlockSpec(
            (None,) + v.shape[1:], lambda ph, i: (LAYERS - 1 - ph,) + (0,) * (v.ndim - 1),
            pipeline_mode=pl.Buffered(1),
        )

    def weight_blocks(count, first, at):
        def spec(half):
            def place(ph, i):
                group = at(ph, i)
                return 0, quarter(group, half, pieces), first, 0, lax.div(group, pieces // 2)

            return pl.BlockSpec((wall.shape[0], 1, count, share, LANES), place)

        return [spec(half) for half in range(2)]

    def group_params(at):
        def spec(half):
            def place(ph, i):
                group = at(i)
                return quarter(group, half, pieces), LAYERS - 1 - ph, 0, lax.div(group, pieces // 2)

            return pl.BlockSpec((1, 1, 8, LANES), place)

        return [spec(half) for half in range(2)]

    def whole(shape):
        return pl.BlockSpec(shape, lambda ph, i: (0,) * len(shape), pipeline_mode=pl.Buffered(1))

    weight_specs, weight_args = [], []
    for layer in range(LAYERS):
        w, few = weights[layer]
        weight_specs += weight_blocks(2, 0, in_turn(layer, late)) + weight_blocks(1, 2, in_turn(layer, early)) + [anywhere]
        weight_args += [w, w, w, w, few]
    return pl.pallas_call(
        partial(backward_kernel, dims + (bits,)),
        grid=(LAYERS, steps),
        in_specs=[anywhere] * (LAYERS + 2) + weight_specs + [
            whole(gain.shape), of_layer(nxt), of_layer(nht), of_layer(r),
            *group_params(early), *group_params(late),
            pl.BlockSpec((pieces, 1, 8, 2 * LANES), lambda ph, i: (0, LAYERS - 1 - ph, 0, 0)),
            whole(csw.shape), whole(csb.shape),
            whole(keep.shape), whole(biast.shape), whole(carried.shape), whole(tail.shape), whole(kept.shape),
            block(tokens, early), block(ext, early), block(tokens, early), block(ext, late),
            pl.BlockSpec((None, 1, chunks, STATE, GC), lambda ph, i: (LAYERS - 1 - ph, late(i), 0, 0, 0)),
            of_layer(shared), of_layer(step_in),
        ],
        out_specs=[
            whole((tokens, depth)), whole((LAYERS, 2, share, wide)), whole((LAYERS, share, wide)),
            whole((LAYERS, share, 2 * STATE + LANES)),
            whole((LAYERS, columns * 8, LANES)), whole((LAYERS, 16, GC)), anywhere,
        ],
        out_shape=[
            jax.ShapeDtypeStruct((tokens, depth), F32),
            jax.ShapeDtypeStruct((LAYERS, 2, share, wide), F32),
            jax.ShapeDtypeStruct((LAYERS, share, wide), F32),
            jax.ShapeDtypeStruct((LAYERS, share, 2 * STATE + LANES), F32),
            jax.ShapeDtypeStruct((LAYERS, columns * 8, LANES), F32),
            jax.ShapeDtypeStruct((LAYERS, 16, GC), F32),
            jax.ShapeDtypeStruct((tokens, depth), F32),
        ],
        scratch_shapes=[
            pltpu.VMEM((tokens, depth), BF),
            pltpu.VMEM((depth, tokens), BF),
            pltpu.VMEM((tokens, LANES), F32),
            pltpu.VMEM((chunks, CH, STATE), BF),
            pltpu.VMEM((chunks, CH, STATE), BF),
            pltpu.VMEM((chunks, STATE, CH), BF),
            pltpu.VMEM((chunks, CH, CH), F32),
            pltpu.VMEM((2, tokens, LANES), F32),
            pltpu.VMEM((groups, 8, tokens), F32),
            pltpu.VMEM((3, tokens, 2 * LANES), BF),
            pltpu.VMEM((groups, 8, GC), F32),
            pltpu.VMEM((slots, tokens, GC), BF),
            pltpu.VMEM((slots, tokens, GC), F32),
            pltpu.VMEM((slots, tokens, GC), F32),
            pltpu.VMEM((slots, tokens, GC), BF),
            pltpu.VMEM((slots, STATE, GC), F32),
            pltpu.VMEM((LAYERS, groups, STATE, GC), BF),
            pltpu.VMEM((groups, STATE, GC), BF),
            pltpu.VMEM((HALO, depth), F32),
            pltpu.VMEM((chunks, CH, STATE), F32),
            pltpu.VMEM((chunks, CH, STATE), F32),
            pltpu.VMEM((chunks, CH, CH), F32),
            pltpu.VMEM((tokens, LANES), F32),
            pltpu.VMEM((tokens, LANES), F32),
            pltpu.VMEM((tokens, LANES), F32),
            pltpu.VMEM((8, LANES), F32),
            pltpu.VMEM((tokens, GC), F32),
            pltpu.VMEM((tokens, GC), BF),
            pltpu.VMEM((LAYERS, HALO, depth), F32),
            pltpu.VMEM((groups, 2) + (2,) * bits + (3 * share, LANES), BF),
            pltpu.VMEM((2,) * bits + (share, 2 * STATE + LANES), BF),
            pltpu.VMEM((LAYERS, pieces, 2 * groups // pieces, 3 * share, LANES), BF),
            pltpu.VMEM((LAYERS, pieces, share, 2 * STATE + LANES), BF),
            pltpu.SemaphoreType.DMA,
            pltpu.SemaphoreType.DMA((LAYERS,)),
            pltpu.SemaphoreType.DMA((groups,)),
            pltpu.SemaphoreType.DMA((LAYERS, groups)),
            pltpu.SemaphoreType.DMA((groups, bits, 2)),
            pltpu.SemaphoreType.DMA((groups, bits, 2)),
            pltpu.SemaphoreType.DMA((groups, 2)),
            pltpu.SemaphoreType.DMA((LAYERS, pieces, 2 * groups // pieces)),
            pltpu.SemaphoreType.DMA((bits,)),
            pltpu.SemaphoreType.DMA((bits,)),
            pltpu.SemaphoreType.DMA((pieces,)),
            pltpu.SemaphoreType.DMA((LAYERS, pieces)),
            pltpu.SemaphoreType.DMA,
            pltpu.SemaphoreType.DMA((2, depth // GC)),
            pltpu.VMEM((8, LANES), F32),
            pltpu.VMEM(row_shape, F32),
            pltpu.VMEM((bits + 1,) + row_shape, F32),
            pltpu.VMEM((bits,) + row_shape, F32),
            pltpu.VMEM((LAYERS, pieces) + row_shape[2:], F32),
            pltpu.VMEM((bits + 1,) + few_shape, F32),
            pltpu.VMEM((bits,) + few_shape, F32),
            pltpu.VMEM((LAYERS, pieces) + few_shape, F32),
            pltpu.VMEM((bits + 1,) + few_shape, F32),
            pltpu.VMEM((bits,) + few_shape, F32),
            pltpu.VMEM((LAYERS, pieces) + few_shape, F32),
            pltpu.SemaphoreType.DMA((3, bits)),
            pltpu.SemaphoreType.DMA((3, bits)),
            pltpu.SemaphoreType.DMA((3, pieces)),
            pltpu.SemaphoreType.DMA((LAYERS, 3, pieces)),
            *[pltpu.VMEM((SLOTS, 2) + dims_left + (3 * share, LANES), BF) for dims_left in halves_of],
            *[pltpu.VMEM(dims_left + (share, 2 * STATE + LANES), BF) for dims_left in halves_of],
        ],
        compiler_params=pltpu.CompilerParams(
            collective_id=3, has_side_effects=True, vmem_limit_bytes=VMEM_LIMIT, dimension_semantics=("arbitrary", "arbitrary")
        ),
        name="layers_backward",
    )(
        g, *line, *weight_args, gain, nxt, nht, r, pack, pack, pack, pack, pack, csw, csb, keep, biast, carried, tail,
        kept, gate, val, y, val, states, shared, step_in,
    )


def near_first(z, pieces):
    table = [sorted(range(pieces), key=lambda k: (abs(k - at), k > at)) for at in range(pieces)]
    return [sum(jnp.where(z == at, table[at][p], 0) for at in range(pieces)) for p in range(pieces)]


class Line:
    def __init__(self, place, z, pieces, mine, wall, own_sem, z_send, z_recv):
        self.place, self.z, self.pieces, self.mine, self.wall = place, z, pieces, mine, wall
        self.z_send, self.z_recv = z_send, z_recv
        self.order = near_first(z, pieces)
        self.own = pltpu.make_async_copy(mine, wall.at[place.mine() + (z,)], own_sem)

    def z_copy(self, zi, up):
        src = self.mine if zi is self.z else self.wall.at[self.place.mine() + (zi,)]
        return pltpu.make_async_remote_copy(
            src_ref=src, dst_ref=self.wall.at[self.place.mine() + (zi,)], send_sem=self.z_send.at[int(up), zi],
            recv_sem=self.z_recv.at[zi], device_id={"tensor": self.z + (1 if up else -1)}, device_id_type=MESH,
        )

    def pass_on(self, zi, act):
        z, last = self.z, self.pieces - 1

        @pl.when(jnp.logical_and(zi <= z, z < last))
        def _():
            act(self.z_copy(zi, True))

        @pl.when(jnp.logical_and(zi >= z, z > 0))
        def _():
            act(self.z_copy(zi, False))

    def start(self):
        self.pass_on(self.z, lambda copy: copy.start())
        self.own.start()

    def arrive(self, p):
        zi = self.order[p]
        pltpu.make_async_remote_copy(
            src_ref=self.mine, dst_ref=self.wall.at[self.place.mine() + (zi,)], send_sem=self.z_send.at[0, zi],
            recv_sem=self.z_recv.at[zi], device_id={"tensor": zi}, device_id_type=MESH,
        ).wait_recv()
        self.pass_on(zi, lambda copy: copy.start())

    def finish(self):
        for p in range(self.pieces):
            self.pass_on(self.order[p], lambda copy: copy.wait_send())


class Plane:
    def __init__(self, place, z, pieces, mine, wall, few, few_z, few_all, *sems):
        self.place, self.z, self.pieces, self.bits = place, z, pieces, place.bits
        self.mine, self.wall, self.few, self.few_z, self.few_all = mine, wall, few, few_z, few_all
        self.d_send, self.d_recv, self.t_send, self.t_recv, self.f_send, self.f_recv = sems
        wide = wall.shape[-1]
        self.cols = [pl.ds(0, wide // 2), pl.ds(wide // 2, wide // 2)]
        self.few_cols = [pl.ds(0, 2 * STATE), pl.ds(2 * STATE, LANES)]
        self.order = near_first(z, pieces)
        rest = list(range(1, self.bits))
        self.paths = [rest + [0], rest[::-1] + [0]]

    def d_copy(self, p, half, step):
        path = self.paths[half]
        cols = (slice(None), slice(None), self.cols[half])
        ref = self.wall.at[self.place.along(path[:step]) + (self.order[p],) + cols]
        return pltpu.make_async_remote_copy(
            src_ref=self.mine.at[cols] if self.mine is not None and p + step == 0 else ref, dst_ref=ref,
            send_sem=self.d_send.at[p, half, step], recv_sem=self.d_recv.at[p, half, step],
            device_id={"dp": self.place.flip(path[step])}, device_id_type=MESH,
        )

    def line_copy(self, k):
        return pltpu.make_async_remote_copy(
            src_ref=self.few.at[:, self.few_cols[1]], dst_ref=self.few_z.at[self.z], send_sem=self.t_send.at[k],
            recv_sem=self.t_recv.at[k], device_id={"tensor": lax.rem(self.z + k, self.pieces)}, device_id_type=MESH,
        )

    def few_copy(self, half, step):
        path = self.paths[half]
        ref = self.few_all.at[self.place.along(path[:step]) + (slice(None), self.few_cols[half])]
        return pltpu.make_async_remote_copy(
            src_ref=ref, dst_ref=ref, send_sem=self.f_send.at[half, step], recv_sem=self.f_recv.at[half, step],
            device_id={"dp": self.place.flip(path[step])}, device_id_type=MESH,
        )

    def few_event(self, step):
        if step == 0:
            total = self.few[:, self.few_cols[1]]
            for k in range(1, self.pieces):
                self.line_copy(k).wait_recv()
                total = total + self.few_z[lax.rem(self.z + self.pieces - k, self.pieces)]
            self.few_all[self.place.mine()] = jnp.concatenate([self.few[:, self.few_cols[0]], total], axis=1)
        for half in range(2):
            if step:
                self.few_copy(half, step - 1).wait_recv()
            if step < self.bits:
                self.few_copy(half, step).start()

    def start(self, p):
        for half in range(2):
            self.d_copy(p, half, 0).start()

    def start_few(self):
        for k in range(1, self.pieces):
            self.line_copy(k).start()

    def double(self, p, step):
        for half in range(2):
            self.d_copy(p, half, step - 1).wait_recv()
            if step < self.bits:
                self.d_copy(p, half, step).start()

    def finish(self):
        for p in range(self.pieces):
            for half in range(2):
                for step in range(self.bits):
                    self.d_copy(p, half, step).wait_send()
        for k in range(1, self.pieces):
            self.line_copy(k).wait_send()
        for half in range(2):
            for step in range(self.bits):
                self.few_copy(half, step).wait_send()


def greet(place, z, pieces):
    barrier = pltpu.get_barrier_semaphore()
    for b in range(place.bits):
        pl.semaphore_signal(barrier, inc=1, device_id={"dp": place.flip(b)}, device_id_type=MESH)
    for k in range(1, pieces):
        pl.semaphore_signal(barrier, inc=1, device_id={"tensor": lax.rem(z + k, pieces)}, device_id_type=MESH)
    pl.semaphore_wait(barrier, place.bits + pieces - 1)


def write_masks(z, tokens, starts_ref, keep_ref, bias_ref, biast_ref, carried_ref, tail_ref, kept_ref):
    first = z * tokens

    def label(position):
        total = None
        for k in range(starts_ref.shape[1]):
            term = jnp.where(position >= starts_ref[0, k], 1.0, 0.0)
            total = term if total is None else total + term
        return total

    def same(a, b):
        return jnp.where(a == b, 1.0, 0.0)

    for c in range(tokens // CH):
        begin = first + c * CH
        down = iota2((CH, LANES), 0) + begin
        across = iota2((CH, LANES), 1) + begin
        own, other = label(down), label(across)
        rows = pl.ds(c * CH, CH)
        for k in range(1, 4):
            keep_ref[k - 1, rows, :] = same(label(down - k), own)
        equal = own == other
        bias_ref[c] = jnp.where(equal, jnp.where(down >= across, 0.0, NEG), NEG)
        biast_ref[c] = jnp.where(equal, jnp.where(down <= across, 0.0, NEG), NEG)
        flat = jnp.zeros((CH, LANES), jnp.int32) + begin
        before, final = label(flat - 1), label(flat + (CH - 1))
        carried_ref[rows, :] = same(own, before)
        tail_ref[rows, :] = same(own, final)
        kept_ref[pl.ds(c, 1), :] = same(final, before)[:1]
    kept_ref[pl.ds(tokens // CH, 8 - tokens // CH), :] = jnp.zeros((8 - tokens // CH, LANES), F32)


def gather_kernel(
    dims, starts, tokens_ref, cotangent_ref, cvw, cvb, gate_gain, skip, bias_in, decay, bc, dt, mine, later,
    wall, wall_later, x_all, g_all, few_out, few_later, pack_out, keep, bias, biast, carried, tail, kept,
    x_wide, g_wide, pack, pack_all, few, few_z, few_all, wide_sem, pk_send, pk_recv, *sems,
):
    pieces, tokens, bits = dims
    place = Place(bits)
    z = lax.axis_index("tensor")
    greet(place, z, pieces)
    line = Line(place, z, pieces, mine, wall, *sems[:3])
    line_later = Line(place, z, pieces, later, wall_later, *sems[3:6])
    plane = Plane(place, z, pieces, mine, wall, few, few_z, few_all, *sems[6:])

    heads = skip.shape[1]
    upper_half = z >= pieces // 2
    first = HG * jnp.where(upper_half, pieces - 1 - z, z) + jnp.where(upper_half, HG // 2, 0)

    def lane_of(head):
        return first + HG * (pieces // 2) * (head // 2) + head % 2

    def spot(ref, layer):
        lane = iota2((1, LANES), 1)
        total = jnp.zeros((1, LANES), F32)
        for head in range(heads):
            total = jnp.where(lane == lane_of(head), ref[layer : layer + 1, head : head + 1], total)
        return total

    low, high = iota2((heads, LANES), 0), iota2((heads, LANES), 1)
    chosen = (lane_of(0) + HG * (pieces // 2) * (low // 2) + low % 2 == high).astype(F32).astype(BF)
    for layer in range(LAYERS):
        wide = jnp.concatenate([bc[layer], dot_nn(dt[layer], chosen).astype(BF)], axis=1)
        if layer == 0:
            few[...] = wide
        else:
            few_later[...] = wide
    plane.start(0)
    line.start()
    plane.start_few()
    channel = iota2((1, cvb.shape[1]), 1) // HD
    for layer in range(LAYERS):
        skips = jnp.zeros(channel.shape, F32)
        for head in range(heads):
            skips = jnp.where(channel == head, skip[layer : layer + 1, head : head + 1], skips)
        own = slice(layer, layer + 1)
        rest = jnp.zeros((1, cvb.shape[1] - 2 * LANES), F32)
        tail_row = jnp.concatenate([spot(bias_in, layer), spot(decay, layer), rest], axis=1)
        pack[layer] = jnp.concatenate([cvw[layer], cvb[own], gate_gain[own], skips, tail_row], axis=0)

    def pack_copy(k):
        return pltpu.make_async_remote_copy(
            src_ref=pack, dst_ref=pack_all.at[z], send_sem=pk_send.at[k], recv_sem=pk_recv.at[k],
            device_id={"tensor": lax.rem(z + k, pieces)}, device_id_type=MESH,
        )

    for k in range(1, pieces):
        pack_copy(k).start()
    pack_all[z] = pack[...]
    wides = []
    for k, (narrow, wide, out) in enumerate(((tokens_ref, x_wide, x_all), (cotangent_ref, g_wide, g_all))):
        wide[...] = narrow[...].astype(F32)
        wides.append(pltpu.make_async_copy(wide, out, wide_sem.at[k]))
        wides[k].start()
    write_masks(z, tokens, starts, keep, bias, biast, carried, tail, kept)

    def arrive(p):
        line.arrive(p)
        plane.start(p)
        if p == min(2, pieces - 1):
            line_later.start()

    def double(p, step):
        if p == 0 and step == 1:
            line.own.wait()
        plane.double(p, step)

    events = []
    for p in range(pieces):
        if p:
            events.append((10.0 * p, partial(arrive, p)))
            events.append((10.0 * (2 + p) + 5.0, partial(line_later.arrive, p)))
        for step in range(1, bits + 1):
            late = 0.0 if step < bits - 1 else 0.8
            events.append((10.0 * p + 9.5 * step + late, partial(double, p, step)))
    for step in range(bits + 1):
        events.append((12.0 + 10.0 * step, partial(plane.few_event, step)))
    for _, act in sorted(events, key=lambda event: event[0]):
        act()
    line_later.own.wait()
    line.finish()
    line_later.finish()
    plane.finish()
    for copy in wides:
        copy.wait()
    for k in range(1, pieces):
        pack_copy(k).wait()
    few_out[...] = few_all[...]
    pack_out[...] = pack_all[...]


def line_sems(pieces):
    dma = pltpu.SemaphoreType.DMA
    return [dma, dma((2, pieces)), dma((pieces,))]


def plane_scratch(pieces, bits, share):
    dma = pltpu.SemaphoreType.DMA
    return [pltpu.VMEM((pieces, share, LANES), BF), pltpu.VMEM((2,) * bits + (share, 2 * STATE + LANES), BF)], [
        dma((pieces, 2, bits)), dma((pieces, 2, bits)), dma((pieces,)), dma((pieces,)), dma((2, bits)), dma((2, bits)),
    ]


def gather_first(dims, starts, x, g, params, bc, dt, share, later):
    pieces, tokens, bits = dims
    cut = (2,) * bits
    chunks = tokens // CH
    dma = pltpu.SemaphoreType.DMA
    anywhere = pl.BlockSpec(memory_space=pl.ANY)
    near = pl.BlockSpec(memory_space=pltpu.VMEM)
    buffers, sems = plane_scratch(pieces, bits, share.shape[1])
    pack = (LAYERS, 8, params[1].shape[1])
    few = (share.shape[1], 2 * STATE + LANES)
    return pl.pallas_call(
        partial(gather_kernel, dims),
        in_specs=[pl.BlockSpec(memory_space=pltpu.SMEM)] + [near] * 12,
        out_specs=[anywhere] * 4 + [near] * 9,
        out_shape=[
            jax.ShapeDtypeStruct(cut + (pieces,) + share.shape, BF),
            jax.ShapeDtypeStruct(cut + (pieces,) + share.shape, BF),
            jax.ShapeDtypeStruct(x.shape, F32),
            jax.ShapeDtypeStruct(g.shape, F32),
            jax.ShapeDtypeStruct(cut + few, BF),
            jax.ShapeDtypeStruct(few, BF),
            jax.ShapeDtypeStruct((pieces,) + pack, F32),
            jax.ShapeDtypeStruct((3, tokens, LANES), F32),
            jax.ShapeDtypeStruct((chunks, CH, CH), F32),
            jax.ShapeDtypeStruct((chunks, CH, CH), F32),
            jax.ShapeDtypeStruct((tokens, LANES), F32),
            jax.ShapeDtypeStruct((tokens, LANES), F32),
            jax.ShapeDtypeStruct((8, LANES), F32),
        ],
        scratch_shapes=[
            pltpu.VMEM(x.shape, F32), pltpu.VMEM(g.shape, F32), pltpu.VMEM(pack, F32), pltpu.VMEM((pieces,) + pack, F32),
            pltpu.VMEM(few, BF),
        ] + buffers + [dma((2,)), dma((pieces,)), dma((pieces,))] + line_sems(pieces) * 2 + sems,
        compiler_params=pltpu.CompilerParams(collective_id=2, has_side_effects=True, vmem_limit_bytes=VMEM_LIMIT),
        name="gather_first",
    )(starts, x, g, *params, bc, dt, share, later)


def local(
    tokens, gate_value_weight, w_bc, w_dt, w_out, norm_gain, conv_value_w, conv_value_b, conv_shared_w, conv_shared_b,
    step_bias, decay_log, skip_gain, gate_gain, starts, cotangent,
):
    pieces, dp = lax.axis_size("tensor"), lax.axis_size("dp")
    z = lax.axis_index("tensor")
    bits = (dp - 1).bit_length()
    count, depth = tokens.shape
    own = conv_value_b.shape[1]
    few = step_bias.shape[1]
    groups = pieces * own // GC
    dims = (pieces, groups, count, pieces - 1)

    shares = [
        jnp.concatenate([jnp.swapaxes(gate_value_weight[layer], 0, 1), w_out[layer][None]], axis=0)
        for layer in range(LAYERS)
    ]
    wall, wall_later, x, grad, few_all, few_later, pack, *masks = gather_first(
        (pieces, count, bits), starts, tokens, cotangent,
        (conv_value_w, conv_value_b, gate_gain, skip_gain, step_bias, decay_log), w_bc, w_dt, *shares,
    )
    line, saved, weights = [x], [], []
    for layer in range(LAYERS):
        weights.append((wall.reshape((dp,) + wall.shape[bits:]), few_all))
        later = (few_later, wall_later) if layer + 1 < LAYERS else None
        x, *saved = layer_forward(
            dims, bits, layer, x, norm_gain, *weights[-1], pack, conv_shared_w, conv_shared_b, masks, later, saved
        )
        if later is not None:
            *saved, few_all, wall = saved
        line.append(x)
    upper_half = z >= pieces // 2
    at = jnp.where(upper_half, pieces - 1 - z, z)

    def own_heads(v):
        v = v[..., : pieces * few].reshape(v.shape[:-1] + (few // 2, pieces // 2, 2, 2))
        v = lax.dynamic_index_in_dim(v, at, axis=v.ndim - 3, keepdims=False)
        v = lax.dynamic_index_in_dim(v, upper_half.astype(jnp.int32), axis=v.ndim - 2, keepdims=False)
        return v.reshape(v.shape[:-2] + (few,))

    grad, gw, go, gm, rows, small, _ = layers_backward(
        dims, bits, grad, line, norm_gain, saved, weights, pack, conv_shared_w, conv_shared_b, masks
    )
    rows = jnp.swapaxes(rows.reshape(LAYERS, -1, 8, LANES), 1, 2).reshape(LAYERS, 8, own)
    gcs, ends = small[:, :8], small[:, 8:]
    cuts = depth // GC
    gheads = own_heads(ends[:, cuts].reshape(LAYERS, 2, LANES))
    return (
        x.astype(BF), grad, jnp.swapaxes(gw, 1, 2), gm[:, :, : 2 * STATE], own_heads(gm[:, :, 2 * STATE :]),
        go, ends[:, :cuts].reshape(LAYERS, depth),
        rows[:, :4], rows[:, 4], gcs[:, :4], gcs[:, 4], gheads[:, 0], gheads[:, 1],
        jnp.sum(rows[:, 6].reshape(LAYERS, few, HD), axis=2), rows[:, 5],
    )


def solution(mesh):
    in_specs = (
        P(("dp", "tensor"), None),
        P(None, "dp", None, "tensor"),
        P(None, "dp", None),
        P(None, "dp", "tensor"),
        P(None, "dp", "tensor"),
        P(),
        P(None, None, "tensor"),
        P(None, "tensor"),
        P(),
        P(),
        P(None, "tensor"),
        P(None, "tensor"),
        P(None, "tensor"),
        P(None, "tensor"),
        P("dp", None),
        P(("dp", "tensor"), None),
    )
    out_specs = (
        P(("dp", "tensor"), None),
        P(("dp", "tensor"), None),
        P(None, "dp", None, "tensor"),
        P(None, "dp", None),
        P(None, "dp", "tensor"),
        P(None, "dp", "tensor"),
        P(),
        P(None, None, "tensor"),
        P(None, "tensor"),
        P(),
        P(),
        P(None, "tensor"),
        P(None, "tensor"),
        P(None, "tensor"),
        P(None, "tensor"),
    )
    return jax.shard_map(local, mesh=mesh, in_specs=in_specs, out_specs=out_specs, check_vma=False)
```
